32 devices in a mesh: row: 8 (over y, x, core), col: 4 (over z).
Axes of the slice: x: 2, y: 2, z: 4, core: 2. Of those that a mesh axis runs over, the one named last changes fastest.
Arguments:
- kernel_tiles: float32 [8, 4, 9, 256, 512], P('row', 'col'), may hold values from -0.09375 to 0.09375
- footprints: int32 [8, 4, 9], P('row', 'col'), may hold values from 0 to 8, as said below
- counts: int32 [8, 4], P('row', 'col'), may hold values from 64 to 256, as said below
- readings: float32 [8, 4, 256], P('row', 'col'), may hold values from -6 to 6
- damping: float32 [1], replicated, may hold values from 0.1 to 0.5
- layer_depth: float32 [2], replicated, may hold values from 1 to 6
- inclinations: float32 [2], replicated, may hold values from 0.6 to 1.3
- declinations: float32 [2], replicated, may hold values from -3.140625 to 3.140625
- resid_grid: float32 [2048, 1024], P('col', 'row'), may hold values from -3 to 3
Outputs:
- coefficients: float32 [8, 4, 512], P('row', 'col')
- rtp_map: float32 [2048, 1024], P(('row', 'col'))
The draws below stay inside these ranges and needn't reach their ends.
Inputs may be any that keep to these rules, and one draw needn't show every extreme that they name: `footprints`: each tile's list holds each of the 9 codes once; code 3 (a + 1) + (b + 1) names the source block a tiles north and b tiles east of the tile; blocks outside the survey are empty. `counts`: reading slots from this count on are ignored.
All inputs are finite; a program needn't handle non-finite values.
Results may differ from the reference program's by a relative error of at most 0.0003.
Values sent between devices are 32-bit elements; how exact they have to be, the bound alone decides.
No kernel may reach another device: no remote copies, remote signals or barrier semaphores. Data moves between devices by JAX's collectives and lax.ppermute only.
A program may use at most 128 MiB of HBM per device.

```python
import math
import jax
import jax.numpy as jnp
from jax import lax

READ_SLOTS = 256
SRC_ROWS = 8
SRC_COLS = 32
LAYERS = 2
REFINE = 16
FOOTPRINT = 9
CG_STEPS = 2
TILE_ROWS = 8
TILE_COLS = 4
BLOCK_SOURCES = 512
MAP_NORTH = 1024
MAP_EAST = 2048


def draw_footprints(key, part):
    tile_keys = jax.random.split(key, TILE_ROWS * TILE_COLS)
    orders = jax.vmap(lambda one_key: jax.random.permutation(one_key, FOOTPRINT))(tile_keys)
    return orders.reshape(TILE_ROWS, TILE_COLS, FOOTPRINT).astype(jnp.int32)


def draw_counts(key, part):
    values = jax.random.randint(key, (TILE_ROWS, TILE_COLS), READ_SLOTS // 4, READ_SLOTS + 1)
    return values.at[0, 0].set(READ_SLOTS).astype(jnp.int32)


def draw_readings(key, part):
    tiles_all = TILE_ROWS * TILE_COLS
    rising = 0.5 + jnp.arange(tiles_all, dtype=jnp.float32) / max(tiles_all - 1, 1)
    values = jnp.clip(jax.random.normal(jax.random.fold_in(key, 3), (tiles_all, READ_SLOTS)), -4.0, 4.0)
    return (rising[:, None] * values).reshape(TILE_ROWS, TILE_COLS, READ_SLOTS).astype(jnp.float32)


def block_scale(key, shape, cuts, least, top_value):
    gain = 1.0
    for dim, parts in cuts:
        heights = jax.random.uniform(jax.random.fold_in(jax.random.fold_in(key, 6), dim), (parts,), jnp.float32, least / len(cuts), top_value / len(cuts))
        gain = gain * jnp.repeat(jnp.exp(heights), shape[dim] // parts).reshape((-1,) + (1,) * (len(shape) - 1 - dim))
    return gain


def gaussian(key, dims, deviation, bound, shards=(), kind=jnp.bfloat16):
    loudness = block_scale(key, dims, shards, -0.22, 0.18) if shards else 1.0
    array = jax.random.normal(key, dims, jnp.float32) * deviation * loudness
    return jnp.minimum(jnp.maximum(array, -bound), bound).astype(kind)


def setup_inputs(seed: int = 0) -> dict:
    streams_of = jax.random.split(jax.random.key(seed), 10)
    return {
        "kernel_tiles": gaussian(streams_of[0], (TILE_ROWS, TILE_COLS, FOOTPRINT, READ_SLOTS, BLOCK_SOURCES), (FOOTPRINT * BLOCK_SOURCES) ** -0.5, 0.09375, ((0, 8), (1, 4)), jnp.float32),
        "footprints": draw_footprints(jax.random.fold_in(streams_of[9], 71), 0),
        "counts": draw_counts(jax.random.fold_in(streams_of[9], 71), 0),
        "readings": draw_readings(jax.random.fold_in(streams_of[9], 71), 0),
        "damping": jnp.clip(jnp.exp(jax.random.uniform(streams_of[4], (1,), jnp.float32, math.log(0.1), math.log(0.5))), 0.1, 0.5),
        "layer_depth": jnp.clip(jnp.exp(jax.random.uniform(streams_of[5], (LAYERS,), jnp.float32, math.log(1.0), math.log(6.0))), 1.0, 6.0),
        "inclinations": jnp.clip(jax.random.uniform(streams_of[6], (2,), jnp.float32, 0.6, 1.3), 0.6, 1.3),
        "declinations": jnp.clip(jax.random.uniform(streams_of[7], (2,), jnp.float32, -3.140625, 3.140625), -3.140625, 3.140625),
        "resid_grid": gaussian(streams_of[8], (MAP_EAST, MAP_NORTH), 0.5, 3.0, ((0, 4), (1, 8)), jnp.float32),
    }


HIGHEST_PRECISION = lax.Precision.HIGHEST
NEIGHBOUR_OFFSETS = tuple(((north_step, east_step) for north_step in (-1, 0, 1) for east_step in (-1, 0, 1)))

def hat_table(fine_start, fine_count, coarse_start, coarse_count):
    fine_pos = jnp.arange(fine_count, dtype=jnp.float32) + fine_start
    coarse_pos = jnp.arange(coarse_count, dtype=jnp.float32) + coarse_start
    offset = (fine_pos[:, None] + 0.5) / REFINE - 0.5 - coarse_pos[None, :]
    return jnp.maximum(0.0, 1.0 - jnp.abs(offset))

def frequency_of(positions, full_len):
    signed = jnp.where(positions < full_len // 2, positions, positions - full_len)
    return signed.astype(jnp.float32) / full_len

def pole_filter(north_freq, east_freq, inclinations, declinations):
    radius = jnp.sqrt(north_freq * north_freq + east_freq * east_freq)
    safe_radius = jnp.where(radius > 0.0, radius, 1.0)
    unit_north = jnp.where(radius > 0.0, north_freq / safe_radius, 0.0)
    unit_east = jnp.where(radius > 0.0, east_freq / safe_radius, 0.0)
    real_part = jnp.ones_like(radius)
    imag_part = jnp.zeros_like(radius)
    for member in range(2):
        vertical = jnp.sin(inclinations[member])
        horizontal = jnp.cos(inclinations[member])
        along_axis = horizontal * (jnp.cos(declinations[member]) * unit_north + jnp.sin(declinations[member]) * unit_east)
        denominator = vertical * vertical + along_axis * along_axis
        inv_real = vertical / denominator
        inv_imag = -along_axis / denominator
        real_part, imag_part = (real_part * inv_real - imag_part * inv_imag, real_part * inv_imag + imag_part * inv_real)
    return (real_part, imag_part)

def reference(kernel_tiles, footprints, counts, readings, damping, layer_depth, inclinations, declinations, resid_grid):
    live_mask = (jnp.arange(READ_SLOTS, dtype=jnp.int32)[None, None, :] < counts[:, :, None]).astype(jnp.float32)
    selector = (footprints[:, :, :, None] == jnp.arange(FOOTPRINT, dtype=jnp.int32)[None, None, None, :]).astype(jnp.float32)
    ridge_weight = damping[0]

    def forward(coefs_all):
        padded = jnp.pad(coefs_all, ((1, 1), (1, 1), (0, 0)))
        blocks = jnp.stack([padded[1 + north_step:1 + north_step + TILE_ROWS, 1 + east_step:1 + east_step + TILE_COLS] for north_step, east_step in NEIGHBOUR_OFFSETS], axis=2)
        chosen = jnp.einsum('abkc,abcs->abks', selector, blocks, precision=HIGHEST_PRECISION)
        return live_mask * jnp.einsum('abkrs,abks->abr', kernel_tiles, chosen, precision=HIGHEST_PRECISION)

    def adjoint(values):
        partial_sums = jnp.einsum('abkrs,abr->abks', kernel_tiles, live_mask * values, precision=HIGHEST_PRECISION)
        spread = jnp.einsum('abkc,abks->abcs', selector, partial_sums, precision=HIGHEST_PRECISION)
        summed = jnp.zeros((TILE_ROWS + 2, TILE_COLS + 2, BLOCK_SOURCES), jnp.float32)
        for position, (north_step, east_step) in enumerate(NEIGHBOUR_OFFSETS):
            summed = summed.at[1 + north_step:1 + north_step + TILE_ROWS, 1 + east_step:1 + east_step + TILE_COLS].add(spread[:, :, position])
        return summed[1:-1, 1:-1]

    def operate(vector):
        return adjoint(forward(vector)) + ridge_weight * vector
    right_side = adjoint(readings)
    solution = jnp.zeros_like(right_side)
    residual = right_side
    direction = right_side
    norm_now = jnp.sum(residual * residual)
    for iteration in range(CG_STEPS):
        applied = operate(direction)
        step_size = norm_now / jnp.sum(direction * applied)
        solution = solution + step_size * direction
        residual = residual - step_size * applied
        if iteration + 1 < CG_STEPS:
            norm_next = jnp.sum(residual * residual)
            direction = residual + norm_next / norm_now * direction
            norm_now = norm_next
    coarse = solution.reshape(TILE_ROWS, TILE_COLS, LAYERS, SRC_ROWS, SRC_COLS).transpose(2, 0, 3, 1, 4)
    coarse = coarse.reshape(LAYERS, TILE_ROWS * SRC_ROWS, TILE_COLS * SRC_COLS)
    up_north = hat_table(0.0, MAP_NORTH, 0.0, TILE_ROWS * SRC_ROWS)
    up_east = hat_table(0.0, MAP_EAST, 0.0, TILE_COLS * SRC_COLS)
    north_freq = frequency_of(jnp.arange(MAP_NORTH, dtype=jnp.int32), MAP_NORTH)[None, :]
    east_freq = frequency_of(jnp.arange(MAP_EAST, dtype=jnp.int32), MAP_EAST)[:, None]
    wavenumber = 2.0 * math.pi * jnp.sqrt(north_freq * north_freq + east_freq * east_freq)
    spectrum = jnp.fft.fft2(resid_grid)
    for layer in range(LAYERS):
        eastward = jnp.dot(up_east, coarse[layer].T, precision=HIGHEST_PRECISION)
        plane = jnp.dot(eastward, up_north.T, precision=HIGHEST_PRECISION)
        spectrum = spectrum + jnp.exp(-wavenumber * layer_depth[layer]) * jnp.fft.fft2(plane)
    row_block = MAP_EAST // TILE_COLS
    spec_blocks = spectrum.reshape(TILE_COLS, row_block, MAP_NORTH)
    east_blocks = east_freq.reshape(TILE_COLS, row_block, 1)

    def apply_filter(pair):
        spec_rows, east_rows = pair
        filt_real, filt_imag = pole_filter(north_freq, east_rows, inclinations, declinations)
        return spec_rows * (filt_real + 1j * filt_imag)
    filtered = lax.map(apply_filter, (spec_blocks, east_blocks)).reshape(MAP_EAST, MAP_NORTH)
    rtp_map = jnp.real(jnp.fft.ifft2(filtered)).astype(jnp.float32)
    return (solution, rtp_map)
```

```python
import functools

import jax
import jax.numpy as jnp
import ml_dtypes
import numpy as np
from jax import lax
from jax.experimental import pallas as pl
from jax.experimental.pallas import tpu as pltpu
from jax.sharding import PartitionSpec as P

SRC_ROWS = 8
SRC_COLS = 32
LAYERS = 2
REFINE = 16
FOOTPRINT = 9
LANES = 128
SUB = 8
HALF = 64
BOTH = ("row", "col")
VMEM_BYTES = 40 * 1024 * 1024
F32 = jnp.float32
BF16 = jnp.bfloat16

VMEM = pl.BlockSpec(memory_space=pltpu.VMEM)
SMEM = pl.BlockSpec(memory_space=pltpu.SMEM)
NN = (((1,), (0,)), ((), ()))
NT = (((1,), (1,)), ((), ()))
TN = (((0,), (0,)), ((), ()))


def split_table(table):
    high = table.astype(ml_dtypes.bfloat16)
    low = (table - high.astype(np.float64)).astype(ml_dtypes.bfloat16)
    return np.stack([high, low])


def group_start(group, rows):
    if group == 0:
        return 0
    if group == 1:
        return rows // 2
    return group // 2 + HALF * rows * (group % 2)


def unit_turn(product, period):
    angle = 2.0 * np.pi * (product % period) / period
    return np.cos(angle), np.sin(angle)


def north_turns(rows):
    north = rows * LANES
    starts = np.array([group_start(g, rows) for g in range(rows)])
    cos, sin = unit_turn(starts[:, None] * np.arange(north)[None, :], north)
    turns = np.stack([cos, -sin]).reshape(2, rows, rows, LANES)
    return turns.astype(np.float32)


def north_forward_table():
    cos, sin = unit_turn(np.outer(np.arange(HALF), np.arange(LANES)), LANES)
    plain = np.concatenate(
        [np.concatenate([cos, sin], 1), np.concatenate([-sin, cos], 1)], 0
    )
    packed = plain.copy()
    packed[HALF, :LANES] = 1.0 - 2.0 * (np.arange(LANES) % 2)
    return np.stack([split_table(packed), split_table(plain)])


def north_inverse_table():
    cos, sin = unit_turn(np.outer(np.arange(HALF), np.arange(LANES)), LANES)
    plain = 2.0 * np.concatenate([cos, sin], 1)
    packed = plain.copy()
    packed[0, :LANES] = 1.0
    packed[0, LANES:] = 2.0 * (np.arange(LANES) % 2) - 1.0
    return np.stack([split_table(packed), split_table(plain)])


def east_tables(east):
    bands = east // LANES
    cos, sin = unit_turn(np.outer(np.arange(LANES), np.arange(LANES)), LANES)
    forward = np.block([[cos, -sin], [sin, cos]])
    inverse = np.block([[cos, sin], [-sin, cos]])
    turn_cos, turn_sin = unit_turn(np.outer(np.arange(bands), np.arange(LANES)), east)
    turns = np.stack([turn_cos, -turn_sin]).astype(np.float32)
    return split_table(forward), split_table(inverse), turns


def hat_table(fine_count, coarse_count):
    offset = (np.arange(fine_count)[:, None] + 0.5) / REFINE - 0.5 - np.arange(coarse_count)[None, :]
    return np.maximum(0.0, 1.0 - np.abs(offset))


def north_hat_table(rows, cols):
    north = rows * LANES
    coarse = rows * SRC_ROWS
    own = HALF // cols
    spectrum = np.fft.fft(hat_table(north, coarse), axis=0)
    out = np.zeros((rows, cols, 2 * own, coarse))
    for group in range(rows):
        for col in range(cols):
            index = group_start(group, rows) + rows * (col * own + np.arange(own))
            part = spectrum[index % north]
            out[group, col, :own] = part.real
            out[group, col, own:] = part.imag
    out[0, 0, own] = spectrum[north // 2].real
    out = out.reshape(rows * cols, 2 * own, 2 * rows, 4).transpose(0, 3, 1, 2)
    return np.moveaxis(split_table(out.reshape(rows * cols, 8 * own, 2 * rows)), 0, 1)


def split(x):
    high = x.astype(BF16)
    return high, (x - high.astype(F32)).astype(BF16)


def dot(a, b, dims):
    return lax.dot_general(a, b, dims, preferred_element_type=F32)


def mul_table(x, high, low, dims=NN):
    x_high, x_low = split(x)
    return dot(x_high, high, dims) + (dot(x_low, high, dims) + dot(x_high, low, dims))


def table_mul(high, low, x, dims=NN):
    x_high, x_low = split(x)
    return dot(high, x_high, dims) + (dot(high, x_low, dims) + dot(low, x_high, dims))


def transform_list(values, sign):
    count = len(values)
    if count == 1:
        return values
    even = transform_list(values[0::2], sign)
    odd = transform_list(values[1::2], sign)
    first, second = [], []
    for k in range(count // 2):
        re, im = odd[k]
        if k == 0:
            turned = (re, im)
        elif 4 * k == count:
            turned = (im, -re) if sign < 0 else (-im, re)
        else:
            cos = float(np.cos(2.0 * np.pi * k / count))
            sin = sign * float(np.sin(2.0 * np.pi * k / count))
            if 8 * k == count or 8 * k == 3 * count:
                if cos * sin > 0:
                    turned = (cos * (re - im), cos * (re + im))
                else:
                    turned = (cos * (re + im), cos * (im - re))
            else:
                turned = (re * cos - im * sin, re * sin + im * cos)
        first.append((even[k][0] + turned[0], even[k][1] + turned[1]))
        second.append((even[k][0] - turned[0], even[k][1] - turned[1]))
    return first + second


def total(x):
    lanes = jnp.sum(jnp.sum(x, axis=0), axis=0, keepdims=True)
    return jnp.sum(lanes, axis=1, keepdims=True)


def neighbour(code, row, col, rows, cols):
    near_row = row + code // 3 - 1
    near_col = col + code % 3 - 1
    inside = (near_row >= 0) & (near_row < rows) & (near_col >= 0) & (near_col < cols)
    device = jnp.clip(near_row * cols + near_col, 0, rows * cols - 1)
    return device, inside


def near_blocks(codes, place, vector, rows, cols):
    blocks = []
    for k in range(FOOTPRINT):
        device, inside = neighbour(codes[k], place[0], place[1], rows, cols)
        blocks.append(vector[device] * jnp.where(inside, 1.0, 0.0))
    return blocks


def apply_forward(tiles, blocks, count, out):
    slots = tiles.shape[1]
    parts = tiles.shape[2] // LANES
    spread = [
        [jnp.broadcast_to(block[p : p + 1], (SUB, LANES)) for p in range(parts)] for block in blocks
    ]

    def step(t, squares):
        at = pl.multiple_of(t * SUB, SUB)
        sums = [None] * parts
        for k in range(FOOTPRINT):
            for p in range(parts):
                term = tiles[k, pl.ds(at, SUB), p * LANES : (p + 1) * LANES] * spread[k][p]
                sums[p] = term if sums[p] is None else sums[p] + term
        acc = functools.reduce(jnp.add, sums)
        slot = at + lax.broadcasted_iota(jnp.int32, (SUB, LANES), 0)
        value = jnp.where(slot < count, jnp.sum(acc, axis=1, keepdims=True), 0.0)
        if out is not None:
            out[pl.ds(at, SUB), :] = value
        return squares + value * value

    zero = jnp.zeros((SUB, LANES), F32)
    squares = lax.fori_loop(0, slots // SUB, step, zero, unroll=4)
    return jnp.sum(squares, axis=0, keepdims=True)


def apply_adjoint(tile, values, out, device):
    slots, width = tile.shape
    for p in range(width // LANES):
        sums = [None] * 4
        for t in range(slots // SUB):
            term = tile[t * SUB : (t + 1) * SUB, p * LANES : (p + 1) * LANES] * values[
                t * SUB : (t + 1) * SUB, :
            ]
            sums[t % 4] = term if sums[t % 4] is None else sums[t % 4] + term
        acc = functools.reduce(jnp.add, sums)
        out[pl.ds(device, 1), p, :] = jnp.sum(acc, axis=0, keepdims=True)


def send_adjoint(tiles, values, codes, place, out, rows, cols):
    out[...] = jnp.zeros(out.shape, F32)
    for k in range(FOOTPRINT):
        device, inside = neighbour(codes[k], place[0], place[1], rows, cols)

        @pl.when(inside)
        def _():
            apply_adjoint(tiles.at[k], values, out, device)


def start_kernel(rows, cols, codes, counts, place, readings, tile, out, values):
    k = pl.program_id(0)

    @pl.when(k == 0)
    def _():
        out[...] = jnp.zeros(out.shape, F32)
        slots = readings.shape[1]
        slot = lax.broadcasted_iota(jnp.int32, (1, slots), 1)
        live = jnp.where(slot < counts[0], readings[...], 0.0)
        for t in range(slots // LANES):
            square = jnp.broadcast_to(live[:, t * LANES : (t + 1) * LANES], (LANES, LANES))
            values[t * LANES : (t + 1) * LANES, :] = square.T

    device, inside = neighbour(codes[k], place[0], place[1], rows, cols)

    @pl.when(inside)
    def _():
        apply_adjoint(tile.at[0, 0, 0], values, out, device)


def gather_kernel(arrived, own, everywhere):
    block = jnp.sum(arrived[...], axis=0)
    own[...] = block
    everywhere[...] = jnp.broadcast_to(block[None], everywhere.shape)


def normal_kernel(rows, cols, codes, counts, place, tiles, vector, out, values):
    blocks = near_blocks(codes, place, vector, rows, cols)
    apply_forward(tiles.at[0, 0], blocks, counts[0], values)
    send_adjoint(tiles.at[0, 0], values, codes, place, out, rows, cols)


def applied_kernel(damping, arrived, own, everywhere):
    block = jnp.sum(arrived[...], axis=0) + damping[0] * own[...]
    everywhere[...] = jnp.broadcast_to(block[None], everywhere.shape)


def north_kernel(place, planes, turns, table, out):
    rows = planes.shape[0]
    re = planes[0] * turns[0, 0, 0:1]
    im = planes[0] * turns[1, 0, 0:1]
    for r in range(1, rows):
        re = re + planes[r] * turns[0, 0, r : r + 1]
        im = im + planes[r] * turns[1, 0, r : r + 1]
    both = jnp.concatenate([re, im], axis=1)
    out[...] = table_mul(table[0, 0], table[0, 1], both, NT)


def pole(north, east, trig):
    square = north * north + east * east
    inverse = jnp.where(square > 0.0, lax.rsqrt(jnp.where(square > 0.0, square, 1.0)), 0.0)
    a0 = (trig[1] * north + trig[2] * east) * inverse
    a1 = (trig[4] * north + trig[5] * east) * inverse
    v0, v1 = trig[0], trig[3]
    scale = 1.0 / ((v0 * v0 + a0 * a0) * (v1 * v1 + a1 * a1))
    return (v0 * v1 - a0 * a1) * scale, -(v0 * a1 + v1 * a0) * scale, square * inverse


def filter_kernel(rows, cols, place, trig, depth, main_re, main_im, side_re, side_im):
    _, bands, own, _ = main_re.shape
    north_len, east_len = rows * LANES, bands * LANES
    scale = 1.0 / (north_len * east_len)
    row, col = place[0], place[1]
    start = jnp.where(
        row == 0, 0, jnp.where(row == 1, rows // 2, row // 2 + HALF * rows * (row % 2))
    )

    def signed(index, length):
        return jnp.where(index < length // 2, index, index - length).astype(F32) / length

    def north_of(shape):
        index = start + rows * (col * own + lax.broadcasted_iota(jnp.int32, shape, 0))
        return signed(index, north_len)

    def weights(re, im, radius):
        damp = [None] + [jnp.exp(radius * (-2.0 * np.pi * depth[l])) for l in range(LAYERS)]
        return [(re, im) if d is None else (re * d, im * d) for d in damp]

    lane = lax.broadcasted_iota(jnp.int32, (own, LANES), 1)
    north = north_of((own, LANES))
    for band in range(bands):
        east = signed(band + bands * lane, east_len)
        re, im, radius = pole(north, east, trig)
        if band == 0:
            re2, im2, _ = pole(north, jnp.where(lane == HALF, 0.5, east), trig)
            re, im = 0.5 * (re + re2), 0.5 * (im + im2)
        for q, (wr, wi) in enumerate(weights(re * scale, im * scale, radius)):
            main_re[q, band] = wr
            main_im[q, band] = wi
    side_re[...] = jnp.zeros(side_re.shape, F32)
    side_im[...] = jnp.zeros(side_im.shape, F32)

    @pl.when((row == 0) & (col == 0))
    def _():
        band = lax.broadcasted_iota(jnp.int32, (bands, LANES), 0)
        lanes = lax.broadcasted_iota(jnp.int32, (bands, LANES), 1)
        east = signed(band + bands * lanes, east_len)
        flipped = jnp.where((band == 0) & (lanes == HALF), 0.5, east)
        pairs = []
        for one, other in ((0.0, 0.0), (-0.5, 0.5)):
            re, im, radius = pole(jnp.full_like(east, one), east, trig)
            re2, im2, _ = pole(jnp.full_like(east, other), flipped, trig)
            half = 0.5 * scale
            pairs.append(weights(half * (re + re2), half * (im + im2), radius))
        for q in range(1 + LAYERS):
            (r0, i0), (r1, i1) = pairs[0][q], pairs[1][q]
            side_re[q] = 0.5 * (r0 - r1)
            side_im[q] = 0.5 * (i0 - i1)
            for b in range(bands):
                main_re[q, b, 0:1, :] = 0.5 * (r0 + r1)[b : b + 1]
                main_im[q, b, 0:1, :] = 0.5 * (i0 + i1)[b : b + 1]


def east_forward(get, own, bands, turns, table, work):
    for g in range(own // SUB):
        values = transform_list([get(m, g) for m in range(bands)], -1.0)
        for b in range(bands):
            cos, sin = turns[0, b : b + 1, :], turns[1, b : b + 1, :]
            re, im = values[b]
            at = b * own + g * SUB
            work[at : at + SUB, :LANES] = re * cos - im * sin
            work[at : at + SUB, LANES:] = re * sin + im * cos
            if g == 0:
                re, im = values[(bands - b) % bands]
                re, im = re[0:1], -im[0:1]
                at = bands * own + b
                work[at : at + 1, :LANES] = re * cos - im * sin
                work[at : at + 1, LANES:] = re * sin + im * cos
    return mul_table(work[...], table[0], table[1])


def weigh(spectrum, q, own, bands, main_re, main_im, side_re, side_im, into, first):
    rows = own * bands
    re, im = spectrum[:rows, :LANES], spectrum[:rows, LANES:]
    wr = main_re[q].reshape(rows, LANES)
    wi = main_im[q].reshape(rows, LANES)
    out_re, out_im = re * wr - im * wi, re * wi + im * wr
    if first:
        into[:, :LANES] = out_re
        into[:, LANES:] = out_im
    else:
        into[:, :LANES] += out_re
        into[:, LANES:] += out_im
    re, im = spectrum[rows:, :LANES], spectrum[rows:, LANES:]
    wr, wi = side_re[q], side_im[q]
    add_re, add_im = re * wr - im * wi, re * wi + im * wr
    for b in range(bands):
        into[b * own : b * own + 1, :LANES] += add_re[b : b + 1]
        into[b * own : b * own + 1, LANES:] += add_im[b : b + 1]


def east_inverse(spectrum, own, bands, turns, table, work, store):
    work[...] = mul_table(spectrum[...], table[0], table[1])
    for g in range(own // SUB):
        values = []
        for b in range(bands):
            at = b * own + g * SUB
            re, im = work[at : at + SUB, :LANES], work[at : at + SUB, LANES:]
            cos, sin = turns[0, b : b + 1, :], turns[1, b : b + 1, :]
            values.append((re * cos + im * sin, im * cos - re * sin))
        values = transform_list(values, 1.0)
        for b in range(bands):
            store(b, g, *values[b])


def store_pieces(out, base, width):
    per_band = LANES // width

    def store(band, g, re, im):
        for s in range(per_band):
            cut = slice(s * width, (s + 1) * width)
            piece = jnp.concatenate([re[:, cut], im[:, cut]], axis=1)
            at = base + 2 * g
            out[band * per_band + s, at] = piece[:4]
            out[band * per_band + s, at + 1] = piece[4:]

    return store


def model_rows(vector, hats, rows, cols, coarse):
    own2 = hats.shape[1] // 4
    for i in range(rows):
        for j in range(cols):
            block = vector[i * cols + j]
            for layer in range(LAYERS):
                coarse[layer, 2 * i : 2 * i + 2, j * LANES : (j + 1) * LANES] = block[
                    2 * layer : 2 * layer + 2
                ]
    out = []
    tiles = cols * SRC_COLS // LANES
    lane = lax.broadcasted_iota(jnp.int32, (own2, LANES), 1) // SRC_COLS
    for layer in range(LAYERS):
        mixed = table_mul(hats[0], hats[1], coarse[layer])
        whole = []
        for tile in range(tiles):
            joined = None
            for place in range(LANES // SRC_COLS):
                j = tile * (LANES // SRC_COLS) + place
                summed = None
                for part in range(4):
                    piece = mixed[part * own2 : (part + 1) * own2, j * LANES : (j + 1) * LANES]
                    shift = ((place - part) * SRC_COLS) % LANES
                    if shift:
                        piece = pltpu.roll(piece, shift, 1)
                    summed = piece if summed is None else summed + piece
                joined = summed if joined is None else jnp.where(lane == place, summed, joined)
            whole.append(joined)
        out.append(whole[0] if tiles == 1 else jnp.concatenate(whole, axis=1))
    return out


def model_spectra(
    vector, hats, up_east, rows, cols, own, bands, turns, table, coarse, fine, work
):
    planes = model_rows(vector, hats, rows, cols, coarse)
    high, low = split(jnp.concatenate(planes, axis=0))
    fine[...] = dot(high, up_east[...], NN) + dot(low, up_east[...], NN)
    for layer in range(LAYERS):

        def get(m, g, base=2 * own * layer):
            at = base + g * SUB
            cut = slice(m * LANES, (m + 1) * LANES)
            return fine[at : at + SUB, cut], fine[at + own : at + own + SUB, cut]

        yield 1 + layer, east_forward(get, own, bands, turns, table, work)


def early_kernel(
    rows, cols, width, place, spec_re, spec_im, vector, hats, up_east, turns, forward, inverse,
    main_re, main_im, side_re, side_im, out_resid, out_first, coarse, fine, work, mixed, back,
):
    _, bands, own, _ = main_re.shape
    per = spec_re.shape[2] // LANES

    def get(m, g):
        cut = slice((m % per) * LANES, (m % per + 1) * LANES)
        at = slice(g * SUB, (g + 1) * SUB)
        return spec_re[m // per, at, cut], spec_im[m // per, at, cut]

    sides = (main_re, main_im, side_re, side_im)
    spectrum = east_forward(get, own, bands, turns, forward, work)
    weigh(spectrum, 0, own, bands, *sides, mixed, True)
    east_inverse(mixed, own, bands, turns, inverse, back, store_pieces(out_resid, 0, width))
    for q, spectrum in model_spectra(
        vector, hats[0], up_east, rows, cols, own, bands, turns, forward, coarse, fine, work
    ):
        weigh(spectrum, q, own, bands, *sides, mixed, q == 1)
    east_inverse(mixed, own, bands, turns, inverse, back, store_pieces(out_first, 0, width))


def late_kernel(
    rows, cols, width, codes, counts, place, damping, tiles, first, applied, early, early_first,
    hats, up_east, turns, forward, inverse, main_re, main_im, side_re, side_im,
    out, own_first, own_second, stats, second, coarse, fine, work, mixed, back,
):
    _, bands, own, _ = main_re.shape
    groups = own // 4
    norm = total(first[...] * first[...])
    step = norm / total(first[...] * applied[...])
    residual = first[...] - step[None] * applied[...]
    norm_next = total(residual * residual)
    second[...] = residual + (norm_next / norm)[None] * first[...]
    ridge = damping[0] * total(second[...] * second[...])
    me = place[0] * cols + place[1]
    own_first[...] = step * first[me]
    own_second[...] = second[me]
    stats[0] = jnp.broadcast_to(norm_next, stats.shape[1:])
    stats[1] = jnp.broadcast_to(ridge, stats.shape[1:])

    blocks = near_blocks(codes, place, second, rows, cols)
    squares = apply_forward(tiles.at[0, 0], blocks, counts[0], None)
    out[:, 2 * groups] = jnp.broadcast_to(
        squares[None, :, : out.shape[3]], (out.shape[0], 4, out.shape[3])
    )
    out[:, :groups] = early[...] + step[None, None] * early_first[...]
    sides = (main_re, main_im, side_re, side_im)
    for q, spectrum in model_spectra(
        second, hats[0], up_east, rows, cols, own, bands, turns, forward, coarse, fine, work
    ):
        weigh(spectrum, q, own, bands, *sides, mixed, q == 1)
    east_inverse(mixed, own, bands, turns, inverse, back, store_pieces(out, groups, width))


def finish_kernel(
    rows, cols, arrived, own_first, own_second, stats, turns, table, coefficients, out, mixed, waves
):
    groups = (arrived.shape[1] - 1) // 2
    width = out.shape[0]
    own = 4 * groups
    measured = jnp.sum(arrived[:, 2 * groups], axis=0)[0:1, 0:1]
    step = stats[0, 0:1, 0:1] / (measured + stats[1, 0:1, 0:1])
    solved = own_first[...] + step * own_second[...]
    for p in range(solved.shape[0]):
        coefficients[:, p * LANES : (p + 1) * LANES] = solved[p : p + 1]
    for i in range(rows):
        for j in range(cols):
            source = i * cols + j
            for q in range(groups):
                at = j * own + 4 * q
                mixed[i, at : at + 4, :] = (
                    arrived[source, q] + step * arrived[source, groups + q]
                )
        kind = min(i, 1)
        both = mul_table(mixed[i], table[kind, 0], table[kind, 1], TN)
        top, bottom = both[:width], both[width:]
        waves[i, :, :LANES] = top[:, :LANES] - bottom[:, LANES:]
        waves[i, :, LANES:] = top[:, LANES:] + bottom[:, :LANES]
    for at in range(0, width, SUB):
        parts = [None] * rows
        for i in range(rows):
            re = waves[i, at : at + SUB, :LANES]
            im = waves[i, at : at + SUB, LANES:]
            for n in range(rows):
                term = re * turns[0, i, n : n + 1] + im * turns[1, i, n : n + 1]
                parts[n] = term if i == 0 else parts[n] + term
        for n in range(rows):
            out[at : at + SUB, n * LANES : (n + 1) * LANES] = parts[n]


def shape(*dims):
    return jax.ShapeDtypeStruct(dims, F32)


def scratch(*dims):
    return pltpu.VMEM(dims, F32)


def call(kernel, outs, ins, work=(), **grid):
    if not grid:
        grid = dict(in_specs=[spec for spec, _ in ins], out_specs=jax.tree.map(lambda _: VMEM, outs))
    return pl.pallas_call(
        kernel,
        out_shape=outs,
        scratch_shapes=list(work),
        compiler_params=pltpu.CompilerParams(vmem_limit_bytes=VMEM_BYTES),
        **grid,
    )(*[value for _, value in ins])


def exchange(pieces):
    return lax.all_to_all(pieces, BOTH, 0, 0, tiled=True)


def on_device(
    kernel_tiles, footprints, counts, readings, damping, layer_depth, inclinations, declinations,
    resid_grid,
):
    rows, cols = lax.axis_size("row"), lax.axis_size("col")
    devices = rows * cols
    row, col = lax.axis_index("row"), lax.axis_index("col")
    place = jnp.stack([row, col]).astype(jnp.int32)
    codes, counts = footprints.reshape(-1), counts.reshape(-1)
    _, _, _, slots, sources = kernel_tiles.shape
    parts = sources // LANES
    tile_east = resid_grid.shape[0]
    east = cols * tile_east
    bands = east // LANES
    own = HALF // cols
    width = east // devices
    groups = own // 4

    turns = north_turns(rows)
    east_table, back_table, east_turns = east_tables(east)
    hats = north_hat_table(rows, cols)
    up_east = hat_table(east, cols * SRC_COLS).T.astype(ml_dtypes.bfloat16)

    planes = lax.all_gather(resid_grid, "row", axis=0)

    tile_shape = (1, 1, 1, slots, sources)
    partial_sums = call(
        functools.partial(start_kernel, rows, cols),
        shape(devices, parts, LANES),
        [(None, codes), (None, counts), (None, place), (None, readings.reshape(1, slots)), (None, kernel_tiles)],
        [scratch(slots, LANES)],
        grid=(FOOTPRINT,),
        in_specs=[SMEM, SMEM, SMEM, VMEM, pl.BlockSpec(tile_shape, lambda k: (0, 0, k, 0, 0))],
        out_specs=VMEM,
    )
    right_own, right_all = call(
        gather_kernel,
        (shape(parts, LANES), shape(devices, parts, LANES)),
        [(VMEM, exchange(partial_sums))],
    )
    right_side = exchange(right_all)
    partial_sums = call(
        functools.partial(normal_kernel, rows, cols),
        shape(devices, parts, LANES),
        [(SMEM, codes), (SMEM, counts), (SMEM, place), (VMEM, kernel_tiles), (VMEM, right_side)],
        [scratch(slots, LANES)],
    )

    trig = []
    for m in range(2):
        flat = jnp.cos(inclinations[m])
        trig += [jnp.sin(inclinations[m]), flat * jnp.cos(declinations[m]), flat * jnp.sin(declinations[m])]
    sides = call(
        functools.partial(filter_kernel, rows, cols),
        (shape(3, bands, own, LANES),) * 2 + (shape(3, bands, LANES),) * 2,
        [(SMEM, place), (SMEM, jnp.stack(trig)), (SMEM, layer_depth)],
    )

    chunk = LANES
    spectrum = pl.pallas_call(
        north_kernel,
        out_shape=shape(2 * HALF, tile_east),
        grid_spec=pltpu.PrefetchScalarGridSpec(
            num_scalar_prefetch=1,
            grid=(tile_east // chunk,),
            in_specs=[
                pl.BlockSpec((rows, chunk, LANES), lambda c, at: (0, c, 0)),
                pl.BlockSpec((2, 1, rows, LANES), lambda c, at: (0, at[0], 0, 0)),
                pl.BlockSpec((1, 2, 2 * HALF, 2 * LANES), lambda c, at: (jnp.minimum(at[0], 1), 0, 0, 0)),
            ],
            out_specs=pl.BlockSpec((2 * HALF, chunk), lambda c, at: (0, c)),
        ),
        compiler_params=pltpu.CompilerParams(vmem_limit_bytes=VMEM_BYTES),
    )(place, planes, turns, north_forward_table())
    spectrum = lax.all_gather(spectrum, "col", axis=0)

    applied_all = call(
        applied_kernel,
        shape(devices, parts, LANES),
        [(SMEM, damping), (VMEM, exchange(partial_sums)), (VMEM, right_own)],
    )
    applied = exchange(applied_all)

    work = [
        scratch(LAYERS, 2 * rows, cols * LANES),
        scratch(LAYERS * 2 * own, east),
        scratch((own + 1) * bands, 2 * LANES),
        scratch(own * bands, 2 * LANES),
        scratch(own * bands, 2 * LANES),
    ]
    full = pl.BlockSpec((None,) * 0)
    whole = lambda a: pl.BlockSpec(a.shape, lambda _, at, n=a.ndim: (0,) * n)
    mine = pl.BlockSpec((1,) + hats.shape[1:], lambda _, at: (at[0] * cols + at[1], 0, 0, 0))
    del full
    pieces = shape(devices, groups, 4, 2 * width)
    early, early_first = pl.pallas_call(
        functools.partial(early_kernel, rows, cols, width),
        out_shape=(pieces, pieces),
        grid_spec=pltpu.PrefetchScalarGridSpec(
            num_scalar_prefetch=1,
            grid=(1,),
            in_specs=[
                pl.BlockSpec((cols, own, tile_east), lambda _, at: (0, at[1], 0)),
                pl.BlockSpec((cols, own, tile_east), lambda _, at: (0, cols + at[1], 0)),
                whole(right_side),
                mine,
                whole(up_east),
                whole(east_turns),
                whole(east_table),
                whole(back_table),
            ]
            + [whole(side) for side in sides],
            out_specs=(whole(pieces),) * 2,
            scratch_shapes=work,
        ),
        compiler_params=pltpu.CompilerParams(vmem_limit_bytes=VMEM_BYTES),
    )(place, spectrum, spectrum, right_side, hats, up_east, east_turns, east_table, back_table, *sides)

    late_out = (
        shape(devices, 2 * groups + 1, 4, 2 * width),
        shape(parts, LANES),
        shape(parts, LANES),
        shape(2, SUB, LANES),
    )
    my_hats = lax.dynamic_index_in_dim(jnp.asarray(hats), row * cols + col, 0, keepdims=True)
    pieces, own_first, own_second, stats = call(
        functools.partial(late_kernel, rows, cols, width),
        late_out,
        [
            (SMEM, codes),
            (SMEM, counts),
            (SMEM, place),
            (SMEM, damping),
            (VMEM, kernel_tiles),
            (VMEM, right_side),
            (VMEM, applied),
            (VMEM, early),
            (VMEM, early_first),
            (VMEM, my_hats),
            (VMEM, up_east),
            (VMEM, east_turns),
            (VMEM, east_table),
            (VMEM, back_table),
        ]
        + [(VMEM, side) for side in sides],
        [scratch(devices, parts, LANES)] + work,
    )
    coefficients, rtp_map = call(
        functools.partial(finish_kernel, rows, cols),
        (shape(1, sources), shape(width, rows * LANES)),
        [
            (VMEM, exchange(pieces)),
            (VMEM, own_first),
            (VMEM, own_second),
            (VMEM, stats),
            (VMEM, turns),
            (VMEM, north_inverse_table()),
        ],
        [scratch(rows, HALF, 2 * width), scratch(rows, width, 2 * LANES)],
    )
    return coefficients.reshape(1, 1, sources), rtp_map


def solution(mesh):
    in_specs = (
        P("row", "col", None, None, None),
        P("row", "col", None),
        P("row", "col"),
        P("row", "col", None),
        P(),
        P(),
        P(),
        P(),
        P("col", "row"),
    )
    out_specs = (P("row", "col", None), P(("row", "col"), None))
    return jax.shard_map(
        on_device, mesh=mesh, in_specs=in_specs, out_specs=out_specs, check_vma=False
    )
```

```python
import functools

import jax
import jax.numpy as jnp
import ml_dtypes
import numpy as np
from jax import lax
from jax.experimental import pallas as pl
from jax.experimental.pallas import tpu as pltpu
from jax.sharding import PartitionSpec as P

SRC_ROWS = 8
SRC_COLS = 32
LAYERS = 2
REFINE = 16
FOOTPRINT = 9
LANES = 128
SUB = 8
HALF = 64
BOTH = ("row", "col")
COUNT, ROW, COL = 9, 10, 11
NORTH_STEPS = 2
MIB = 1024 * 1024
SMALL, LARGE = 24 * MIB, 62 * MIB
F32 = jnp.float32
BF16 = jnp.bfloat16

VMEM = pl.BlockSpec(memory_space=pltpu.VMEM)
SMEM = pl.BlockSpec(memory_space=pltpu.SMEM)
HBM = pl.BlockSpec(memory_space=pltpu.HBM)
NN = (((1,), (0,)), ((), ()))
NT = (((1,), (1,)), ((), ()))
TN = (((0,), (0,)), ((), ()))


def split_table(table):
    high = table.astype(ml_dtypes.bfloat16)
    low = (table - high.astype(np.float64)).astype(ml_dtypes.bfloat16)
    return np.stack([high, low])


def group_start(group, rows):
    if group == 0:
        return 0
    if group == 1:
        return rows // 2
    return group // 2 + HALF * rows * (group % 2)


def unit_turn(product, period):
    angle = 2.0 * np.pi * (product % period) / period
    return np.cos(angle), np.sin(angle)


def north_turns(rows):
    north = rows * LANES
    starts = np.array([group_start(g, rows) for g in range(rows)])
    cos, sin = unit_turn(starts[:, None] * np.arange(north)[None, :], north)
    turns = np.stack([cos, -sin]).reshape(2, rows, rows, LANES)
    return turns.astype(np.float32)


def north_forward_table(cols):
    cos, sin = unit_turn(np.outer(np.arange(HALF), np.arange(LANES)), LANES)
    plain = np.concatenate(
        [np.concatenate([cos, sin], 1), np.concatenate([-sin, cos], 1)], 0
    )
    packed = plain.copy()
    packed[HALF, :LANES] = 1.0 - 2.0 * (np.arange(LANES) % 2)
    order = np.arange(2 * HALF).reshape(2, cols, -1).transpose(1, 0, 2).reshape(-1)
    return np.stack([split_table(packed[order]), split_table(plain[order])])


def north_inverse_table():
    cos, sin = unit_turn(np.outer(np.arange(HALF), np.arange(LANES)), LANES)
    plain = 2.0 * np.concatenate([cos, sin], 1)
    packed = plain.copy()
    packed[0, :LANES] = 1.0
    packed[0, LANES:] = 2.0 * (np.arange(LANES) % 2) - 1.0
    return np.stack([split_table(packed), split_table(plain)])


def east_tables(east):
    bands = east // LANES
    cos, sin = unit_turn(np.outer(np.arange(LANES), np.arange(LANES)), LANES)
    forward = np.block([[cos, -sin], [sin, cos]])
    inverse = np.block([[cos, sin], [-sin, cos]])
    turn_cos, turn_sin = unit_turn(np.outer(np.arange(bands), np.arange(LANES)), east)
    turns = np.concatenate([turn_cos, -turn_sin]).astype(np.float32)
    up_east = hat_table(east, east // REFINE).reshape(-1, 2 * LANES, east // REFINE)
    up_east = up_east.transpose(0, 2, 1).reshape(-1, 2 * LANES).astype(ml_dtypes.bfloat16)
    tables = [split_table(forward), split_table(inverse)]
    return np.concatenate([t.reshape(-1, 2 * LANES) for t in tables] + [up_east]), turns


def hat_table(fine_count, coarse_count):
    offset = (np.arange(fine_count)[:, None] + 0.5) / REFINE - 0.5 - np.arange(coarse_count)[None, :]
    return np.maximum(0.0, 1.0 - np.abs(offset))


def north_hat_table(rows, cols):
    north = rows * LANES
    coarse = rows * SRC_ROWS
    own = HALF // cols
    spectrum = np.fft.fft(hat_table(north, coarse), axis=0)
    out = np.zeros((rows, cols, 2 * own, coarse))
    for group in range(rows):
        for col in range(cols):
            index = group_start(group, rows) + rows * (col * own + np.arange(own))
            part = spectrum[index % north]
            out[group, col, :own] = part.real
            out[group, col, own:] = part.imag
    out[0, 0, own] = spectrum[north // 2].real
    out = out.reshape(rows * cols, 2 * own, 2 * rows, 4).transpose(0, 2, 3, 1)
    out = out.reshape(rows * cols, 2 * rows, 8 * own)
    return np.pad(out, ((0, 0), (0, 0), (0, LANES - 8 * own))).astype(np.float32)


def split(x):
    high = x.astype(BF16)
    return high, (x - high.astype(F32)).astype(BF16)


def dot(a, b, dims):
    return lax.dot_general(a, b, dims, preferred_element_type=F32)


def mul_table(x, high, low, dims=NN):
    x_high, x_low = split(x)
    return dot(x_high, high, dims) + (dot(x_low, high, dims) + dot(x_high, low, dims))


def table_mul(high, low, x, dims=NN):
    x_high, x_low = split(x)
    return dot(high, x_high, dims) + (dot(high, x_low, dims) + dot(low, x_high, dims))


def transform_list(values, sign):
    count = len(values)
    if count == 1:
        return values
    even = transform_list(values[0::2], sign)
    odd = transform_list(values[1::2], sign)
    first, second = [], []
    for k in range(count // 2):
        re, im = odd[k]
        if k == 0:
            turned = (re, im)
        elif 4 * k == count:
            turned = (im, -re) if sign < 0 else (-im, re)
        else:
            cos = float(np.cos(2.0 * np.pi * k / count))
            sin = sign * float(np.sin(2.0 * np.pi * k / count))
            if 8 * k == count or 8 * k == 3 * count:
                if cos * sin > 0:
                    turned = (cos * (re - im), cos * (re + im))
                else:
                    turned = (cos * (re + im), cos * (im - re))
            else:
                turned = (re * cos - im * sin, re * sin + im * cos)
        first.append((even[k][0] + turned[0], even[k][1] + turned[1]))
        second.append((even[k][0] - turned[0], even[k][1] - turned[1]))
    return first + second


def total(x):
    lanes = jnp.sum(jnp.sum(x, axis=0), axis=0, keepdims=True)
    return jnp.sum(lanes, axis=1, keepdims=True)


def neighbour(k, ints, rows, cols):
    code = ints[k]
    near_row = ints[ROW] + code // 3 - 1
    near_col = ints[COL] + code % 3 - 1
    inside = (near_row >= 0) & (near_row < rows) & (near_col >= 0) & (near_col < cols)
    device = jnp.clip(near_row * cols + near_col, 0, rows * cols - 1)
    return device, inside


def near_blocks(ints, vector, rows, cols):
    blocks = []
    for k in range(FOOTPRINT):
        device, inside = neighbour(k, ints, rows, cols)
        blocks.append(vector[device] * jnp.where(inside, 1.0, 0.0))
    return blocks


def apply_forward(tiles, copies, blocks, count, out, work):
    slots, width = tiles.shape[1:]
    parts = width // LANES
    squares = jnp.zeros((SUB, LANES), F32)
    for group in range(0, FOOTPRINT, 3):
        for k in range(group, group + 3):
            copies[k].wait()
        spread = [
            [jnp.broadcast_to(blocks[k][p : p + 1], (SUB, LANES)) for p in range(parts)]
            for k in range(group, group + 3)
        ]

        def step(t, squares, group=group, spread=spread):
            at = pl.multiple_of(t * SUB, SUB)
            sums = [None] * parts
            for k in range(3):
                for p in range(parts):
                    tile = tiles[group + k, pl.ds(at, SUB), p * LANES : (p + 1) * LANES]
                    term = tile * spread[k][p]
                    sums[p] = term if sums[p] is None else sums[p] + term
            acc = functools.reduce(jnp.add, sums)
            if group > 0:
                acc = acc + work[pl.ds(at, SUB), :]
            if group + 3 < FOOTPRINT:
                work[pl.ds(at, SUB), :] = acc
                return squares
            slot = at + lax.broadcasted_iota(jnp.int32, (SUB, LANES), 0)
            value = jnp.where(slot < count, jnp.sum(acc, axis=1, keepdims=True), 0.0)
            if out is not None:
                out[pl.ds(at, SUB), :] = value
            return squares + value * value

        squares = lax.fori_loop(0, slots // SUB, step, squares, unroll=8)
    return jnp.sum(squares, axis=0, keepdims=True)


def apply_adjoint(tile, values, out, device):
    slots, width = tile.shape
    for p in range(width // LANES):
        sums = [None] * 4
        for t in range(slots // SUB):
            term = tile[t * SUB : (t + 1) * SUB, p * LANES : (p + 1) * LANES] * values[
                t * SUB : (t + 1) * SUB, :
            ]
            sums[t % 4] = term if sums[t % 4] is None else sums[t % 4] + term
        acc = functools.reduce(jnp.add, sums)
        out[pl.ds(device, 1), p, :] = jnp.sum(acc, axis=0, keepdims=True)


def send_adjoint(tile, values, k, ints, out, rows, cols):
    device, inside = neighbour(k, ints, rows, cols)

    @pl.when(inside)
    def _():
        apply_adjoint(tile, values, out, device)


def tile_copies(source, tiles, sems):
    copies = [
        pltpu.make_async_copy(source.at[0, 0, k], tiles.at[k], sems.at[k]) for k in range(FOOTPRINT)
    ]
    for copy in copies:
        copy.start()
    return copies


def start_kernel(rows, cols, ints, readings, source, out, tiles, values, sems):
    copies = tile_copies(source, tiles, sems)
    out[...] = jnp.zeros(out.shape, F32)
    slots = readings.shape[1]
    slot = lax.broadcasted_iota(jnp.int32, (1, slots), 1)
    live = jnp.where(slot < ints[COUNT], readings[...], 0.0)
    for t in range(slots // LANES):
        square = jnp.broadcast_to(live[:, t * LANES : (t + 1) * LANES], (LANES, LANES))
        values[t * LANES : (t + 1) * LANES, :] = square.T
    for k in range(FOOTPRINT):
        copies[k].wait()
        send_adjoint(tiles.at[k], values, k, ints, out, rows, cols)


def gather_kernel(arrived, everywhere):
    block = jnp.sum(arrived[...], axis=0)
    everywhere[...] = jnp.broadcast_to(block[None], everywhere.shape)


def normal_kernel(rows, cols, ints, floats, source, vector, out, tiles, sems, values, work):
    copies = tile_copies(source, tiles, sems)
    blocks = near_blocks(ints, vector, rows, cols)
    apply_forward(tiles, copies, blocks, ints[COUNT], values, work)
    out[...] = jnp.zeros(out.shape, F32)
    for k in range(FOOTPRINT):
        send_adjoint(tiles.at[k], values, k, ints, out, rows, cols)
    me = ints[ROW] * cols + ints[COL]
    out[me] = out[me] + floats[0] * vector[me]


def north_kernel(cols, ints, planes, turns, table, *outs):
    outs, mixed = outs[:-1], outs[-1]
    rows = planes.shape[0]
    re = planes[0] * turns[0, 0, 0:1]
    im = planes[0] * turns[1, 0, 0:1]
    for r in range(1, rows):
        re = re + planes[r] * turns[0, 0, r : r + 1]
        im = im + planes[r] * turns[1, 0, r : r + 1]
    both = jnp.concatenate([re, im], axis=1)
    result = table_mul(table[0, 0], table[0, 1], both, NT)
    own2 = outs[0].shape[0]
    for col in range(cols):
        mixed[col] = result[col * own2 : (col + 1) * own2]
    for step in range(cols):
        outs[step][...] = mixed[ints[COL] ^ step]


def pole(north, east, trig):
    square = north * north + east * east
    inverse = jnp.where(square > 0.0, lax.rsqrt(jnp.where(square > 0.0, square, 1.0)), 0.0)
    a0 = (trig[1] * north + trig[2] * east) * inverse
    a1 = (trig[4] * north + trig[5] * east) * inverse
    v0, v1 = trig[0], trig[3]
    scale = 1.0 / ((v0 * v0 + a0 * a0) * (v1 * v1 + a1 * a1))
    return (v0 * v1 - a0 * a1) * scale, -(v0 * a1 + v1 * a0) * scale, square * inverse


def side_rows(own, bands, rows):
    span = (own + 1) * bands
    turns = 2 * (1 + LAYERS) * span
    return span, turns, turns + 2 * bands, turns + 2 * bands + 2 * rows


def filter_kernel(rows, cols, own, bands, ints, floats, turns, hats, side):
    span, turns_at, hats_at, end = side_rows(own, bands, rows)
    side[turns_at:hats_at, :] = turns[...]
    side[hats_at:end, :] = hats[0]
    depth = [floats[1 + l] for l in range(LAYERS)]
    trig = [floats[1 + LAYERS + t] for t in range(6)]

    def put(part, q, at, value):
        base = (part * (1 + LAYERS) + q) * span + at
        side[base : base + value.shape[0], :] = value

    north_len, east_len = rows * LANES, bands * LANES
    scale = 1.0 / (north_len * east_len)
    row, col = ints[ROW], ints[COL]
    start = jnp.where(
        row == 0, 0, jnp.where(row == 1, rows // 2, row // 2 + HALF * rows * (row % 2))
    )

    def signed(index, length):
        return jnp.where(index < length // 2, index, index - length).astype(F32) / length

    def north_of(shape):
        index = start + rows * (col * own + lax.broadcasted_iota(jnp.int32, shape, 0))
        return signed(index, north_len)

    def weights(re, im, radius):
        damp = [None] + [jnp.exp(radius * (-2.0 * np.pi * depth[l])) for l in range(LAYERS)]
        return [(re, im) if d is None else (re * d, im * d) for d in damp]

    lane = lax.broadcasted_iota(jnp.int32, (own, LANES), 1)
    north = north_of((own, LANES))
    for band in range(bands):
        east = signed(band + bands * lane, east_len)
        re, im, radius = pole(north, east, trig)
        if band == 0:
            re2, im2, _ = pole(north, jnp.where(lane == HALF, 0.5, east), trig)
            re, im = 0.5 * (re + re2), 0.5 * (im + im2)
        for q, (wr, wi) in enumerate(weights(re * scale, im * scale, radius)):
            put(0, q, band * own, wr)
            put(1, q, band * own, wi)
            put(0, q, bands * own, jnp.zeros((bands, LANES), F32))
            put(1, q, bands * own, jnp.zeros((bands, LANES), F32))

    @pl.when((row == 0) & (col == 0))
    def _():
        band = lax.broadcasted_iota(jnp.int32, (bands, LANES), 0)
        lanes = lax.broadcasted_iota(jnp.int32, (bands, LANES), 1)
        east = signed(band + bands * lanes, east_len)
        flipped = jnp.where((band == 0) & (lanes == HALF), 0.5, east)
        pairs = []
        for one, other in ((0.0, 0.0), (-0.5, 0.5)):
            re, im, radius = pole(jnp.full_like(east, one), east, trig)
            re2, im2, _ = pole(jnp.full_like(east, other), flipped, trig)
            half = 0.5 * scale
            pairs.append(weights(half * (re + re2), half * (im + im2), radius))
        for q in range(1 + LAYERS):
            (r0, i0), (r1, i1) = pairs[0][q], pairs[1][q]
            put(0, q, bands * own, 0.5 * (r0 - r1))
            put(1, q, bands * own, 0.5 * (i0 - i1))
            for b in range(bands):
                put(0, q, b * own, 0.5 * (r0 + r1)[b : b + 1])
                put(1, q, b * own, 0.5 * (i0 + i1)[b : b + 1])


def turn_rows(side, turns_at, band, bands):
    cos, sin = turns_at + band, turns_at + bands + band
    return side[cos : cos + 1, :], side[sin : sin + 1, :]


def east_table(tables, index):
    span = 2 * LANES
    return tables[2 * index * span : (2 * index + 1) * span], tables[
        (2 * index + 1) * span : (2 * index + 2) * span
    ]


def east_forward(get, sizes, side, tables, work):
    rows, _, own, bands = sizes
    turns_at = side_rows(own, bands, rows)[1]
    for g in range(own // SUB):
        values = transform_list([get(m, g) for m in range(bands)], -1.0)
        for b in range(bands):
            cos, sin = turn_rows(side, turns_at, b, bands)
            re, im = values[b]
            at = b * own + g * SUB
            work[at : at + SUB, :LANES] = re * cos - im * sin
            work[at : at + SUB, LANES:] = re * sin + im * cos
            if g == 0:
                re, im = values[(bands - b) % bands]
                re, im = re[0:1], -im[0:1]
                at = bands * own + b
                work[at : at + 1, :LANES] = re * cos - im * sin
                work[at : at + 1, LANES:] = re * sin + im * cos
    return mul_table(work[...], *east_table(tables, 0))


def weigh(spectrum, q, sizes, side, into, first):
    rows, _, own, bands = sizes
    span = side_rows(own, bands, rows)[0]
    re, im = spectrum[:, :LANES], spectrum[:, LANES:]
    wr = side[q * span : (q + 1) * span, :]
    wi = side[(1 + LAYERS + q) * span : (2 + LAYERS + q) * span, :]
    out_re, out_im = re * wr - im * wi, re * wi + im * wr
    main = own * bands
    if first:
        into[:, :LANES] = out_re[:main]
        into[:, LANES:] = out_im[:main]
    else:
        into[:, :LANES] += out_re[:main]
        into[:, LANES:] += out_im[:main]
    for b in range(bands):
        into[b * own : b * own + 1, :LANES] += out_re[main + b : main + b + 1]
        into[b * own : b * own + 1, LANES:] += out_im[main + b : main + b + 1]


def east_inverse(spectrum, sizes, side, tables, work, store):
    rows, _, own, bands = sizes
    turns_at = side_rows(own, bands, rows)[1]
    work[...] = mul_table(spectrum[...], *east_table(tables, 1))
    for g in range(own // SUB):
        values = []
        for b in range(bands):
            at = b * own + g * SUB
            re, im = work[at : at + SUB, :LANES], work[at : at + SUB, LANES:]
            cos, sin = turn_rows(side, turns_at, b, bands)
            values.append((re * cos + im * sin, im * cos - re * sin))
        values = transform_list(values, 1.0)
        for b in range(bands):
            store(b, g, *values[b])


def store_pieces(out, width):
    per_band = LANES // width

    def store(band, g, re, im):
        for s in range(per_band):
            cut = slice(s * width, (s + 1) * width)
            piece = jnp.concatenate([re[:, cut], im[:, cut]], axis=1)
            out[band * per_band + s, g * SUB : (g + 1) * SUB] = piece

    return store


def model_rows(vector, sizes, side, coarse):
    rows, cols, own, bands = sizes
    own2 = 2 * own
    for i in range(rows):
        for j in range(cols):
            block = vector[i * cols + j]
            for layer in range(LAYERS):
                coarse[layer, 2 * i : 2 * i + 2, j * LANES : (j + 1) * LANES] = block[
                    2 * layer : 2 * layer + 2
                ]
    out = []
    _, _, hats_at, end = side_rows(own, bands, rows)
    high, low = split(side[hats_at:end, :])
    tiles = cols * SRC_COLS // LANES
    lane = lax.broadcasted_iota(jnp.int32, (own2, LANES), 1) // SRC_COLS
    for layer in range(LAYERS):
        mixed = table_mul(high, low, coarse[layer], TN)
        whole = []
        for tile in range(tiles):
            joined = None
            for place in range(LANES // SRC_COLS):
                j = tile * (LANES // SRC_COLS) + place
                summed = None
                for part in range(4):
                    piece = mixed[part * own2 : (part + 1) * own2, j * LANES : (j + 1) * LANES]
                    shift = ((place - part) * SRC_COLS) % LANES
                    if shift:
                        piece = pltpu.roll(piece, shift, 1)
                    summed = piece if summed is None else summed + piece
                joined = summed if joined is None else jnp.where(lane == place, summed, joined)
            whole.append(joined)
        out.append(whole[0] if tiles == 1 else jnp.concatenate(whole, axis=1))
    return out


def model_response(vector, sizes, side, tables, store, coarse, fine, work, mixed, back):
    rows, cols, own, bands = sizes
    depth = cols * SRC_COLS
    high, low = split(jnp.concatenate(model_rows(vector, sizes, side, coarse), axis=0))
    for c in range(bands // 2):
        at = 8 * LANES + c * depth
        table = tables[at : at + depth, :]
        fine[:, 2 * LANES * c : 2 * LANES * (c + 1)] = dot(high, table, NN) + dot(low, table, NN)
    for layer in range(LAYERS):

        def get(m, g, base=2 * own * layer):
            at = base + g * SUB
            cut = slice(m * LANES, (m + 1) * LANES)
            return fine[at : at + SUB, cut], fine[at + own : at + own + SUB, cut]

        spectrum = east_forward(get, sizes, side, tables, work)
        weigh(spectrum, 1 + layer, sizes, side, mixed, layer == 0)
    east_inverse(mixed, sizes, side, tables, back, store)


def resid_kernel(sizes, width, ints, *refs):
    rows, cols, own, bands = sizes
    arrived, (tables, side, out, spec, work, mixed, back) = refs[:cols], refs[cols:]
    per = arrived[0].shape[1] // LANES
    for step in range(cols):
        spec[ints[COL] ^ step] = arrived[step][...]

    def get(m, g):
        cut = slice((m % per) * LANES, (m % per + 1) * LANES)
        at = g * SUB
        return spec[m // per, at : at + SUB, cut], spec[m // per, own + at : own + at + SUB, cut]

    spectrum = east_forward(get, sizes, side, tables, work)
    weigh(spectrum, 0, sizes, side, mixed, True)
    east_inverse(mixed, sizes, side, tables, back, store_pieces(out, width))


def first_kernel(sizes, width, vector, tables, side, out, *work):
    model_response(vector, sizes, side, tables, store_pieces(out, width), *work)


def direction_kernel(
    rows, cols, ints, floats, source, first, applied, second, measured, carry, tiles, sems, work
):
    copies = tile_copies(source, tiles, sems)
    norm = total(first[...] * first[...])
    step = norm / total(first[...] * applied[...])
    residual = first[...] - step[None] * applied[...]
    norm_next = total(residual * residual)
    second[...] = residual + (norm_next / norm)[None] * first[...]
    blocks = near_blocks(ints, second, rows, cols)
    squares = apply_forward(tiles, copies, blocks, ints[COUNT], None, work)
    measured[...] = jnp.broadcast_to(squares[None], measured.shape)
    ridge = floats[0] * total(second[...] * second[...])
    me = ints[ROW] * cols + ints[COL]
    carry[0] = step * first[me]
    carry[1] = second[me]
    for at, value in ((2, norm_next), (3, ridge), (4, step)):
        carry[at] = jnp.broadcast_to(value, carry.shape[1:])


def second_kernel(sizes, width, vector, tables, side, early, early_first, carry, known, out, *work):
    known[...] = early[...] + carry[4, 0:1, 0:1][None] * early_first[...]
    model_response(vector, sizes, side, tables, store_pieces(out, width), *work)


def combine_kernel(measured, carry, known, response, out, coefficients):
    squares = jnp.sum(measured[:, 0:1], axis=0)
    step = carry[2, 0:1, 0:1] / (squares[:, 0:1] + carry[3, 0:1, 0:1])
    out[...] = known[...] + step[None] * response[...]
    solved = carry[0] + step * carry[1]
    for p in range(solved.shape[0]):
        coefficients[:, p * LANES : (p + 1) * LANES] = solved[p : p + 1]


def finish_kernel(rows, cols, arrived, turns, table, out, mixed, waves):
    own = arrived.shape[1]
    width = out.shape[0]
    for i in range(rows):
        for j in range(cols):
            mixed[i, j * own : (j + 1) * own, :] = arrived[i * cols + j]
        kind = min(i, 1)
        both = mul_table(mixed[i], table[kind, 0], table[kind, 1], TN)
        top, bottom = both[:width], both[width:]
        waves[i, :, :LANES] = top[:, :LANES] - bottom[:, LANES:]
        waves[i, :, LANES:] = top[:, LANES:] + bottom[:, :LANES]
    for at in range(0, width, SUB):
        parts = [None] * rows
        for i in range(rows):
            re = waves[i, at : at + SUB, :LANES]
            im = waves[i, at : at + SUB, LANES:]
            for n in range(rows):
                term = re * turns[0, i, n : n + 1] + im * turns[1, i, n : n + 1]
                parts[n] = term if i == 0 else parts[n] + term
        for n in range(rows):
            out[at : at + SUB, n * LANES : (n + 1) * LANES] = parts[n]


def shape(*dims):
    return jax.ShapeDtypeStruct(dims, F32)


def scratch(*dims):
    return pltpu.VMEM(dims, F32)


def call(kernel, outs, ins, work=(), limit=SMALL):
    return pl.pallas_call(
        kernel,
        out_shape=outs,
        in_specs=[spec for spec, _ in ins],
        out_specs=jax.tree.map(lambda _: VMEM, outs),
        scratch_shapes=list(work),
        compiler_params=pltpu.CompilerParams(vmem_limit_bytes=limit),
    )(*[value for _, value in ins])


def placed_call(kernel, out, ints, ins, work=(), limit=SMALL, steps=1, out_block=None):
    def whole(a):
        return pl.BlockSpec(a.shape, lambda step, at, n=a.ndim: (0,) * n)

    return pl.pallas_call(
        kernel,
        out_shape=out,
        grid_spec=pltpu.PrefetchScalarGridSpec(
            num_scalar_prefetch=1,
            grid=(steps,),
            in_specs=[whole(value) if spec is None else spec for spec, value in ins],
            out_specs=whole(out) if out_block is None else out_block,
            scratch_shapes=list(work),
        ),
        compiler_params=pltpu.CompilerParams(vmem_limit_bytes=limit),
    )(ints, *[value for _, value in ins])


def exchange(pieces):
    return lax.all_to_all(pieces, BOTH, 0, 0, tiled=True)


def on_device(
    kernel_tiles, footprints, counts, readings, damping, layer_depth, inclinations, declinations,
    resid_grid,
):
    rows, cols = lax.axis_size("row"), lax.axis_size("col")
    devices = rows * cols
    place = jnp.stack([lax.axis_index("row"), lax.axis_index("col")]).astype(jnp.int32)
    ints = jnp.concatenate([footprints.reshape(-1), counts.reshape(-1), place])
    slots, sources = kernel_tiles.shape[3:]
    parts = sources // LANES
    tile_east = resid_grid.shape[0]
    east = cols * tile_east
    bands = east // LANES
    own = HALF // cols
    width = east // devices
    sizes = (rows, cols, own, bands)

    turns = north_turns(rows)
    tables, east_turns = east_tables(east)
    hats = north_hat_table(rows, cols)

    planes = lax.all_gather(resid_grid, "row", axis=0)

    kernel_tiles = pltpu.with_memory_space_constraint(kernel_tiles, pltpu.HBM)
    tile_scratch = scratch(FOOTPRINT, slots, sources)
    tile_sems = pltpu.SemaphoreType.DMA((FOOTPRINT,))

    sums = call(
        functools.partial(start_kernel, rows, cols),
        shape(devices, parts, LANES),
        [(SMEM, ints), (VMEM, readings.reshape(1, slots)), (HBM, kernel_tiles)],
        [tile_scratch, scratch(slots, LANES), tile_sems],
    )
    sums, damping, layer_depth, inclinations, declinations = lax.optimization_barrier(
        (sums, damping, layer_depth, inclinations, declinations)
    )
    flat = jnp.cos(inclinations)
    trig = [jnp.sin(inclinations), flat * jnp.cos(declinations), flat * jnp.sin(declinations)]
    floats = jnp.concatenate([damping, layer_depth, jnp.stack(trig, axis=1).reshape(-1)])
    side = placed_call(
        functools.partial(filter_kernel, rows, cols, own, bands),
        shape(side_rows(own, bands, rows)[-1], LANES),
        ints,
        [
            (SMEM, floats),
            (None, east_turns),
            (pl.BlockSpec((1,) + hats.shape[1:], lambda _, at: (at[ROW] * cols + at[COL], 0, 0)), hats),
        ],
    )
    everywhere = shape(devices, parts, LANES)
    right_all = call(gather_kernel, everywhere, [(VMEM, exchange(sums))])
    right_all, side = lax.optimization_barrier((right_all, side))
    right_side = exchange(right_all)

    sums = call(
        functools.partial(normal_kernel, rows, cols),
        everywhere,
        [(SMEM, ints), (SMEM, floats), (HBM, kernel_tiles), (VMEM, right_side)],
        [tile_scratch, tile_sems, scratch(slots, LANES), scratch(slots, LANES)],
    )
    sums, planes, right_side = lax.optimization_barrier((sums, planes, right_side))
    chunk = tile_east // NORTH_STEPS
    spectra = placed_call(
        functools.partial(north_kernel, cols),
        [shape(2 * own, tile_east)] * cols,
        ints,
        [
            (pl.BlockSpec((rows, chunk, LANES), lambda c, at: (0, c, 0)), pltpu.with_memory_space_constraint(planes, pltpu.HBM)),
            (pl.BlockSpec((2, 1, rows, LANES), lambda c, at: (0, at[ROW], 0, 0)), turns),
            (
                pl.BlockSpec(
                    (1, 2, 2 * HALF, 2 * LANES), lambda c, at: (jnp.minimum(at[ROW], 1), 0, 0, 0)
                ),
                north_forward_table(cols),
            ),
        ],
        [scratch(cols, 2 * own, chunk)],
        steps=NORTH_STEPS,
        out_block=[pl.BlockSpec((2 * own, chunk), lambda c, at: (0, c))] * cols,
        limit=48 * MIB,
    )
    right_side, spectra = lax.optimization_barrier((right_side, spectra))
    spectra = list(spectra[:1]) + [
        lax.ppermute(spectra[s], "col", [(c, c ^ s) for c in range(cols)]) for s in range(1, cols)
    ]
    work = [
        scratch((own + 1) * bands, 2 * LANES),
        scratch(own * bands, 2 * LANES),
        scratch(own * bands, 2 * LANES),
    ]
    model_work = [scratch(LAYERS, 2 * rows, cols * LANES), scratch(LAYERS * 2 * own, east)] + work
    pieces = shape(devices, own, 2 * width)
    early_first = call(
        functools.partial(first_kernel, sizes, width),
        pieces,
        [(VMEM, right_side), (VMEM, tables), (VMEM, side)],
        model_work,
    )
    applied_all = call(gather_kernel, everywhere, [(VMEM, exchange(sums))])
    applied_all, early_first = lax.optimization_barrier((applied_all, early_first))
    applied = exchange(applied_all)

    second, measured, carry = call(
        functools.partial(direction_kernel, rows, cols),
        (everywhere, everywhere, shape(5, parts, LANES)),
        [(SMEM, ints), (SMEM, floats), (HBM, kernel_tiles), (VMEM, right_side), (VMEM, applied)],
        [tile_scratch, tile_sems, scratch(slots, LANES)],
    )
    measured, spectra = lax.optimization_barrier((measured, spectra))
    early = call(
        functools.partial(resid_kernel, sizes, width),
        pieces,
        [(SMEM, ints)] + [(VMEM, part) for part in spectra] + [(VMEM, tables), (VMEM, side)],
        [scratch(cols, 2 * own, tile_east)] + work,
    )

    known, response = call(
        functools.partial(second_kernel, sizes, width),
        (pieces, pieces),
        [
            (VMEM, second),
            (VMEM, tables),
            (VMEM, side),
            (VMEM, early),
            (VMEM, early_first),
            (VMEM, carry),
        ],
        model_work,
    )
    outgoing, coefficients = call(
        combine_kernel,
        (pieces, shape(1, sources)),
        [(VMEM, exchange(measured)), (VMEM, carry), (VMEM, known), (VMEM, response)],
    )
    rtp_map = call(
        functools.partial(finish_kernel, rows, cols),
        shape(width, rows * LANES),
        [(VMEM, exchange(outgoing)), (VMEM, turns), (VMEM, north_inverse_table())],
        [scratch(rows, HALF, 2 * width), scratch(rows, width, 2 * LANES)],
    )
    return coefficients.reshape(1, 1, sources), rtp_map


def solution(mesh):
    in_specs = (
        P("row", "col", None, None, None),
        P("row", "col", None),
        P("row", "col"),
        P("row", "col", None),
        P(),
        P(),
        P(),
        P(),
        P("col", "row"),
    )
    out_specs = (P("row", "col", None), P(("row", "col"), None))
    return jax.shard_map(
        on_device, mesh=mesh, in_specs=in_specs, out_specs=out_specs, check_vma=False
    )
```

```python
import functools

import jax
import jax.numpy as jnp
import ml_dtypes
import numpy as np
from jax import lax
from jax.experimental import pallas as pl
from jax.experimental.pallas import tpu as pltpu
from jax.sharding import PartitionSpec as P

SRC_ROWS = 8
SRC_COLS = 32
LAYERS = 2
REFINE = 16
FOOTPRINT = 9
LANES = 128
SUB = 8
HALF = 64
BOTH = ("row", "col")
COUNT, ROW, COL = 9, 10, 11
MIB = 1024 * 1024
SMALL, LARGE = 24 * MIB, 62 * MIB
F32 = jnp.float32
BF16 = jnp.bfloat16

VMEM = pl.BlockSpec(memory_space=pltpu.VMEM)
SMEM = pl.BlockSpec(memory_space=pltpu.SMEM)
HBM = pl.BlockSpec(memory_space=pltpu.HBM)
ANY = pl.BlockSpec(memory_space=pl.ANY)
NN = (((1,), (0,)), ((), ()))
NT = (((1,), (1,)), ((), ()))
TN = (((0,), (0,)), ((), ()))


def split_table(table):
    high = table.astype(ml_dtypes.bfloat16)
    low = (table - high.astype(np.float64)).astype(ml_dtypes.bfloat16)
    return np.stack([high, low])


def group_start(group, rows):
    if group == 0:
        return 0
    if group == 1:
        return rows // 2
    return group // 2 + HALF * rows * (group % 2)


def unit_turn(product, period):
    angle = 2.0 * np.pi * (product % period) / period
    return np.cos(angle), np.sin(angle)


def north_turns(rows):
    north = rows * LANES
    starts = np.array([group_start(g, rows) for g in range(rows)])
    cos, sin = unit_turn(starts[:, None] * np.arange(north)[None, :], north)
    turns = np.stack([cos, -sin]).reshape(2, rows, rows, LANES)
    return turns.astype(np.float32)


def north_forward_table():
    cos, sin = unit_turn(np.outer(np.arange(HALF), np.arange(LANES)), LANES)
    plain = np.concatenate(
        [np.concatenate([cos, sin], 1), np.concatenate([-sin, cos], 1)], 0
    )
    packed = plain.copy()
    packed[HALF, :LANES] = 1.0 - 2.0 * (np.arange(LANES) % 2)
    return np.stack([split_table(packed), split_table(plain)])


def north_inverse_table():
    cos, sin = unit_turn(np.outer(np.arange(HALF), np.arange(LANES)), LANES)
    plain = 2.0 * np.concatenate([cos, sin], 1)
    packed = plain.copy()
    packed[0, :LANES] = 1.0
    packed[0, LANES:] = 2.0 * (np.arange(LANES) % 2) - 1.0
    return np.stack([split_table(packed), split_table(plain)])


def east_tables(east):
    bands = east // LANES
    cos, sin = unit_turn(np.outer(np.arange(LANES), np.arange(LANES)), LANES)
    forward = np.block([[cos, -sin], [sin, cos]])
    inverse = np.block([[cos, sin], [-sin, cos]])
    turn_cos, turn_sin = unit_turn(np.outer(np.arange(bands), np.arange(LANES)), east)
    turns = np.concatenate([turn_cos, -turn_sin]).astype(np.float32)
    up_east = hat_table(east, east // REFINE).reshape(-1, 2 * LANES, east // REFINE)
    up_east = up_east.transpose(0, 2, 1).reshape(-1, 2 * LANES).astype(ml_dtypes.bfloat16)
    tables = [split_table(forward), split_table(inverse)]
    return np.concatenate([t.reshape(-1, 2 * LANES) for t in tables] + [up_east]), turns


def hat_table(fine_count, coarse_count):
    offset = (np.arange(fine_count)[:, None] + 0.5) / REFINE - 0.5 - np.arange(coarse_count)[None, :]
    return np.maximum(0.0, 1.0 - np.abs(offset))


def north_hat_table(rows, cols):
    north = rows * LANES
    coarse = rows * SRC_ROWS
    own = HALF // cols
    spectrum = np.fft.fft(hat_table(north, coarse), axis=0)
    out = np.zeros((rows, cols, 2 * own, coarse))
    for group in range(rows):
        for col in range(cols):
            index = group_start(group, rows) + rows * (col * own + np.arange(own))
            part = spectrum[index % north]
            out[group, col, :own] = part.real
            out[group, col, own:] = part.imag
    out[0, 0, own] = spectrum[north // 2].real
    out = out.reshape(rows * cols, 2 * own, 2 * rows, 4).transpose(0, 2, 3, 1)
    out = out.reshape(rows * cols, 2 * rows, 8 * own)
    return np.pad(out, ((0, 0), (0, 0), (0, LANES - 8 * own))).astype(np.float32)


def split(x):
    high = x.astype(BF16)
    return high, (x - high.astype(F32)).astype(BF16)


def dot(a, b, dims):
    return lax.dot_general(a, b, dims, preferred_element_type=F32)


def mul_table(x, high, low, dims=NN):
    x_high, x_low = split(x)
    return dot(x_high, high, dims) + (dot(x_low, high, dims) + dot(x_high, low, dims))


def table_mul(high, low, x, dims=NN):
    x_high, x_low = split(x)
    return dot(high, x_high, dims) + (dot(high, x_low, dims) + dot(low, x_high, dims))


def transform_list(values, sign):
    count = len(values)
    if count == 1:
        return values
    even = transform_list(values[0::2], sign)
    odd = transform_list(values[1::2], sign)
    first, second = [], []
    for k in range(count // 2):
        re, im = odd[k]
        if k == 0:
            turned = (re, im)
        elif 4 * k == count:
            turned = (im, -re) if sign < 0 else (-im, re)
        else:
            cos = float(np.cos(2.0 * np.pi * k / count))
            sin = sign * float(np.sin(2.0 * np.pi * k / count))
            if 8 * k == count or 8 * k == 3 * count:
                if cos * sin > 0:
                    turned = (cos * (re - im), cos * (re + im))
                else:
                    turned = (cos * (re + im), cos * (im - re))
            else:
                turned = (re * cos - im * sin, re * sin + im * cos)
        first.append((even[k][0] + turned[0], even[k][1] + turned[1]))
        second.append((even[k][0] - turned[0], even[k][1] - turned[1]))
    return first + second


def total(x):
    lanes = jnp.sum(jnp.sum(x, axis=0), axis=0, keepdims=True)
    return jnp.sum(lanes, axis=1, keepdims=True)


def neighbour(k, ints, rows, cols):
    code = ints[k]
    near_row = ints[ROW] + code // 3 - 1
    near_col = ints[COL] + code % 3 - 1
    inside = (near_row >= 0) & (near_row < rows) & (near_col >= 0) & (near_col < cols)
    device = jnp.clip(near_row * cols + near_col, 0, rows * cols - 1)
    return device, inside


def near_blocks(ints, vector, rows, cols):
    blocks = []
    for k in range(FOOTPRINT):
        device, inside = neighbour(k, ints, rows, cols)
        blocks.append(vector[device] * jnp.where(inside, 1.0, 0.0))
    return blocks


def apply_forward(tiles, copies, blocks, count, out, work):
    slots, width = tiles.shape[1:]
    parts = width // LANES
    squares = jnp.zeros((SUB, LANES), F32)
    for group, end in ((0, 4), (4, 8), (8, FOOTPRINT)):
        for k in range(group, end):
            copies[k].wait()
        spread = [
            [jnp.broadcast_to(blocks[k][p : p + 1], (SUB, LANES)) for p in range(parts)]
            for k in range(group, end)
        ]

        def step(t, squares, group=group, spread=spread):
            at = pl.multiple_of(t * SUB, SUB)
            sums = [None] * parts
            for k in range(len(spread)):
                for p in range(parts):
                    tile = tiles[group + k, pl.ds(at, SUB), p * LANES : (p + 1) * LANES]
                    term = tile * spread[k][p]
                    sums[p] = term if sums[p] is None else sums[p] + term
            acc = functools.reduce(jnp.add, sums)
            if group > 0:
                acc = acc + work[pl.ds(at, SUB), :]
            if group + len(spread) < FOOTPRINT:
                work[pl.ds(at, SUB), :] = acc
                return squares
            slot = at + lax.broadcasted_iota(jnp.int32, (SUB, LANES), 0)
            value = jnp.where(slot.astype(F32) < count, jnp.sum(acc, axis=1, keepdims=True), 0.0)
            if out is not None:
                out[pl.ds(at, SUB), :] = value
            return squares + value * value

        squares = lax.fori_loop(0, slots // SUB, step, squares, unroll=8)
    return jnp.sum(squares, axis=0, keepdims=True)


def apply_adjoint(tile, values):
    slots, width = tile.shape
    parts = width // LANES
    sums = [[None, None] for _ in range(parts)]
    for t in range(slots // SUB):
        rows = slice(t * SUB, (t + 1) * SUB)
        weight = values[rows, :]
        for p in range(parts):
            term = tile[rows, p * LANES : (p + 1) * LANES] * weight
            sums[p][t % 2] = term if t < 2 else sums[p][t % 2] + term
    return jnp.concatenate([jnp.sum(a + b, axis=0, keepdims=True) for a, b in sums], axis=0)


def send_adjoint(tile, values, k, ints, out, rows, cols):
    device, inside = neighbour(k, ints, rows, cols)
    block = jnp.where(inside, apply_adjoint(tile, values), 0.0)
    if len(out.shape) == 4:
        out[device, 0] = out[device, 0] + block
    else:
        out[device] = out[device] + block


def tile_copies(source, tiles, sems):
    copies = [
        pltpu.make_async_copy(source.at[0, 0, k], tiles.at[k], sems.at[k]) for k in range(FOOTPRINT)
    ]
    for copy in copies:
        copy.start()
    return copies


def start_kernel(
    sizes, codes, counts, damping, readings, depth, inclinations, declinations, turns, hats, resid,
    source, out, side, meta, codes_in, counts_in, damping_in, depth_in, angles, read, map_rows, tiles, values, sems, more,
):
    rows, cols, own, bands = sizes
    row, col = lax.axis_index("row"), lax.axis_index("col")
    _, turns_at, hats_at, end = side_rows(own, bands, rows)
    pairs = [
        (codes.at[0], codes_in),
        (counts, counts_in),
        (damping, damping_in),
        (depth, depth_in),
        (inclinations, angles.at[0]),
        (declinations, angles.at[1]),
        (readings.at[0], read),
        (turns, side.at[turns_at:hats_at]),
        (hats.at[row * cols + col], side.at[hats_at:end]),
        (resid, map_rows),
    ]
    first = [pltpu.make_async_copy(a, b, more.at[n]) for n, (a, b) in enumerate(pairs)]
    for copy in first:
        copy.start()
    copies = tile_copies(source, tiles, sems)
    out[...] = jnp.zeros(out.shape, F32)
    for copy in first:
        copy.wait()
    if len(out.shape) == 4:
        place_rows(out, lambda d, g: map_rows[(4 * d + g) * 4 : (4 * d + g + 1) * 4])
    ints = [codes_in[0, k] for k in range(FOOTPRINT)] + [counts_in[0, 0], row, col]
    meta[0:1, :] = jnp.full((1, LANES), counts_in[0, 0].astype(F32), F32)
    meta[1:2, :] = jnp.full((1, LANES), damping_in[0], F32)
    slots = read.shape[1]
    slot = lax.broadcasted_iota(jnp.int32, (1, slots), 1)
    live = jnp.where(slot < ints[COUNT], read[...], 0.0)
    for t in range(slots // LANES):
        square = jnp.broadcast_to(live[:, t * LANES : (t + 1) * LANES], (LANES, LANES))
        values[t * LANES : (t + 1) * LANES, :] = square.T
    trig = []
    for m in range(2):
        up = jnp.full((1, LANES), angles[0, m], F32)
        turn = jnp.full((1, LANES), angles[1, m], F32)
        flat = jnp.cos(up)
        trig += [jnp.sin(up), flat * jnp.cos(turn), flat * jnp.sin(turn)]
    put_weights(sizes, row, col, [depth_in[l] for l in range(LAYERS)], trig, side)
    for k in range(FOOTPRINT):
        copies[k].wait()
        send_adjoint(tiles.at[k], values, k, ints, out, rows, cols)


def place_rows(out, get):
    for d in range(out.shape[0]):
        for g in range(out.shape[1] - 1):
            out[d, 1 + g] = get(d, g)


def gather_kernel(arrived, everywhere):
    block = jnp.sum(arrived[:, 0] if len(arrived.shape) == 4 else arrived[...], axis=0)
    everywhere[...] = jnp.broadcast_to(block[None], everywhere.shape)


def normal_kernel(
    rows, cols, codes, meta, source, vector, arrived, turns, table, out, *refs
):
    (*apart, codes_in, tiles, sems, values, work, planes, codes_sem) = refs
    fetch = pltpu.make_async_copy(codes.at[0], codes_in, codes_sem.at[0])
    fetch.start()
    copies = tile_copies(source, tiles, sems)
    row, col = lax.axis_index("row"), lax.axis_index("col")
    fetch.wait()
    ints = [codes_in[0, k] for k in range(FOOTPRINT)] + [None, row, col]
    blocks = near_blocks(ints, vector, rows, cols)
    me = row * cols + col
    out[...] = jnp.zeros(out.shape, F32)
    ridge = meta[1:2, :] * vector[me]
    if apart:
        out[me] = ridge
    else:
        out[me, 0] = ridge

    def store(device, piece):
        if apart:
            apart[0][device] = piece
        else:
            for g in range(out.shape[1] - 1):
                out[device, 1 + g] = piece[4 * g : 4 * g + 4]

    north_transform(rows, cols, arrived, turns, table, planes, store)
    apply_forward(tiles, copies, blocks, meta[0:1, :], values, work)
    for k in range(FOOTPRINT):
        send_adjoint(tiles.at[k], values, k, ints, out, rows, cols)


def north_transform(rows, cols, arrived, turns, table, planes, store):
    width = planes.shape[1]
    each = width // cols
    own = HALF // cols
    for i in range(rows):
        for j in range(cols):
            if len(arrived.shape) == 4:
                for g in range(each // 4):
                    at = j * each + 4 * g
                    planes[i, at : at + 4, :] = arrived[i * cols + j, 1 + g]
            else:
                planes[i, j * each : (j + 1) * each, :] = arrived[i * cols + j]
    for group in range(rows):
        re = planes[0] * turns[0, group, 0:1]
        im = planes[0] * turns[1, group, 0:1]
        for i in range(1, rows):
            re = re + planes[i] * turns[0, group, i : i + 1]
            im = im + planes[i] * turns[1, group, i : i + 1]
        kind = min(group, 1)
        both = jnp.concatenate([re, im], axis=1)
        result = table_mul(table[kind, 0], table[kind, 1], both, NT)
        for j in range(cols):
            real, imag = result[j * own : (j + 1) * own], result[HALF + j * own : HALF + (j + 1) * own]
            store(group * cols + j, jnp.concatenate([real, imag], axis=1))


def pole(north, east, trig):
    square = north * north + east * east
    inverse = jnp.where(square > 0.0, lax.rsqrt(jnp.where(square > 0.0, square, 1.0)), 0.0)
    a0 = (trig[1] * north + trig[2] * east) * inverse
    a1 = (trig[4] * north + trig[5] * east) * inverse
    v0, v1 = trig[0], trig[3]
    scale = 1.0 / ((v0 * v0 + a0 * a0) * (v1 * v1 + a1 * a1))
    return (v0 * v1 - a0 * a1) * scale, -(v0 * a1 + v1 * a0) * scale, square * inverse


def side_rows(own, bands, rows):
    span = (own + 1) * bands
    turns = 2 * (1 + LAYERS) * span
    return span, turns, turns + 2 * bands, turns + 2 * bands + 2 * rows


def put_weights(sizes, row, col, depth, trig, side):
    rows, _, own, bands = sizes
    span = side_rows(own, bands, rows)[0]

    def put(part, q, at, value):
        base = (part * (1 + LAYERS) + q) * span + at
        side[base : base + value.shape[0], :] = value

    north_len, east_len = rows * LANES, bands * LANES
    scale = 1.0 / (north_len * east_len)
    start = jnp.where(
        row == 0, 0, jnp.where(row == 1, rows // 2, row // 2 + HALF * rows * (row % 2))
    )

    def signed(index, length):
        return jnp.where(index < length // 2, index, index - length).astype(F32) / length

    def north_of(shape):
        index = start + rows * (col * own + lax.broadcasted_iota(jnp.int32, shape, 0))
        return signed(index, north_len)

    def weights(re, im, radius):
        damp = [None] + [jnp.exp(radius * (-2.0 * np.pi * depth[l])) for l in range(LAYERS)]
        return [(re, im) if d is None else (re * d, im * d) for d in damp]

    lane = lax.broadcasted_iota(jnp.int32, (own, LANES), 1)
    north = north_of((own, LANES))
    for band in range(bands):
        east = signed(band + bands * lane, east_len)
        re, im, radius = pole(north, east, trig)
        if band == 0:
            re2, im2, _ = pole(north, jnp.where(lane == HALF, 0.5, east), trig)
            re, im = 0.5 * (re + re2), 0.5 * (im + im2)
        for q, (wr, wi) in enumerate(weights(re * scale, im * scale, radius)):
            put(0, q, band * own, wr)
            put(1, q, band * own, wi)
            put(0, q, bands * own, jnp.zeros((bands, LANES), F32))
            put(1, q, bands * own, jnp.zeros((bands, LANES), F32))

    @pl.when((row == 0) & (col == 0))
    def _():
        band = lax.broadcasted_iota(jnp.int32, (bands, LANES), 0)
        lanes = lax.broadcasted_iota(jnp.int32, (bands, LANES), 1)
        east = signed(band + bands * lanes, east_len)
        flipped = jnp.where((band == 0) & (lanes == HALF), 0.5, east)
        pairs = []
        for one, other in ((0.0, 0.0), (-0.5, 0.5)):
            re, im, radius = pole(jnp.full_like(east, one), east, trig)
            re2, im2, _ = pole(jnp.full_like(east, other), flipped, trig)
            half = 0.5 * scale
            pairs.append(weights(half * (re + re2), half * (im + im2), radius))
        for q in range(1 + LAYERS):
            (r0, i0), (r1, i1) = pairs[0][q], pairs[1][q]
            put(0, q, bands * own, 0.5 * (r0 - r1))
            put(1, q, bands * own, 0.5 * (i0 - i1))
            for b in range(bands):
                put(0, q, b * own, 0.5 * (r0 + r1)[b : b + 1])
                put(1, q, b * own, 0.5 * (i0 + i1)[b : b + 1])


def turn_rows(side, turns_at, band, bands):
    cos, sin = turns_at + band, turns_at + bands + band
    return side[cos : cos + 1, :], side[sin : sin + 1, :]


def east_table(tables, index):
    span = 2 * LANES
    return tables[2 * index * span : (2 * index + 1) * span], tables[
        (2 * index + 1) * span : (2 * index + 2) * span
    ]


def east_forward(get, sizes, side, tables, work):
    rows, _, own, bands = sizes
    turns_at = side_rows(own, bands, rows)[1]
    for g in range(own // SUB):
        values = transform_list([get(m, g) for m in range(bands)], -1.0)
        for b in range(bands):
            cos, sin = turn_rows(side, turns_at, b, bands)
            re, im = values[b]
            at = b * own + g * SUB
            work[at : at + SUB, :LANES] = re * cos - im * sin
            work[at : at + SUB, LANES:] = re * sin + im * cos
            if g == 0:
                re, im = values[(bands - b) % bands]
                re, im = re[0:1], -im[0:1]
                at = bands * own + b
                work[at : at + 1, :LANES] = re * cos - im * sin
                work[at : at + 1, LANES:] = re * sin + im * cos
    return mul_table(work[...], *east_table(tables, 0))


def weigh(spectrum, q, sizes, side, into, first):
    rows, _, own, bands = sizes
    span = side_rows(own, bands, rows)[0]
    re, im = spectrum[:, :LANES], spectrum[:, LANES:]
    wr = side[q * span : (q + 1) * span, :]
    wi = side[(1 + LAYERS + q) * span : (2 + LAYERS + q) * span, :]
    out_re, out_im = re * wr - im * wi, re * wi + im * wr
    main = own * bands
    if first:
        into[:, :LANES] = out_re[:main]
        into[:, LANES:] = out_im[:main]
    else:
        into[:, :LANES] += out_re[:main]
        into[:, LANES:] += out_im[:main]
    for b in range(bands):
        into[b * own : b * own + 1, :LANES] += out_re[main + b : main + b + 1]
        into[b * own : b * own + 1, LANES:] += out_im[main + b : main + b + 1]


def east_inverse(spectrum, sizes, side, tables, work, store):
    rows, _, own, bands = sizes
    turns_at = side_rows(own, bands, rows)[1]
    work[...] = mul_table(spectrum[...], *east_table(tables, 1))
    for g in range(own // SUB):
        values = []
        for b in range(bands):
            at = b * own + g * SUB
            re, im = work[at : at + SUB, :LANES], work[at : at + SUB, LANES:]
            cos, sin = turn_rows(side, turns_at, b, bands)
            values.append((re * cos + im * sin, im * cos - re * sin))
        values = transform_list(values, 1.0)
        for b in range(bands):
            store(b, g, *values[b])


def store_pieces(out, width):
    per_band = LANES // width

    def store(band, g, re, im):
        for s in range(per_band):
            cut = slice(s * width, (s + 1) * width)
            piece = jnp.concatenate([re[:, cut], im[:, cut]], axis=1)
            out[band * per_band + s, g * SUB : (g + 1) * SUB] = piece

    return store


def model_rows(vector, sizes, side, coarse):
    rows, cols, own, bands = sizes
    own2 = 2 * own
    for i in range(rows):
        for j in range(cols):
            block = vector[i * cols + j]
            for layer in range(LAYERS):
                coarse[layer, 2 * i : 2 * i + 2, j * LANES : (j + 1) * LANES] = block[
                    2 * layer : 2 * layer + 2
                ]
    out = []
    _, _, hats_at, end = side_rows(own, bands, rows)
    high, low = split(side[hats_at:end, :])
    tiles = cols * SRC_COLS // LANES
    lane = lax.broadcasted_iota(jnp.int32, (own2, LANES), 1) // SRC_COLS
    for layer in range(LAYERS):
        mixed = table_mul(high, low, coarse[layer], TN)
        whole = []
        for tile in range(tiles):
            joined = None
            for place in range(LANES // SRC_COLS):
                j = tile * (LANES // SRC_COLS) + place
                summed = None
                for part in range(4):
                    piece = mixed[part * own2 : (part + 1) * own2, j * LANES : (j + 1) * LANES]
                    shift = ((place - part) * SRC_COLS) % LANES
                    if shift:
                        piece = pltpu.roll(piece, shift, 1)
                    summed = piece if summed is None else summed + piece
                joined = summed if joined is None else jnp.where(lane == place, summed, joined)
            whole.append(joined)
        out.append(whole[0] if tiles == 1 else jnp.concatenate(whole, axis=1))
    return out


def model_mix(vector, scale, sizes, side, tables, coarse, fine, work, mixed, first):
    rows, cols, own, bands = sizes
    depth = cols * SRC_COLS
    planes = jnp.concatenate(model_rows(vector, sizes, side, coarse), axis=0)
    high, low = split(planes if scale is None else planes * scale)
    for c in range(bands // 2):
        at = 8 * LANES + c * depth
        table = tables[at : at + depth, :]
        fine[:, 2 * LANES * c : 2 * LANES * (c + 1)] = dot(high, table, NN) + dot(low, table, NN)
    for layer in range(LAYERS):

        def get(m, g, base=2 * own * layer):
            at = base + g * SUB
            cut = slice(m * LANES, (m + 1) * LANES)
            return fine[at : at + SUB, cut], fine[at + own : at + own + SUB, cut]

        spectrum = east_forward(get, sizes, side, tables, work)
        weigh(spectrum, 1 + layer, sizes, side, mixed, first and layer == 0)


def swap_groups(values, size):
    group = lax.broadcasted_iota(jnp.int32, values[0].shape, 1) // size
    bit = len(values) // 2
    while bit:
        low = (group & bit) == 0
        for s in range(len(values)):
            if not s & bit:
                x, y = values[s], values[s | bit]
                values[s] = jnp.where(low, x, pltpu.roll(y, bit * size, 1))
                values[s | bit] = jnp.where(low, pltpu.roll(x, LANES - bit * size, 1), y)
        bit //= 2
    return values


def sort_east(arrived, sizes, spec):
    rows, cols, own, bands = sizes
    count = 2 * cols
    for a in range(rows * cols // count):
        for g in range(own // SUB):
            values = []
            for s in range(count):
                at = 1 + 2 * g
                both = [arrived[a * count + s, at], arrived[a * count + s, at + 1]]
                values.append(jnp.concatenate(both, axis=0))
            values = swap_groups(values, LANES // count)
            for t in range(count):
                at = (t // cols) * own + g * SUB
                spec[t % cols, at : at + SUB, a * LANES : (a + 1) * LANES] = values[t]


def map_kernel(
    sizes, width, arrived, first, second, carry, tables, side, known, response,
    coarse, fine, work, mixed, back, *spec,
):
    rows, cols, own, bands = sizes
    if spec:
        sort_east(arrived, sizes, spec[0])
    spec = spec[0] if spec else arrived
    per = spec.shape[2] // LANES

    def get(m, g):
        cut = slice((m % per) * LANES, (m % per + 1) * LANES)
        at = g * SUB
        return spec[m // per, at : at + SUB, cut], spec[m // per, own + at : own + at + SUB, cut]

    spectrum = east_forward(get, sizes, side, tables, work)
    weigh(spectrum, 0, sizes, side, mixed, True)
    model_mix(first, carry[4, 0:1, 0:1], sizes, side, tables, coarse, fine, work, mixed, False)
    east_inverse(mixed, sizes, side, tables, back, store_pieces(known, width))
    model_mix(second, None, sizes, side, tables, coarse, fine, work, mixed, True)
    east_inverse(mixed, sizes, side, tables, back, store_pieces(response, width))


def direction_kernel(
    rows, cols, codes, meta, source, first, applied, second, measured, carry,
    codes_in, tiles, sems, work, codes_sem,
):
    fetch = pltpu.make_async_copy(codes.at[0], codes_in, codes_sem.at[0])
    fetch.start()
    copies = tile_copies(source, tiles, sems)
    row, col = lax.axis_index("row"), lax.axis_index("col")
    norm = total(first[...] * first[...])
    step = norm / total(first[...] * applied[...])
    residual = first[...] - step[None] * applied[...]
    norm_next = total(residual * residual)
    second[...] = residual + (norm_next / norm)[None] * first[...]
    ridge = meta[1:2, 0:1] * total(second[...] * second[...])
    me = row * cols + col
    carry[0] = step * first[me]
    carry[1] = second[me]
    for at, value in ((2, norm_next), (3, ridge), (4, step)):
        carry[at] = jnp.broadcast_to(value, carry.shape[1:])
    fetch.wait()
    ints = [codes_in[0, k] for k in range(FOOTPRINT)] + [None, row, col]
    blocks = near_blocks(ints, second, rows, cols)
    squares = apply_forward(tiles, copies, blocks, meta[0:1, :], None, work)
    measured[...] = jnp.broadcast_to(squares[None], measured.shape)


def last_step(measured, carry):
    squares = jnp.sum(measured[:, 0:1], axis=0)
    return carry[2, 0:1, 0:1] / (squares[:, 0:1] + carry[3, 0:1, 0:1])


def combine_kernel(measured, carry, known, response, out):
    out[...] = known[...] + last_step(measured, carry)[None] * response[...]


def finish_kernel(
    rows, cols, arrived, measured, carry, turns, table, coefficients, out, mixed, waves
):
    solved = carry[0] + last_step(measured, carry) * carry[1]
    for p in range(solved.shape[0]):
        coefficients[:, p * LANES : (p + 1) * LANES] = solved[p : p + 1]
    own = arrived.shape[1]
    width = out.shape[0]
    for i in range(rows):
        for j in range(cols):
            mixed[i, j * own : (j + 1) * own, :] = arrived[i * cols + j]
        kind = min(i, 1)
        both = mul_table(mixed[i], table[kind, 0], table[kind, 1], TN)
        top, bottom = both[:width], both[width:]
        waves[i, :, :LANES] = top[:, :LANES] - bottom[:, LANES:]
        waves[i, :, LANES:] = top[:, LANES:] + bottom[:, :LANES]
    for at in range(0, width, SUB):
        parts = [None] * rows
        for i in range(rows):
            re = waves[i, at : at + SUB, :LANES]
            im = waves[i, at : at + SUB, LANES:]
            for n in range(rows):
                term = re * turns[0, i, n : n + 1] + im * turns[1, i, n : n + 1]
                parts[n] = term if i == 0 else parts[n] + term
        for n in range(rows):
            out[at : at + SUB, n * LANES : (n + 1) * LANES] = parts[n]


def shape(*dims):
    return jax.ShapeDtypeStruct(dims, F32)


def scratch(*dims):
    return pltpu.VMEM(dims, F32)


def call(kernel, outs, ins, work=(), limit=SMALL):
    return pl.pallas_call(
        kernel,
        out_shape=outs,
        in_specs=[spec for spec, _ in ins],
        out_specs=jax.tree.map(lambda _: VMEM, outs),
        scratch_shapes=list(work),
        compiler_params=pltpu.CompilerParams(vmem_limit_bytes=limit),
    )(*[value for _, value in ins])


def exchange(pieces):
    return lax.all_to_all(pieces, BOTH, 0, 0, tiled=True)


def on_device(
    kernel_tiles, footprints, counts, readings, damping, layer_depth, inclinations, declinations,
    resid_grid,
):
    rows, cols = lax.axis_size("row"), lax.axis_size("col")
    devices = rows * cols
    slots, sources = kernel_tiles.shape[3:]
    parts = sources // LANES
    tile_east = resid_grid.shape[0]
    east = cols * tile_east
    bands = east // LANES
    own = HALF // cols
    width = east // devices
    sizes = (rows, cols, own, bands)

    turns = north_turns(rows)
    tables, east_turns = east_tables(east)
    hats = north_hat_table(rows, cols)

    joined = 2 * width == LANES
    everywhere = shape(devices, parts, LANES)
    beside = shape(devices, 1 + own // 4, 4, LANES) if joined else everywhere
    pieces = shape(devices, own, 2 * width)

    def apart(value):
        return HBM, pltpu.with_memory_space_constraint(value, pltpu.HBM)

    tile_scratch = scratch(FOOTPRINT, slots, sources)
    tile_sems = pltpu.SemaphoreType.DMA((FOOTPRINT,))
    codes_scratch = pltpu.SMEM((1, FOOTPRINT), jnp.int32)
    one_sem = pltpu.SemaphoreType.DMA((1,))
    resid = resid_grid if joined else resid_grid[:SUB]

    sums, side, meta = call(
        functools.partial(start_kernel, sizes),
        (beside, shape(side_rows(own, bands, rows)[-1], LANES), shape(2, LANES)),
        [apart(footprints), (ANY, counts), (ANY, damping)]
        + [
            apart(value)
            for value in (
                readings, layer_depth, inclinations, declinations,
                jnp.asarray(east_turns), jnp.asarray(hats), resid, kernel_tiles,
            )
        ],
        [
            codes_scratch,
            pltpu.SMEM((1, 1), jnp.int32),
            pltpu.SMEM((1,), F32),
            pltpu.SMEM((LAYERS,), F32),
            pltpu.SMEM((2, 2), F32),
            scratch(1, slots),
            scratch(*resid.shape),
            tile_scratch,
            scratch(slots, LANES),
            tile_sems,
            pltpu.SemaphoreType.DMA((10,)),
        ],
    )
    sums = exchange(sums)
    right_all = call(gather_kernel, everywhere, [(VMEM, sums)])
    if not joined:
        right_all, resid_grid = lax.optimization_barrier((right_all, resid_grid))
    planes = sums if joined else exchange(resid_grid.reshape(devices, -1, LANES))
    right_side = exchange(right_all)

    sums = call(
        functools.partial(normal_kernel, rows, cols),
        beside if joined else (everywhere, pieces),
        [
            apart(footprints),
            (VMEM, meta),
            apart(kernel_tiles),
            (VMEM, right_side),
            (VMEM, planes),
            (VMEM, turns),
            (VMEM, north_forward_table()),
        ],
        [codes_scratch, tile_scratch, tile_sems, scratch(slots, LANES), scratch(slots, LANES)]
        + [scratch(rows, width, LANES), one_sem],
    )
    if not joined:
        sums, spectrum = sums
    sums = exchange(sums)
    applied_all = call(gather_kernel, everywhere, [(VMEM, sums)])
    applied = exchange(applied_all)
    if joined:
        spectrum, sorted_work = sums, [scratch(cols, 2 * own, tile_east)]
    else:
        spectrum, sorted_work = exchange(spectrum), []
        spectrum = spectrum.reshape(devices, own, 2, cols, width // cols).transpose(3, 2, 1, 0, 4)
        spectrum = spectrum.reshape(cols, 2 * own, tile_east)

    second, measured, carry = call(
        functools.partial(direction_kernel, rows, cols),
        (everywhere, everywhere, shape(5, parts, LANES)),
        [apart(footprints), (VMEM, meta), apart(kernel_tiles), (VMEM, right_side), (VMEM, applied)],
        [codes_scratch, tile_scratch, tile_sems, scratch(slots, LANES), one_sem],
    )
    work = [
        scratch(LAYERS, 2 * rows, cols * LANES),
        scratch(LAYERS * 2 * own, east),
        scratch((own + 1) * bands, 2 * LANES),
        scratch(own * bands, 2 * LANES),
        scratch(own * bands, 2 * LANES),
    ]
    known, response = call(
        functools.partial(map_kernel, sizes, width),
        (pieces, pieces),
        [
            (VMEM, spectrum),
            (VMEM, right_side),
            (VMEM, second),
            (VMEM, carry),
            (VMEM, tables),
            (VMEM, side),
        ],
        work + sorted_work,
    )
    measured = exchange(measured)
    outgoing = call(
        combine_kernel,
        pieces,
        [(VMEM, measured), (VMEM, carry), (VMEM, known), (VMEM, response)],
    )
    coefficients, rtp_map = call(
        functools.partial(finish_kernel, rows, cols),
        (shape(1, sources), shape(width, rows * LANES)),
        [
            (VMEM, exchange(outgoing)),
            (VMEM, measured),
            (VMEM, carry),
            (VMEM, turns),
            (VMEM, north_inverse_table()),
        ],
        [scratch(rows, HALF, 2 * width), scratch(rows, width, 2 * LANES)],
    )
    return coefficients.reshape(1, 1, sources), rtp_map


def solution(mesh):
    in_specs = (
        P("row", "col", None, None, None),
        P("row", "col", None),
        P("row", "col"),
        P("row", "col", None),
        P(),
        P(),
        P(),
        P(),
        P("col", "row"),
    )
    out_specs = (P("row", "col", None), P(("row", "col"), None))
    return jax.shard_map(
        on_device, mesh=mesh, in_specs=in_specs, out_specs=out_specs, check_vma=False
    )
```

```python
import functools

import jax
import jax.numpy as jnp
import ml_dtypes
import numpy as np
from jax import lax
from jax.experimental import pallas as pl
from jax.experimental.pallas import tpu as pltpu
from jax.sharding import PartitionSpec as P

SRC_ROWS = 8
SRC_COLS = 32
LAYERS = 2
REFINE = 16
FOOTPRINT = 9
LANES = 128
SUB = 8
HALF = 64
BOTH = ("row", "col")
COUNT, ROW, COL = 9, 10, 11
MIB = 1024 * 1024
SMALL, LARGE = 24 * MIB, 62 * MIB
F32 = jnp.float32
BF16 = jnp.bfloat16

VMEM = pl.BlockSpec(memory_space=pltpu.VMEM)
SMEM = pl.BlockSpec(memory_space=pltpu.SMEM)
HBM = pl.BlockSpec(memory_space=pltpu.HBM)
NN = (((1,), (0,)), ((), ()))
NT = (((1,), (1,)), ((), ()))
TN = (((0,), (0,)), ((), ()))


def split_table(table):
    high = table.astype(ml_dtypes.bfloat16)
    low = (table - high.astype(np.float64)).astype(ml_dtypes.bfloat16)
    return np.stack([high, low])


def group_start(group, rows):
    if group == 0:
        return 0
    if group == 1:
        return rows // 2
    return group // 2 + HALF * rows * (group % 2)


def unit_turn(product, period):
    angle = 2.0 * np.pi * (product % period) / period
    return np.cos(angle), np.sin(angle)


def north_starts(rows):
    return [0, rows // 2] + list(range(1, rows // 2))


def north_turns(rows):
    north = rows * LANES
    starts = np.array(north_starts(rows))
    cos, sin = unit_turn(starts[:, None] * np.arange(north // 2)[None, :], north)
    turns = np.stack([cos, -sin]).reshape(2, len(starts), rows // 2, LANES)
    return turns.astype(np.float32)


def north_forward_tables():
    cos, sin = unit_turn(np.outer(np.arange(LANES), np.arange(LANES)), LANES)
    plain = np.block([[cos, sin], [-sin, cos]])
    packed = np.concatenate([cos[:HALF], -sin[:HALF]], 0)
    packed[HALF] = 1.0 - 2.0 * (np.arange(LANES) % 2)
    return split_table(packed), split_table(plain)


def north_inverse_tables():
    cos, sin = unit_turn(np.outer(np.arange(LANES), np.arange(LANES)), LANES)
    plain = 2.0 * np.concatenate([cos, sin], 1)
    packed = plain[:HALF].copy()
    packed[0, :LANES] = 1.0
    packed[0, LANES:] = 2.0 * (np.arange(LANES) % 2) - 1.0
    return split_table(packed), split_table(plain)


def east_tables(east):
    bands = east // LANES
    cos, sin = unit_turn(np.outer(np.arange(LANES), np.arange(LANES)), LANES)
    forward = np.block([[cos, -sin], [sin, cos]])
    inverse = np.block([[cos, sin], [-sin, cos]])
    turn_cos, turn_sin = unit_turn(np.outer(np.arange(bands), np.arange(LANES)), east)
    turns = np.concatenate([turn_cos, -turn_sin]).astype(np.float32)
    up_east = hat_table(east, east // REFINE).reshape(-1, 2 * LANES, east // REFINE)
    up_east = up_east.transpose(0, 2, 1).reshape(-1, 2 * LANES).astype(ml_dtypes.bfloat16)
    tables = [split_table(forward), split_table(inverse)]
    return np.concatenate([t.reshape(-1, 2 * LANES) for t in tables] + [up_east]), turns


def hat_table(fine_count, coarse_count):
    offset = (np.arange(fine_count)[:, None] + 0.5) / REFINE - 0.5 - np.arange(coarse_count)[None, :]
    return np.maximum(0.0, 1.0 - np.abs(offset))


def north_hat_table(rows, cols):
    north = rows * LANES
    coarse = rows * SRC_ROWS
    own = HALF // cols
    spectrum = np.fft.fft(hat_table(north, coarse), axis=0)
    out = np.zeros((rows, cols, 2 * own, coarse))
    for group in range(rows):
        for col in range(cols):
            index = group_start(group, rows) + rows * (col * own + np.arange(own))
            part = spectrum[index % north]
            out[group, col, :own] = part.real
            out[group, col, own:] = part.imag
    out[0, 0, own] = spectrum[north // 2].real
    out = out.reshape(rows * cols, 2 * own, 2 * rows, 4).transpose(0, 2, 3, 1)
    out = out.reshape(rows * cols, 2 * rows, 8 * own)
    return np.pad(out, ((0, 0), (0, 0), (0, LANES - 8 * own))).astype(np.float32)


def split(x):
    high = x.astype(BF16)
    return high, (x - high.astype(F32)).astype(BF16)


def dot(a, b, dims):
    return lax.dot_general(a, b, dims, preferred_element_type=F32)


def mul_table(x, high, low, dims=NN):
    x_high, x_low = split(x)
    return dot(x_high, high, dims) + (dot(x_low, high, dims) + dot(x_high, low, dims))


def table_mul(high, low, x, dims=NN):
    x_high, x_low = split(x)
    return dot(high, x_high, dims) + (dot(high, x_low, dims) + dot(low, x_high, dims))


def transform_list(values, sign):
    count = len(values)
    if count == 1:
        return values
    even = transform_list(values[0::2], sign)
    odd = transform_list(values[1::2], sign)
    first, second = [], []
    for k in range(count // 2):
        re, im = odd[k]
        if k == 0:
            turned = (re, im)
        elif 4 * k == count:
            turned = (im, -re) if sign < 0 else (-im, re)
        else:
            cos = float(np.cos(2.0 * np.pi * k / count))
            sin = sign * float(np.sin(2.0 * np.pi * k / count))
            if 8 * k == count or 8 * k == 3 * count:
                if cos * sin > 0:
                    turned = (cos * (re - im), cos * (re + im))
                else:
                    turned = (cos * (re + im), cos * (im - re))
            else:
                turned = (re * cos - im * sin, re * sin + im * cos)
        first.append((even[k][0] + turned[0], even[k][1] + turned[1]))
        second.append((even[k][0] - turned[0], even[k][1] - turned[1]))
    return first + second


def total(x):
    lanes = jnp.sum(jnp.sum(x, axis=0), axis=0, keepdims=True)
    return jnp.sum(lanes, axis=1, keepdims=True)


def neighbour(k, ints, rows, cols):
    code = ints[k]
    near_row = ints[ROW] + code // 3 - 1
    near_col = ints[COL] + code % 3 - 1
    inside = (near_row >= 0) & (near_row < rows) & (near_col >= 0) & (near_col < cols)
    device = jnp.clip(near_row * cols + near_col, 0, rows * cols - 1)
    return device, inside


def near_blocks(ints, vector, rows, cols):
    blocks = []
    for k in range(FOOTPRINT):
        device, inside = neighbour(k, ints, rows, cols)
        blocks.append(vector[device] * jnp.where(inside, 1.0, 0.0))
    return blocks


def apply_forward(tiles, copies, blocks, count, out, work):
    slots, width = tiles.shape[1:]
    parts = width // LANES
    squares = jnp.zeros((SUB, LANES), F32)
    for group, end in ((0, 4), (4, 8), (8, FOOTPRINT)):
        for k in range(group, end if copies else group):
            copies[k].wait()
        spread = [
            [jnp.broadcast_to(blocks[k][p : p + 1], (SUB, LANES)) for p in range(parts)]
            for k in range(group, end)
        ]

        def step(t, squares, group=group, spread=spread):
            at = pl.multiple_of(t * SUB, SUB)
            sums = [None] * parts
            for k in range(len(spread)):
                for p in range(parts):
                    tile = tiles[group + k, pl.ds(at, SUB), p * LANES : (p + 1) * LANES]
                    term = tile * spread[k][p]
                    sums[p] = term if sums[p] is None else sums[p] + term
            acc = functools.reduce(jnp.add, sums)
            if group > 0:
                acc = acc + work[pl.ds(at, SUB), :]
            if group + len(spread) < FOOTPRINT:
                work[pl.ds(at, SUB), :] = acc
                return squares
            slot = at + lax.broadcasted_iota(jnp.int32, (SUB, LANES), 0)
            value = jnp.where(slot.astype(F32) < count, jnp.sum(acc, axis=1, keepdims=True), 0.0)
            if out is not None:
                out[pl.ds(at, SUB), :] = value
            return squares + value * value

        squares = lax.fori_loop(0, slots // SUB, step, squares, unroll=8)
    return jnp.sum(squares, axis=0, keepdims=True)


def apply_adjoint(tile, values):
    slots, width = tile.shape
    parts = width // LANES
    sums = [[None, None] for _ in range(parts)]
    for t in range(slots // SUB):
        rows = slice(t * SUB, (t + 1) * SUB)
        weight = values[rows, :]
        for p in range(parts):
            term = tile[rows, p * LANES : (p + 1) * LANES] * weight
            sums[p][t % 2] = term if t < 2 else sums[p][t % 2] + term
    return jnp.concatenate([jnp.sum(a + b, axis=0, keepdims=True) for a, b in sums], axis=0)


def send_adjoint(tile, values, k, ints, out, rows, cols):
    device, inside = neighbour(k, ints, rows, cols)
    block = jnp.where(inside, apply_adjoint(tile, values), 0.0)
    if len(out.shape) == 4:
        out[device, 0] = out[device, 0] + block
    else:
        out[device] = out[device] + block


def tile_copies(source, tiles, sems):
    copies = [
        pltpu.make_async_copy(source.at[0, 0, k], tiles.at[k], sems.at[k]) for k in range(FOOTPRINT)
    ]
    for copy in copies:
        copy.start()
    return copies


def start_kernel(
    sizes, codes, counts, damping, readings, depth, inclinations, declinations, turns, hats, resid,
    source, out, side, meta, codes_in, depth_in, angles, read, map_rows, tiles, values, sems, more,
):
    rows, cols, own, bands = sizes
    row, col = lax.axis_index("row"), lax.axis_index("col")
    _, turns_at, hats_at, end = side_rows(own, bands, rows)
    pairs = [
        (codes.at[0], codes_in),
        (depth, depth_in),
        (inclinations, angles.at[0]),
        (declinations, angles.at[1]),
        (readings.at[0], read),
        (turns, side.at[turns_at:hats_at]),
        (hats.at[row * cols + col], side.at[hats_at:end]),
        (resid, map_rows),
    ]
    first = [pltpu.make_async_copy(a, b, more.at[n]) for n, (a, b) in enumerate(pairs)]
    for copy in first:
        copy.start()
    copies = tile_copies(source, tiles, sems)
    for copy in first:
        copy.wait()
    width = map_rows.shape[0] // rows
    for i in range(rows):
        for g in range(width // 4):
            at = i * width + 4 * g
            out[i, FOOTPRINT + g] = map_rows[at : at + 4]
    ints = [codes_in[0, k] for k in range(FOOTPRINT)] + [None, row, col]
    meta[0:1, :] = jnp.broadcast_to(counts[...].astype(F32), (1, LANES))
    for k in range(FOOTPRINT):
        meta[2 + k : 3 + k, :] = jnp.full((1, LANES), codes_in[0, k].astype(F32), F32)
    meta[1:2, :] = jnp.broadcast_to(damping[...], (1, LANES))
    slots = read.shape[1]
    slot = lax.broadcasted_iota(jnp.int32, (1, slots), 1)
    live = jnp.where(slot < counts[...], read[...], 0.0)
    for t in range(slots // LANES):
        square = jnp.broadcast_to(live[:, t * LANES : (t + 1) * LANES], (LANES, LANES))
        values[t * LANES : (t + 1) * LANES, :] = square.T
    trig = []
    for m in range(2):
        up = jnp.full((1, LANES), angles[0, m], F32)
        turn = jnp.full((1, LANES), angles[1, m], F32)
        flat = jnp.cos(up)
        trig += [jnp.sin(up), flat * jnp.cos(turn), flat * jnp.sin(turn)]
    put_weights(sizes, row, col, [depth_in[l] for l in range(LAYERS)], trig, side)
    for k in range(FOOTPRINT):
        copies[k].wait()
        block = apply_adjoint(tiles.at[k], values)
        out[:, ints[k]] = jnp.broadcast_to(block[None], (rows,) + block.shape)


def place_rows(out, get):
    for d in range(out.shape[0]):
        for g in range(out.shape[1] - 1):
            out[d, 1 + g] = get(d, g)


def column_kernel(rows, cols, arrived, out):
    row, col = lax.axis_index("row"), lax.axis_index("col")
    for code in range(FOOTPRINT):
        target, step = row + code // 3 - 1, code % 3 - 1
        block = None
        for a in range(3):
            source = target - (a - 1)
            here = (source >= 0) & (source < rows)
            part = arrived[jnp.clip(source, 0, rows - 1), 3 * a + step + 1]
            part = jnp.where(here, part, 0.0)
            block = part if block is None else block + part
        inside = (target >= 0) & (target < rows) & (col + step >= 0) & (col + step < cols)
        block = jnp.where(inside, block, 0.0)
        out[:, code] = jnp.broadcast_to(block[None], (cols,) + block.shape)


def share_kernel(arrived, own, everywhere):
    block = jnp.sum(arrived[:, 0] if len(arrived.shape) == 4 else arrived[...], axis=0)
    both = jnp.stack([own[...], block])
    everywhere[...] = jnp.broadcast_to(both[None], everywhere.shape)


def normal_kernel(
    rows, cols, meta, source, summed, arrived, turns, packed, plain, out, own, *refs
):
    (*apart, near, values, work, planes) = refs
    tiles, copies = source.at[0, 0], None
    row, col = lax.axis_index("row"), lax.axis_index("col")
    ints = [meta[2 + k, 0].astype(jnp.int32) for k in range(FOOTPRINT)] + [None, row, col]
    for code in range(FOOTPRINT):
        block = None
        for j in range(cols):
            step = col + code % 3 - 1 - j
            part = summed[j, 3 * (code // 3) + jnp.clip(step, -1, 1) + 1]
            part = jnp.where((step >= -1) & (step <= 1), part, 0.0)
            block = part if block is None else block + part
        near[code] = block
    blocks = [near[ints[k]] for k in range(FOOTPRINT)]
    me = row * cols + col
    out[...] = jnp.zeros(out.shape, F32)
    own[...] = near[FOOTPRINT // 2]
    ridge = meta[1:2, :] * own[...]
    if apart:
        out[me] = ridge
    else:
        out[me, 0] = ridge

    def store(device, piece):
        if apart:
            apart[0][device] = piece
        else:
            for g in range(out.shape[1] - 1):
                out[device, 1 + g] = piece[4 * g : 4 * g + 4]

    north_transform(rows, cols, arrived, turns, (packed, plain), planes, store)
    apply_forward(tiles, copies, blocks, meta[0:1, :], values, work)
    for k in range(FOOTPRINT):
        send_adjoint(tiles.at[k], values, k, ints, out, rows, cols)


def north_transform(rows, cols, arrived, turns, tables, planes, store):
    own = HALF // cols
    near, count = rows // 2, planes.shape[1]
    for i in range(rows):
        for g in range(count // 4):
            planes[i, 4 * g : 4 * g + 4, :] = arrived[i, FOOTPRINT + g]
    for i in range(near):
        one, other = planes[i], planes[i + near]
        planes[i] = one + other
        planes[i + near] = one - other
    packed, plain = tables
    for n, start in enumerate(north_starts(rows)):
        base = near * (start % 2)
        re, im = None, None
        for i in range(near):
            plane = planes[base + i]
            a = plane if start == 0 else plane * turns[0, n, i : i + 1]
            re = a if re is None else re + a
            if start:
                a = plane * turns[1, n, i : i + 1]
                im = a if im is None else im + a
        if start == 0:
            result = table_mul(packed[0], packed[1], re, NT)
        else:
            result = table_mul(plain[0], plain[1], jnp.concatenate([re, im], axis=1), NT)
        imag_at = result.shape[0] // 2
        groups = [n] if n < 2 else [2 * start, 2 * start + 1]
        for h, group in enumerate(groups):
            for j in range(cols):
                at = h * HALF + j * own
                real, imag = result[at : at + own], result[imag_at + at : imag_at + at + own]
                store(group * cols + j, jnp.concatenate([real, imag], axis=1))


def pole(north, east, trig):
    square = north * north + east * east
    inverse = jnp.where(square > 0.0, lax.rsqrt(jnp.where(square > 0.0, square, 1.0)), 0.0)
    a0 = (trig[1] * north + trig[2] * east) * inverse
    a1 = (trig[4] * north + trig[5] * east) * inverse
    v0, v1 = trig[0], trig[3]
    scale = 1.0 / ((v0 * v0 + a0 * a0) * (v1 * v1 + a1 * a1))
    return (v0 * v1 - a0 * a1) * scale, -(v0 * a1 + v1 * a0) * scale, square * inverse


def side_rows(own, bands, rows):
    span = (own + 1) * bands
    turns = 2 * (1 + LAYERS) * span
    return span, turns, turns + 2 * bands, turns + 2 * bands + 2 * rows


def put_weights(sizes, row, col, depth, trig, side):
    rows, _, own, bands = sizes
    span = side_rows(own, bands, rows)[0]

    def put(part, q, at, value):
        base = (part * (1 + LAYERS) + q) * span + at
        side[base : base + value.shape[0], :] = value

    north_len, east_len = rows * LANES, bands * LANES
    scale = 1.0 / (north_len * east_len)
    start = jnp.where(
        row == 0, 0, jnp.where(row == 1, rows // 2, row // 2 + HALF * rows * (row % 2))
    )

    def signed(index, length):
        return jnp.where(index < length // 2, index, index - length).astype(F32) / length

    def north_of(shape):
        index = start + rows * (col * own + lax.broadcasted_iota(jnp.int32, shape, 0))
        return signed(index, north_len)

    def weights(re, im, radius):
        damp = [None] + [jnp.exp(radius * (-2.0 * np.pi * depth[l])) for l in range(LAYERS)]
        return [(re, im) if d is None else (re * d, im * d) for d in damp]

    lane = lax.broadcasted_iota(jnp.int32, (own, LANES), 1)
    north = north_of((own, LANES))
    for band in range(bands):
        east = signed(band + bands * lane, east_len)
        re, im, radius = pole(north, east, trig)
        if band == 0:
            re2, im2, _ = pole(north, jnp.where(lane == HALF, 0.5, east), trig)
            re, im = 0.5 * (re + re2), 0.5 * (im + im2)
        for q, (wr, wi) in enumerate(weights(re * scale, im * scale, radius)):
            put(0, q, band * own, wr)
            put(1, q, band * own, wi)
            put(0, q, bands * own, jnp.zeros((bands, LANES), F32))
            put(1, q, bands * own, jnp.zeros((bands, LANES), F32))

    @pl.when((row == 0) & (col == 0))
    def _():
        band = lax.broadcasted_iota(jnp.int32, (bands, LANES), 0)
        lanes = lax.broadcasted_iota(jnp.int32, (bands, LANES), 1)
        east = signed(band + bands * lanes, east_len)
        flipped = jnp.where((band == 0) & (lanes == HALF), 0.5, east)
        pairs = []
        for one, other in ((0.0, 0.0), (-0.5, 0.5)):
            re, im, radius = pole(jnp.full_like(east, one), east, trig)
            re2, im2, _ = pole(jnp.full_like(east, other), flipped, trig)
            half = 0.5 * scale
            pairs.append(weights(half * (re + re2), half * (im + im2), radius))
        for q in range(1 + LAYERS):
            (r0, i0), (r1, i1) = pairs[0][q], pairs[1][q]
            put(0, q, bands * own, 0.5 * (r0 - r1))
            put(1, q, bands * own, 0.5 * (i0 - i1))
            for b in range(bands):
                put(0, q, b * own, 0.5 * (r0 + r1)[b : b + 1])
                put(1, q, b * own, 0.5 * (i0 + i1)[b : b + 1])


def turn_rows(side, turns_at, band, bands):
    cos, sin = turns_at + band, turns_at + bands + band
    return side[cos : cos + 1, :], side[sin : sin + 1, :]


def east_table(tables, index):
    span = 2 * LANES
    return tables[2 * index * span : (2 * index + 1) * span], tables[
        (2 * index + 1) * span : (2 * index + 2) * span
    ]


def east_forward(get, sizes, side, tables, work):
    rows, _, own, bands = sizes
    turns_at = side_rows(own, bands, rows)[1]
    for g in range(own // SUB):
        values = transform_list([get(m, g) for m in range(bands)], -1.0)
        for b in range(bands):
            cos, sin = turn_rows(side, turns_at, b, bands)
            re, im = values[b]
            at = b * own + g * SUB
            work[at : at + SUB, :LANES] = re * cos - im * sin
            work[at : at + SUB, LANES:] = re * sin + im * cos
            if g == 0:
                re, im = values[(bands - b) % bands]
                re, im = re[0:1], -im[0:1]
                at = bands * own + b
                work[at : at + 1, :LANES] = re * cos - im * sin
                work[at : at + 1, LANES:] = re * sin + im * cos
    return mul_table(work[...], *east_table(tables, 0))


def weigh(spectrum, q, sizes, side, into, first):
    rows, _, own, bands = sizes
    span = side_rows(own, bands, rows)[0]
    re, im = spectrum[:, :LANES], spectrum[:, LANES:]
    wr = side[q * span : (q + 1) * span, :]
    wi = side[(1 + LAYERS + q) * span : (2 + LAYERS + q) * span, :]
    out_re, out_im = re * wr - im * wi, re * wi + im * wr
    main = own * bands
    if first:
        into[:, :LANES] = out_re[:main]
        into[:, LANES:] = out_im[:main]
    else:
        into[:, :LANES] += out_re[:main]
        into[:, LANES:] += out_im[:main]
    for b in range(bands):
        into[b * own : b * own + 1, :LANES] += out_re[main + b : main + b + 1]
        into[b * own : b * own + 1, LANES:] += out_im[main + b : main + b + 1]


def east_inverse(spectrum, sizes, side, tables, work, store):
    rows, _, own, bands = sizes
    turns_at = side_rows(own, bands, rows)[1]
    work[...] = mul_table(spectrum[...], *east_table(tables, 1))
    for g in range(own // SUB):
        values = []
        for b in range(bands):
            at = b * own + g * SUB
            re, im = work[at : at + SUB, :LANES], work[at : at + SUB, LANES:]
            cos, sin = turn_rows(side, turns_at, b, bands)
            values.append((re * cos + im * sin, im * cos - re * sin))
        values = transform_list(values, 1.0)
        for b in range(bands):
            store(b, g, *values[b])


def store_pieces(out, width):
    per_band = LANES // width

    def store(band, g, re, im):
        for s in range(per_band):
            cut = slice(s * width, (s + 1) * width)
            piece = jnp.concatenate([re[:, cut], im[:, cut]], axis=1)
            out[band * per_band + s, g * SUB : (g + 1) * SUB] = piece

    return store


def model_rows(vector, sizes, side, coarse):
    rows, cols, own, bands = sizes
    own2 = 2 * own
    for i in range(rows):
        for j in range(cols):
            block = vector[i * cols + j]
            for layer in range(LAYERS):
                coarse[layer, 2 * i : 2 * i + 2, j * LANES : (j + 1) * LANES] = block[
                    2 * layer : 2 * layer + 2
                ]
    out = []
    _, _, hats_at, end = side_rows(own, bands, rows)
    high, low = split(side[hats_at:end, :])
    tiles = cols * SRC_COLS // LANES
    lane = lax.broadcasted_iota(jnp.int32, (own2, LANES), 1) // SRC_COLS
    for layer in range(LAYERS):
        mixed = table_mul(high, low, coarse[layer], TN)
        whole = []
        for tile in range(tiles):
            joined = None
            for place in range(LANES // SRC_COLS):
                j = tile * (LANES // SRC_COLS) + place
                summed = None
                for part in range(4):
                    piece = mixed[part * own2 : (part + 1) * own2, j * LANES : (j + 1) * LANES]
                    shift = ((place - part) * SRC_COLS) % LANES
                    if shift:
                        piece = pltpu.roll(piece, shift, 1)
                    summed = piece if summed is None else summed + piece
                joined = summed if joined is None else jnp.where(lane == place, summed, joined)
            whole.append(joined)
        out.append(whole[0] if tiles == 1 else jnp.concatenate(whole, axis=1))
    return out


def model_mix(vector, scale, sizes, side, tables, coarse, fine, work, mixed, first):
    rows, cols, own, bands = sizes
    depth = cols * SRC_COLS
    planes = jnp.concatenate(model_rows(vector, sizes, side, coarse), axis=0)
    high, low = split(planes if scale is None else planes * scale)
    for c in range(bands // 2):
        at = 8 * LANES + c * depth
        table = tables[at : at + depth, :]
        fine[:, 2 * LANES * c : 2 * LANES * (c + 1)] = dot(high, table, NN) + dot(low, table, NN)
    for layer in range(LAYERS):

        def get(m, g, base=2 * own * layer):
            at = base + g * SUB
            cut = slice(m * LANES, (m + 1) * LANES)
            return fine[at : at + SUB, cut], fine[at + own : at + own + SUB, cut]

        spectrum = east_forward(get, sizes, side, tables, work)
        weigh(spectrum, 1 + layer, sizes, side, mixed, first and layer == 0)


def sort_east(arrived, sizes, spec):
    rows, cols, own, bands = sizes
    left = lax.broadcasted_iota(jnp.int32, (SUB, LANES), 1) < HALF
    for j in range(cols):
        for i in range(0, rows, 2):
            for g in range(own // SUB):
                pair = []
                for source in (i * cols + j, (i + 1) * cols + j):
                    at = 1 + 2 * g
                    both = [arrived[source, at], arrived[source, at + 1]]
                    pair.append(jnp.concatenate(both, axis=0))
                cut = slice(i * HALF, (i + 2) * HALF)
                at = g * SUB
                spec[j, at : at + SUB, cut] = jnp.where(left, pair[0], pltpu.roll(pair[1], HALF, 1))
                at = own + g * SUB
                spec[j, at : at + SUB, cut] = jnp.where(left, pltpu.roll(pair[0], HALF, 1), pair[1])


def map_kernel(
    sizes, width, arrived, shared, second, carry, tables, side, known, response,
    coarse, fine, work, mixed, back, *spec,
):
    rows, cols, own, bands = sizes
    if spec:
        sort_east(arrived, sizes, spec[0])
    spec = spec[0] if spec else arrived
    per = spec.shape[2] // LANES

    def get(m, g):
        cut = slice((m % per) * LANES, (m % per + 1) * LANES)
        at = g * SUB
        return spec[m // per, at : at + SUB, cut], spec[m // per, own + at : own + at + SUB, cut]

    spectrum = east_forward(get, sizes, side, tables, work)
    weigh(spectrum, 0, sizes, side, mixed, True)
    model_mix(shared.at[:, 0], carry[4, 0:1, 0:1], sizes, side, tables, coarse, fine, work, mixed, False)
    east_inverse(mixed, sizes, side, tables, back, store_pieces(known, width))
    model_mix(second, None, sizes, side, tables, coarse, fine, work, mixed, True)
    east_inverse(mixed, sizes, side, tables, back, store_pieces(response, width))


def direction_kernel(
    rows, cols, meta, source, shared, second, measured, carry,
    work,
):
    tiles, copies = source.at[0, 0], None
    row, col = lax.axis_index("row"), lax.axis_index("col")
    first, applied = shared.at[:, 0], shared.at[:, 1]
    norm = total(first[...] * first[...])
    step = norm / total(first[...] * applied[...])
    residual = first[...] - step[None] * applied[...]
    norm_next = total(residual * residual)
    second[...] = residual + (norm_next / norm)[None] * first[...]
    ridge = meta[1:2, 0:1] * total(second[...] * second[...])
    me = row * cols + col
    carry[0] = step * first[me]
    carry[1] = second[me]
    for at, value in ((2, norm_next), (3, ridge), (4, step)):
        carry[at] = jnp.broadcast_to(value, carry.shape[1:])
    ints = [meta[2 + k, 0].astype(jnp.int32) for k in range(FOOTPRINT)] + [None, row, col]
    blocks = near_blocks(ints, second, rows, cols)
    squares = apply_forward(tiles, copies, blocks, meta[0:1, :], None, work)
    measured[...] = jnp.broadcast_to(squares[None], measured.shape)


def last_step(measured, carry):
    squares = jnp.sum(measured[:, 0:1], axis=0)
    return carry[2, 0:1, 0:1] / (squares[:, 0:1] + carry[3, 0:1, 0:1])


def combine_kernel(measured, carry, known, response, out):
    out[...] = known[...] + last_step(measured, carry)[None] * response[...]


def finish_kernel(
    rows, cols, arrived, measured, carry, turns, packed, plain, coefficients, out, mixed, waves
):
    solved = carry[0] + last_step(measured, carry) * carry[1]
    for p in range(solved.shape[0]):
        coefficients[:, p * LANES : (p + 1) * LANES] = solved[p : p + 1]
    own = arrived.shape[1]
    width = out.shape[0]
    near = rows // 2
    for i in range(rows):
        for j in range(cols):
            at = i * HALF + j * own
            mixed[at : at + own, :] = arrived[i * cols + j]
    starts = north_starts(rows)
    for n, start in enumerate(starts):
        if n == 0:
            both = mul_table(mixed[0:HALF], packed[0], packed[1], TN)
        elif n == 1:
            both = mul_table(mixed[HALF : 2 * HALF], plain[0, :HALF], plain[1, :HALF], TN)
        else:
            at = 2 * start * HALF
            both = mul_table(mixed[at : at + 2 * HALF], plain[0], plain[1], TN)
        top, bottom = both[:width], both[width:]
        waves[n, :, :LANES] = top[:, :LANES] - bottom[:, LANES:]
        waves[n, :, LANES:] = top[:, LANES:] + bottom[:, :LANES]
    for at in range(0, width, SUB):
        parts = [[None, None] for _ in range(near)]
        for n, start in enumerate(starts):
            re = waves[n, at : at + SUB, :LANES]
            im = waves[n, at : at + SUB, LANES:]
            for i in range(near):
                if start == 0:
                    term = re
                else:
                    term = re * turns[0, n, i : i + 1] + im * turns[1, n, i : i + 1]
                sums = parts[i]
                sums[start % 2] = term if sums[start % 2] is None else sums[start % 2] + term
        for i in range(near):
            even, odd = parts[i]
            out[at : at + SUB, i * LANES : (i + 1) * LANES] = even + odd
            out[at : at + SUB, (near + i) * LANES : (near + i + 1) * LANES] = even - odd


def shape(*dims):
    return jax.ShapeDtypeStruct(dims, F32)


def scratch(*dims):
    return pltpu.VMEM(dims, F32)


def call(kernel, outs, ins, work=(), limit=SMALL):
    return pl.pallas_call(
        kernel,
        out_shape=outs,
        in_specs=[spec for spec, _ in ins],
        out_specs=jax.tree.map(lambda _: VMEM, outs),
        scratch_shapes=list(work),
        compiler_params=pltpu.CompilerParams(vmem_limit_bytes=limit),
    )(*[value for _, value in ins])


def exchange(pieces):
    return lax.all_to_all(pieces, BOTH, 0, 0, tiled=True)


def on_device(
    kernel_tiles, footprints, counts, readings, damping, layer_depth, inclinations, declinations,
    resid_grid,
):
    rows, cols = lax.axis_size("row"), lax.axis_size("col")
    devices = rows * cols
    slots, sources = kernel_tiles.shape[3:]
    parts = sources // LANES
    tile_east = resid_grid.shape[0]
    east = cols * tile_east
    bands = east // LANES
    own = HALF // cols
    width = east // devices
    sizes = (rows, cols, own, bands)

    turns = north_turns(rows)
    forward_tables, inverse_tables = north_forward_tables(), north_inverse_tables()
    tables, east_turns = east_tables(east)
    hats = north_hat_table(rows, cols)

    joined = 2 * width == LANES
    everywhere = shape(devices, parts, LANES)
    beside = shape(devices, 1 + own // 4, 4, LANES) if joined else everywhere
    pieces = shape(devices, own, 2 * width)

    def apart(value):
        return HBM, pltpu.with_memory_space_constraint(value, pltpu.HBM)

    tile_scratch = scratch(FOOTPRINT, slots, sources)
    tile_sems = pltpu.SemaphoreType.DMA((FOOTPRINT,))
    codes_scratch = pltpu.SMEM((1, FOOTPRINT), jnp.int32)

    sums, side, meta = call(
        functools.partial(start_kernel, sizes),
        (
            shape(rows, FOOTPRINT + width // 4, parts, LANES),
            shape(side_rows(own, bands, rows)[-1], LANES),
            shape(2 + FOOTPRINT, LANES),
        ),
        [apart(footprints), (VMEM, counts), (VMEM, damping.reshape(1, 1))]
        + [
            apart(value)
            for value in (
                readings, layer_depth, inclinations, declinations,
                jnp.asarray(east_turns), jnp.asarray(hats), resid_grid, kernel_tiles,
            )
        ],
        [
            codes_scratch,
            pltpu.SMEM((LAYERS,), F32),
            pltpu.SMEM((2, 2), F32),
            scratch(1, slots),
            scratch(*resid_grid.shape),
            tile_scratch,
            scratch(slots, LANES),
            tile_sems,
            pltpu.SemaphoreType.DMA((8,)),
        ],
    )
    arrived = lax.all_to_all(sums, "row", 0, 0, tiled=True)
    summed = call(
        functools.partial(column_kernel, rows, cols),
        shape(cols, FOOTPRINT, parts, LANES),
        [(VMEM, arrived)],
    )
    summed = lax.all_to_all(summed, "col", 0, 0, tiled=True)

    sums, right_own, *spectrum = call(
        functools.partial(normal_kernel, rows, cols),
        (beside, shape(parts, LANES)) if joined else (everywhere, shape(parts, LANES), pieces),
        [
            (VMEM, meta),
            (VMEM, kernel_tiles),
            (VMEM, summed),
            (VMEM, arrived),
            (VMEM, turns),
            (VMEM, forward_tables[0]),
            (VMEM, forward_tables[1]),
        ],
        [scratch(FOOTPRINT, parts, LANES)]
        + [scratch(slots, LANES), scratch(slots, LANES)]
        + [scratch(rows, width, LANES)],
    )
    sums = exchange(sums)
    shared = call(
        share_kernel, shape(devices, 2, parts, LANES), [(VMEM, sums), (VMEM, right_own)]
    )
    shared = exchange(shared)
    if joined:
        spectrum, sorted_work = sums, [scratch(cols, 2 * own, tile_east)]
    else:
        spectrum, sorted_work = exchange(spectrum[0]), []
        spectrum = spectrum.reshape(rows, cols, own, 2, width).transpose(1, 3, 2, 0, 4)
        spectrum = spectrum.reshape(cols, 2 * own, tile_east)

    second, measured, carry = call(
        functools.partial(direction_kernel, rows, cols),
        (everywhere, everywhere, shape(5, parts, LANES)),
        [(VMEM, meta), (VMEM, kernel_tiles), (VMEM, shared)],
        [scratch(slots, LANES)],
    )
    work = [
        scratch(LAYERS, 2 * rows, cols * LANES),
        scratch(LAYERS * 2 * own, east),
        scratch((own + 1) * bands, 2 * LANES),
        scratch(own * bands, 2 * LANES),
        scratch(own * bands, 2 * LANES),
    ]
    known, response = call(
        functools.partial(map_kernel, sizes, width),
        (pieces, pieces),
        [
            (VMEM, spectrum),
            (VMEM, shared),
            (VMEM, second),
            (VMEM, carry),
            (VMEM, tables),
            (VMEM, side),
        ],
        work + sorted_work,
    )
    measured = exchange(measured)
    outgoing = call(
        combine_kernel,
        pieces,
        [(VMEM, measured), (VMEM, carry), (VMEM, known), (VMEM, response)],
    )
    coefficients, rtp_map = call(
        functools.partial(finish_kernel, rows, cols),
        (shape(1, sources), shape(width, rows * LANES)),
        [
            (VMEM, exchange(outgoing)),
            (VMEM, measured),
            (VMEM, carry),
            (VMEM, turns),
            (VMEM, inverse_tables[0]),
            (VMEM, inverse_tables[1]),
        ],
        [scratch(rows * HALF, 2 * width), scratch(rows // 2 + 1, width, 2 * LANES)],
    )
    return coefficients.reshape(1, 1, sources), rtp_map


def solution(mesh):
    in_specs = (
        P("row", "col", None, None, None),
        P("row", "col", None),
        P("row", "col"),
        P("row", "col", None),
        P(),
        P(),
        P(),
        P(),
        P("col", "row"),
    )
    out_specs = (P("row", "col", None), P(("row", "col"), None))
    return jax.shard_map(
        on_device, mesh=mesh, in_specs=in_specs, out_specs=out_specs, check_vma=False
    )
```

```python
import functools

import jax
import jax.numpy as jnp
import ml_dtypes
import numpy as np
from jax import lax
from jax.experimental import pallas as pl
from jax.experimental.pallas import tpu as pltpu
from jax.sharding import PartitionSpec as P

SRC_ROWS = 8
SRC_COLS = 32
LAYERS = 2
REFINE = 16
FOOTPRINT = 9
LANES = 128
SUB = 8
HALF = 64
BOTH = ("row", "col")
COUNT, ROW, COL = 9, 10, 11
SENT = 6
MIB = 1024 * 1024
SMALL, LARGE = 24 * MIB, 62 * MIB
F32 = jnp.float32
BF16 = jnp.bfloat16

VMEM = pl.BlockSpec(memory_space=pltpu.VMEM)
SMEM = pl.BlockSpec(memory_space=pltpu.SMEM)
HBM = pl.BlockSpec(memory_space=pltpu.HBM)
NN = (((1,), (0,)), ((), ()))
NT = (((1,), (1,)), ((), ()))
TN = (((0,), (0,)), ((), ()))


def split_table(table):
    high = table.astype(ml_dtypes.bfloat16)
    low = (table - high.astype(np.float64)).astype(ml_dtypes.bfloat16)
    return np.stack([high, low])


def group_start(group, rows):
    if group == 0:
        return 0
    if group == 1:
        return rows // 2
    return group // 2 + HALF * rows * (group % 2)


def unit_turn(product, period):
    angle = 2.0 * np.pi * (product % period) / period
    return np.cos(angle), np.sin(angle)


def north_starts(rows):
    return [0, rows // 2] + list(range(1, rows // 2))


def north_turns(rows):
    north = rows * LANES
    starts = np.array(north_starts(rows))
    cos, sin = unit_turn(starts[:, None] * np.arange(north // 2)[None, :], north)
    turns = np.stack([cos, -sin]).reshape(2, len(starts), rows // 2, LANES)
    return turns.astype(np.float32)


def north_forward_tables():
    cos, sin = unit_turn(np.outer(np.arange(LANES), np.arange(LANES)), LANES)
    plain = np.block([[cos, sin], [-sin, cos]])
    packed = np.concatenate([cos[:HALF], -sin[:HALF]], 0)
    packed[HALF] = 1.0 - 2.0 * (np.arange(LANES) % 2)
    return split_table(packed), split_table(plain)


def north_inverse_tables():
    cos, sin = unit_turn(np.outer(np.arange(LANES), np.arange(LANES)), LANES)
    plain = 2.0 * np.concatenate([cos, sin], 1)
    packed = plain[:HALF].copy()
    packed[0, :LANES] = 1.0
    packed[0, LANES:] = 2.0 * (np.arange(LANES) % 2) - 1.0
    return split_table(packed), split_table(plain)


def east_tables(east):
    bands = east // LANES
    cos, sin = unit_turn(np.outer(np.arange(LANES), np.arange(LANES)), LANES)
    forward = np.block([[cos, -sin], [sin, cos]])
    inverse = np.block([[cos, sin], [-sin, cos]])
    turn_cos, turn_sin = unit_turn(np.outer(np.arange(bands), np.arange(LANES)), east)
    turns = np.concatenate([turn_cos, -turn_sin]).astype(np.float32)
    up_east = hat_table(east, east // REFINE).reshape(-1, 2 * LANES, east // REFINE)
    up_east = up_east.transpose(0, 2, 1).reshape(-1, 2 * LANES).astype(ml_dtypes.bfloat16)
    tables = [split_table(forward), split_table(inverse)]
    return np.concatenate([t.reshape(-1, 2 * LANES) for t in tables] + [up_east]), turns


def hat_table(fine_count, coarse_count):
    offset = (np.arange(fine_count)[:, None] + 0.5) / REFINE - 0.5 - np.arange(coarse_count)[None, :]
    return np.maximum(0.0, 1.0 - np.abs(offset))


def north_hat_table(rows, cols):
    north = rows * LANES
    coarse = rows * SRC_ROWS
    own = HALF // cols
    spectrum = np.fft.fft(hat_table(north, coarse), axis=0)
    out = np.zeros((rows, cols, 2 * own, coarse))
    for group in range(rows):
        for col in range(cols):
            index = group_start(group, rows) + rows * (col * own + np.arange(own))
            part = spectrum[index % north]
            out[group, col, :own] = part.real
            out[group, col, own:] = part.imag
    out[0, 0, own] = spectrum[north // 2].real
    out = out.reshape(rows * cols, 2 * own, 2 * rows, 4).transpose(0, 2, 3, 1)
    out = out.reshape(rows * cols, 2 * rows, 8 * own)
    return np.pad(out, ((0, 0), (0, 0), (0, LANES - 8 * own))).astype(np.float32)


def split(x):
    high = x.astype(BF16)
    return high, (x - high.astype(F32)).astype(BF16)


def dot(a, b, dims):
    return lax.dot_general(a, b, dims, preferred_element_type=F32)


def mul_table(x, high, low, dims=NN):
    x_high, x_low = split(x)
    return dot(x_high, high, dims) + (dot(x_low, high, dims) + dot(x_high, low, dims))


def table_mul(high, low, x, dims=NN):
    x_high, x_low = split(x)
    return dot(high, x_high, dims) + (dot(high, x_low, dims) + dot(low, x_high, dims))


def transform_list(values, sign):
    count = len(values)
    if count == 1:
        return values
    even = transform_list(values[0::2], sign)
    odd = transform_list(values[1::2], sign)
    first, second = [], []
    for k in range(count // 2):
        re, im = odd[k]
        if k == 0:
            turned = (re, im)
        elif 4 * k == count:
            turned = (im, -re) if sign < 0 else (-im, re)
        else:
            cos = float(np.cos(2.0 * np.pi * k / count))
            sin = sign * float(np.sin(2.0 * np.pi * k / count))
            if 8 * k == count or 8 * k == 3 * count:
                if cos * sin > 0:
                    turned = (cos * (re - im), cos * (re + im))
                else:
                    turned = (cos * (re + im), cos * (im - re))
            else:
                turned = (re * cos - im * sin, re * sin + im * cos)
        first.append((even[k][0] + turned[0], even[k][1] + turned[1]))
        second.append((even[k][0] - turned[0], even[k][1] - turned[1]))
    return first + second


def total(x):
    lanes = jnp.sum(jnp.sum(x, axis=0), axis=0, keepdims=True)
    return jnp.sum(lanes, axis=1, keepdims=True)


def neighbour(k, ints, rows, cols):
    code = ints[k]
    near_row = ints[ROW] + code // 3 - 1
    near_col = ints[COL] + code % 3 - 1
    inside = (near_row >= 0) & (near_row < rows) & (near_col >= 0) & (near_col < cols)
    device = jnp.clip(near_row * cols + near_col, 0, rows * cols - 1)
    return device, inside


def near_blocks(ints, vector, rows, cols):
    blocks = []
    for k in range(FOOTPRINT):
        device, inside = neighbour(k, ints, rows, cols)
        blocks.append(vector[device] * jnp.where(inside, 1.0, 0.0))
    return blocks


def apply_forward(tiles, copies, blocks, count, out, work):
    slots, width = tiles.shape[1:]
    parts = width // LANES
    squares = jnp.zeros((SUB, LANES), F32)
    for group, end in ((0, 4), (4, 8), (8, FOOTPRINT)):
        for k in range(group, end if copies else group):
            copies[k].wait()
        spread = [
            [jnp.broadcast_to(blocks[k][p : p + 1], (SUB, LANES)) for p in range(parts)]
            for k in range(group, end)
        ]

        def step(t, squares, group=group, spread=spread):
            at = pl.multiple_of(t * SUB, SUB)
            sums = [None] * parts
            for k in range(len(spread)):
                for p in range(parts):
                    tile = tiles[group + k, pl.ds(at, SUB), p * LANES : (p + 1) * LANES]
                    term = tile * spread[k][p]
                    sums[p] = term if sums[p] is None else sums[p] + term
            acc = functools.reduce(jnp.add, sums)
            if group > 0:
                acc = acc + work[pl.ds(at, SUB), :]
            if group + len(spread) < FOOTPRINT:
                work[pl.ds(at, SUB), :] = acc
                return squares
            slot = at + lax.broadcasted_iota(jnp.int32, (SUB, LANES), 0)
            value = jnp.where(slot.astype(F32) < count, jnp.sum(acc, axis=1, keepdims=True), 0.0)
            if out is not None:
                out[pl.ds(at, SUB), :] = value
            return squares + value * value

        squares = lax.fori_loop(0, slots // SUB, step, squares, unroll=8)
    return jnp.sum(squares, axis=0, keepdims=True)


def apply_adjoint(tile, values):
    slots, width = tile.shape
    parts = width // LANES
    sums = [[None, None] for _ in range(parts)]
    for t in range(slots // SUB):
        rows = slice(t * SUB, (t + 1) * SUB)
        weight = values[rows, :]
        for p in range(parts):
            term = tile[rows, p * LANES : (p + 1) * LANES] * weight
            sums[p][t % 2] = term if t < 2 else sums[p][t % 2] + term
    return jnp.concatenate([jnp.sum(a + b, axis=0, keepdims=True) for a, b in sums], axis=0)


def send_adjoint(tile, values, k, ints, out, rows, cols):
    device, inside = neighbour(k, ints, rows, cols)
    block = jnp.where(inside, apply_adjoint(tile, values), 0.0)
    if len(out.shape) == 4:
        out[device, 0] = out[device, 0] + block
    else:
        out[device] = out[device] + block


def tile_copies(source, tiles, sems):
    copies = [
        pltpu.make_async_copy(source.at[0, 0, k], tiles.at[k], sems.at[k]) for k in range(FOOTPRINT)
    ]
    for copy in copies:
        copy.start()
    return copies


def start_kernel(
    sizes, codes, counts, damping, readings, depth, inclinations, declinations, turns, hats, resid,
    source, out, kept, side, meta, codes_in, depth_in, angles, read, map_rows, tiles, values, sems, more,
):
    rows, cols, own, bands = sizes
    row, col = lax.axis_index("row"), lax.axis_index("col")
    _, turns_at, hats_at, end = side_rows(own, bands, rows)
    pairs = [
        (codes.at[0], codes_in),
        (depth, depth_in),
        (inclinations, angles.at[0]),
        (declinations, angles.at[1]),
        (readings.at[0], read),
        (turns, side.at[turns_at:hats_at]),
        (hats.at[row * cols + col], side.at[hats_at:end]),
        (resid, map_rows),
    ]
    first = [pltpu.make_async_copy(a, b, more.at[n]) for n, (a, b) in enumerate(pairs)]
    for copy in first:
        copy.start()
    copies = tile_copies(source, tiles, sems)
    for copy in first:
        copy.wait()
    width = map_rows.shape[0] // rows
    for i in range(rows):
        for g in range(width // 4):
            at = i * width + 4 * g
            out[i, SENT + g] = map_rows[at : at + 4]
    ints = [codes_in[0, k] for k in range(FOOTPRINT)] + [None, row, col]
    meta[0:1, :] = jnp.broadcast_to(counts[...].astype(F32), (1, LANES))
    for k in range(FOOTPRINT):
        meta[2 + k : 3 + k, :] = jnp.full((1, LANES), codes_in[0, k].astype(F32), F32)
    meta[1:2, :] = jnp.broadcast_to(damping[...], (1, LANES))
    slots = read.shape[1]
    slot = lax.broadcasted_iota(jnp.int32, (1, slots), 1)
    live = jnp.where(slot < counts[...], read[...], 0.0)
    for t in range(slots // LANES):
        square = jnp.broadcast_to(live[:, t * LANES : (t + 1) * LANES], (LANES, LANES))
        values[t * LANES : (t + 1) * LANES, :] = square.T
    trig = []
    for m in range(2):
        up = jnp.full((1, LANES), angles[0, m], F32)
        turn = jnp.full((1, LANES), angles[1, m], F32)
        flat = jnp.cos(up)
        trig += [jnp.sin(up), flat * jnp.cos(turn), flat * jnp.sin(turn)]
    put_weights(sizes, row, col, [depth_in[l] for l in range(LAYERS)], trig, side)
    for k in range(FOOTPRINT):
        copies[k].wait()
        kept[ints[k]] = apply_adjoint(tiles.at[k], values)
    fill_pieces(out, kept, row)


def fill_pieces(out, kept, here):
    for peer in range(out.shape[0]):
        low = jnp.maximum(peer - here - 1, -1)
        for slot in range(2):
            at = 3 * (jnp.clip(low + slot, -1, 1) + 1)
            out[peer, 3 * slot : 3 * slot + 3] = kept[pl.ds(at, 3)]


def arrived_part(arrived, kept, here, offset, which, other):
    if offset == 0:
        return kept[3 * (which + 1) + other]
    peer, count = here - offset, arrived.shape[0]
    slot = which - max(offset - 1, -1)
    part = arrived[jnp.clip(peer, 0, count - 1), 3 * slot + other]
    return jnp.where((peer >= 0) & (peer < count), part, 0.0)


def place_rows(out, get):
    for d in range(out.shape[0]):
        for g in range(out.shape[1] - 1):
            out[d, 1 + g] = get(d, g)


def column_kernel(rows, cols, arrived, kept, out, sums):
    row, col = lax.axis_index("row"), lax.axis_index("col")
    for north in (-1, 0, 1):
        for east in (-1, 0, 1):
            parts = [
                arrived_part(arrived, kept, row, a - north, a, east + 1) for a in (-1, 0, 1)
            ]
            target, column = row + north, col + east
            inside = (target >= 0) & (target < rows) & (column >= 0) & (column < cols)
            sums[3 * (east + 1) + north + 1] = jnp.where(inside, parts[0] + parts[1] + parts[2], 0.0)
    fill_pieces(out, sums, col)


def share_kernel(arrived, own, everywhere):
    block = jnp.sum(arrived[:, 0] if len(arrived.shape) == 4 else arrived[...], axis=0)
    both = jnp.stack([own[...], block])
    everywhere[...] = jnp.broadcast_to(both[None], everywhere.shape)


def normal_kernel(
    rows, cols, meta, source, summed, sums, arrived, turns, packed, plain, out, own, *refs
):
    (*apart, near, values, work, planes) = refs
    tiles, copies = source.at[0, 0], None
    row, col = lax.axis_index("row"), lax.axis_index("col")
    ints = [meta[2 + k, 0].astype(jnp.int32) for k in range(FOOTPRINT)] + [None, row, col]
    for code in range(FOOTPRINT):
        north, east = code // 3 - 1, code % 3 - 1
        parts = [arrived_part(summed, sums, col, b - east, b, north + 1) for b in (-1, 0, 1)]
        near[code] = parts[0] + parts[1] + parts[2]
    blocks = [near[ints[k]] for k in range(FOOTPRINT)]
    me = row * cols + col
    out[...] = jnp.zeros(out.shape, F32)
    own[...] = near[FOOTPRINT // 2]
    ridge = meta[1:2, :] * own[...]
    if apart:
        out[me] = ridge
    else:
        out[me, 0] = ridge

    def store(device, piece):
        if apart:
            apart[0][device] = piece
        else:
            for g in range(out.shape[1] - 1):
                out[device, 1 + g] = piece[4 * g : 4 * g + 4]

    north_transform(rows, cols, arrived, turns, (packed, plain), planes, store)
    apply_forward(tiles, copies, blocks, meta[0:1, :], values, work)
    for k in range(FOOTPRINT):
        send_adjoint(tiles.at[k], values, k, ints, out, rows, cols)


def north_transform(rows, cols, arrived, turns, tables, planes, store):
    own = HALF // cols
    near, count = rows // 2, planes.shape[1]
    for i in range(rows):
        for g in range(count // 4):
            planes[i, 4 * g : 4 * g + 4, :] = arrived[i, SENT + g]
    for i in range(near):
        one, other = planes[i], planes[i + near]
        planes[i] = one + other
        planes[i + near] = one - other
    packed, plain = tables
    for n, start in enumerate(north_starts(rows)):
        base = near * (start % 2)
        re, im = None, None
        for i in range(near):
            plane = planes[base + i]
            a = plane if start == 0 else plane * turns[0, n, i : i + 1]
            re = a if re is None else re + a
            if start:
                a = plane * turns[1, n, i : i + 1]
                im = a if im is None else im + a
        if start == 0:
            result = table_mul(packed[0], packed[1], re, NT)
        else:
            result = table_mul(plain[0], plain[1], jnp.concatenate([re, im], axis=1), NT)
        imag_at = result.shape[0] // 2
        groups = [n] if n < 2 else [2 * start, 2 * start + 1]
        for h, group in enumerate(groups):
            for j in range(cols):
                at = h * HALF + j * own
                real, imag = result[at : at + own], result[imag_at + at : imag_at + at + own]
                store(group * cols + j, jnp.concatenate([real, imag], axis=1))


def pole(north, east, trig):
    square = north * north + east * east
    inverse = jnp.where(square > 0.0, lax.rsqrt(jnp.where(square > 0.0, square, 1.0)), 0.0)
    a0 = (trig[1] * north + trig[2] * east) * inverse
    a1 = (trig[4] * north + trig[5] * east) * inverse
    v0, v1 = trig[0], trig[3]
    scale = 1.0 / ((v0 * v0 + a0 * a0) * (v1 * v1 + a1 * a1))
    return (v0 * v1 - a0 * a1) * scale, -(v0 * a1 + v1 * a0) * scale, square * inverse


def side_rows(own, bands, rows):
    span = (own + 1) * bands
    turns = 2 * (1 + LAYERS) * span
    return span, turns, turns + 2 * bands, turns + 2 * bands + 2 * rows


def put_weights(sizes, row, col, depth, trig, side):
    rows, _, own, bands = sizes
    span = side_rows(own, bands, rows)[0]

    def put(part, q, at, value):
        base = (part * (1 + LAYERS) + q) * span + at
        side[base : base + value.shape[0], :] = value

    north_len, east_len = rows * LANES, bands * LANES
    scale = 1.0 / (north_len * east_len)
    start = jnp.where(
        row == 0, 0, jnp.where(row == 1, rows // 2, row // 2 + HALF * rows * (row % 2))
    )

    def signed(index, length):
        return jnp.where(index < length // 2, index, index - length).astype(F32) / length

    def north_of(shape):
        index = start + rows * (col * own + lax.broadcasted_iota(jnp.int32, shape, 0))
        return signed(index, north_len)

    def weights(re, im, radius):
        damp = [None] + [jnp.exp(radius * (-2.0 * np.pi * depth[l])) for l in range(LAYERS)]
        return [(re, im) if d is None else (re * d, im * d) for d in damp]

    lane = lax.broadcasted_iota(jnp.int32, (own, LANES), 1)
    north = north_of((own, LANES))
    for band in range(bands):
        east = signed(band + bands * lane, east_len)
        re, im, radius = pole(north, east, trig)
        if band == 0:
            re2, im2, _ = pole(north, jnp.where(lane == HALF, 0.5, east), trig)
            re, im = 0.5 * (re + re2), 0.5 * (im + im2)
        for q, (wr, wi) in enumerate(weights(re * scale, im * scale, radius)):
            put(0, q, band * own, wr)
            put(1, q, band * own, wi)
            put(0, q, bands * own, jnp.zeros((bands, LANES), F32))
            put(1, q, bands * own, jnp.zeros((bands, LANES), F32))

    @pl.when((row == 0) & (col == 0))
    def _():
        band = lax.broadcasted_iota(jnp.int32, (bands, LANES), 0)
        lanes = lax.broadcasted_iota(jnp.int32, (bands, LANES), 1)
        east = signed(band + bands * lanes, east_len)
        flipped = jnp.where((band == 0) & (lanes == HALF), 0.5, east)
        pairs = []
        for one, other in ((0.0, 0.0), (-0.5, 0.5)):
            re, im, radius = pole(jnp.full_like(east, one), east, trig)
            re2, im2, _ = pole(jnp.full_like(east, other), flipped, trig)
            half = 0.5 * scale
            pairs.append(weights(half * (re + re2), half * (im + im2), radius))
        for q in range(1 + LAYERS):
            (r0, i0), (r1, i1) = pairs[0][q], pairs[1][q]
            put(0, q, bands * own, 0.5 * (r0 - r1))
            put(1, q, bands * own, 0.5 * (i0 - i1))
            for b in range(bands):
                put(0, q, b * own, 0.5 * (r0 + r1)[b : b + 1])
                put(1, q, b * own, 0.5 * (i0 + i1)[b : b + 1])


def turn_rows(side, turns_at, band, bands):
    cos, sin = turns_at + band, turns_at + bands + band
    return side[cos : cos + 1, :], side[sin : sin + 1, :]


def east_table(tables, index):
    span = 2 * LANES
    return tables[2 * index * span : (2 * index + 1) * span], tables[
        (2 * index + 1) * span : (2 * index + 2) * span
    ]


def east_forward(get, sizes, side, tables, work):
    rows, _, own, bands = sizes
    turns_at = side_rows(own, bands, rows)[1]
    for g in range(own // SUB):
        values = transform_list([get(m, g) for m in range(bands)], -1.0)
        for b in range(bands):
            cos, sin = turn_rows(side, turns_at, b, bands)
            re, im = values[b]
            at = b * own + g * SUB
            work[at : at + SUB, :LANES] = re * cos - im * sin
            work[at : at + SUB, LANES:] = re * sin + im * cos
            if g == 0:
                re, im = values[(bands - b) % bands]
                re, im = re[0:1], -im[0:1]
                at = bands * own + b
                work[at : at + 1, :LANES] = re * cos - im * sin
                work[at : at + 1, LANES:] = re * sin + im * cos
    return mul_table(work[...], *east_table(tables, 0))


def weigh(spectrum, q, sizes, side, into, first):
    rows, _, own, bands = sizes
    span = side_rows(own, bands, rows)[0]
    re, im = spectrum[:, :LANES], spectrum[:, LANES:]
    wr = side[q * span : (q + 1) * span, :]
    wi = side[(1 + LAYERS + q) * span : (2 + LAYERS + q) * span, :]
    out_re, out_im = re * wr - im * wi, re * wi + im * wr
    main = own * bands
    if first:
        into[:, :LANES] = out_re[:main]
        into[:, LANES:] = out_im[:main]
    else:
        into[:, :LANES] += out_re[:main]
        into[:, LANES:] += out_im[:main]
    for b in range(bands):
        into[b * own : b * own + 1, :LANES] += out_re[main + b : main + b + 1]
        into[b * own : b * own + 1, LANES:] += out_im[main + b : main + b + 1]


def east_inverse(spectrum, sizes, side, tables, work, store):
    rows, _, own, bands = sizes
    turns_at = side_rows(own, bands, rows)[1]
    work[...] = mul_table(spectrum[...], *east_table(tables, 1))
    for g in range(own // SUB):
        values = []
        for b in range(bands):
            at = b * own + g * SUB
            re, im = work[at : at + SUB, :LANES], work[at : at + SUB, LANES:]
            cos, sin = turn_rows(side, turns_at, b, bands)
            values.append((re * cos + im * sin, im * cos - re * sin))
        values = transform_list(values, 1.0)
        for b in range(bands):
            store(b, g, *values[b])


def store_pieces(out, width):
    per_band = LANES // width

    def store(band, g, re, im):
        for s in range(per_band):
            cut = slice(s * width, (s + 1) * width)
            piece = jnp.concatenate([re[:, cut], im[:, cut]], axis=1)
            out[band * per_band + s, g * SUB : (g + 1) * SUB] = piece

    return store


def model_rows(vector, sizes, side, coarse):
    rows, cols, own, bands = sizes
    own2 = 2 * own
    for i in range(rows):
        for j in range(cols):
            block = vector[i * cols + j]
            for layer in range(LAYERS):
                coarse[layer, 2 * i : 2 * i + 2, j * LANES : (j + 1) * LANES] = block[
                    2 * layer : 2 * layer + 2
                ]
    out = []
    _, _, hats_at, end = side_rows(own, bands, rows)
    high, low = split(side[hats_at:end, :])
    tiles = cols * SRC_COLS // LANES
    lane = lax.broadcasted_iota(jnp.int32, (own2, LANES), 1) // SRC_COLS
    for layer in range(LAYERS):
        mixed = table_mul(high, low, coarse[layer], TN)
        whole = []
        for tile in range(tiles):
            joined = None
            for place in range(LANES // SRC_COLS):
                j = tile * (LANES // SRC_COLS) + place
                summed = None
                for part in range(4):
                    piece = mixed[part * own2 : (part + 1) * own2, j * LANES : (j + 1) * LANES]
                    shift = ((place - part) * SRC_COLS) % LANES
                    if shift:
                        piece = pltpu.roll(piece, shift, 1)
                    summed = piece if summed is None else summed + piece
                joined = summed if joined is None else jnp.where(lane == place, summed, joined)
            whole.append(joined)
        out.append(whole[0] if tiles == 1 else jnp.concatenate(whole, axis=1))
    return out


def model_mix(vector, scale, sizes, side, tables, coarse, fine, work, mixed, first):
    rows, cols, own, bands = sizes
    depth = cols * SRC_COLS
    planes = jnp.concatenate(model_rows(vector, sizes, side, coarse), axis=0)
    high, low = split(planes if scale is None else planes * scale)
    for c in range(bands // 2):
        at = 8 * LANES + c * depth
        table = tables[at : at + depth, :]
        fine[:, 2 * LANES * c : 2 * LANES * (c + 1)] = dot(high, table, NN) + dot(low, table, NN)
    for layer in range(LAYERS):

        def get(m, g, base=2 * own * layer):
            at = base + g * SUB
            cut = slice(m * LANES, (m + 1) * LANES)
            return fine[at : at + SUB, cut], fine[at + own : at + own + SUB, cut]

        spectrum = east_forward(get, sizes, side, tables, work)
        weigh(spectrum, 1 + layer, sizes, side, mixed, first and layer == 0)


def sort_east(arrived, sizes, spec):
    rows, cols, own, bands = sizes
    left = lax.broadcasted_iota(jnp.int32, (SUB, LANES), 1) < HALF
    for j in range(cols):
        for i in range(0, rows, 2):
            for g in range(own // SUB):
                pair = []
                for source in (i * cols + j, (i + 1) * cols + j):
                    at = 1 + 2 * g
                    both = [arrived[source, at], arrived[source, at + 1]]
                    pair.append(jnp.concatenate(both, axis=0))
                cut = slice(i * HALF, (i + 2) * HALF)
                at = g * SUB
                spec[j, at : at + SUB, cut] = jnp.where(left, pair[0], pltpu.roll(pair[1], HALF, 1))
                at = own + g * SUB
                spec[j, at : at + SUB, cut] = jnp.where(left, pltpu.roll(pair[0], HALF, 1), pair[1])


def map_kernel(
    sizes, width, arrived, shared, second, carry, tables, side, known, response,
    coarse, fine, work, mixed, back, *spec,
):
    rows, cols, own, bands = sizes
    if spec:
        sort_east(arrived, sizes, spec[0])
    spec = spec[0] if spec else arrived
    per = spec.shape[2] // LANES

    def get(m, g):
        cut = slice((m % per) * LANES, (m % per + 1) * LANES)
        at = g * SUB
        return spec[m // per, at : at + SUB, cut], spec[m // per, own + at : own + at + SUB, cut]

    spectrum = east_forward(get, sizes, side, tables, work)
    weigh(spectrum, 0, sizes, side, mixed, True)
    model_mix(shared.at[:, 0], carry[4, 0:1, 0:1], sizes, side, tables, coarse, fine, work, mixed, False)
    east_inverse(mixed, sizes, side, tables, back, store_pieces(known, width))
    model_mix(second, None, sizes, side, tables, coarse, fine, work, mixed, True)
    east_inverse(mixed, sizes, side, tables, back, store_pieces(response, width))


def direction_kernel(
    rows, cols, meta, source, shared, second, measured, carry,
    work,
):
    tiles, copies = source.at[0, 0], None
    row, col = lax.axis_index("row"), lax.axis_index("col")
    first, applied = shared.at[:, 0], shared.at[:, 1]
    norm = total(first[...] * first[...])
    step = norm / total(first[...] * applied[...])
    residual = first[...] - step[None] * applied[...]
    norm_next = total(residual * residual)
    second[...] = residual + (norm_next / norm)[None] * first[...]
    ridge = meta[1:2, 0:1] * total(second[...] * second[...])
    me = row * cols + col
    carry[0] = step * first[me]
    carry[1] = second[me]
    for at, value in ((2, norm_next), (3, ridge), (4, step)):
        carry[at] = jnp.broadcast_to(value, carry.shape[1:])
    ints = [meta[2 + k, 0].astype(jnp.int32) for k in range(FOOTPRINT)] + [None, row, col]
    blocks = near_blocks(ints, second, rows, cols)
    squares = apply_forward(tiles, copies, blocks, meta[0:1, :], None, work)
    measured[...] = jnp.broadcast_to(squares[None], measured.shape)


def last_step(measured, carry):
    squares = jnp.sum(measured[:, 0:1], axis=0)
    return carry[2, 0:1, 0:1] / (squares[:, 0:1] + carry[3, 0:1, 0:1])


def combine_kernel(measured, carry, known, response, out):
    out[...] = known[...] + last_step(measured, carry)[None] * response[...]


def finish_kernel(
    rows, cols, arrived, measured, carry, turns, packed, plain, coefficients, out, mixed, waves
):
    solved = carry[0] + last_step(measured, carry) * carry[1]
    for p in range(solved.shape[0]):
        coefficients[:, p * LANES : (p + 1) * LANES] = solved[p : p + 1]
    own = arrived.shape[1]
    width = out.shape[0]
    near = rows // 2
    for i in range(rows):
        for j in range(cols):
            at = i * HALF + j * own
            mixed[at : at + own, :] = arrived[i * cols + j]
    starts = north_starts(rows)
    for n, start in enumerate(starts):
        if n == 0:
            both = mul_table(mixed[0:HALF], packed[0], packed[1], TN)
        elif n == 1:
            both = mul_table(mixed[HALF : 2 * HALF], plain[0, :HALF], plain[1, :HALF], TN)
        else:
            at = 2 * start * HALF
            both = mul_table(mixed[at : at + 2 * HALF], plain[0], plain[1], TN)
        top, bottom = both[:width], both[width:]
        waves[n, :, :LANES] = top[:, :LANES] - bottom[:, LANES:]
        waves[n, :, LANES:] = top[:, LANES:] + bottom[:, :LANES]
    for at in range(0, width, SUB):
        parts = [[None, None] for _ in range(near)]
        for n, start in enumerate(starts):
            re = waves[n, at : at + SUB, :LANES]
            im = waves[n, at : at + SUB, LANES:]
            for i in range(near):
                if start == 0:
                    term = re
                else:
                    term = re * turns[0, n, i : i + 1] + im * turns[1, n, i : i + 1]
                sums = parts[i]
                sums[start % 2] = term if sums[start % 2] is None else sums[start % 2] + term
        for i in range(near):
            even, odd = parts[i]
            out[at : at + SUB, i * LANES : (i + 1) * LANES] = even + odd
            out[at : at + SUB, (near + i) * LANES : (near + i + 1) * LANES] = even - odd


def shape(*dims):
    return jax.ShapeDtypeStruct(dims, F32)


def scratch(*dims):
    return pltpu.VMEM(dims, F32)


def call(kernel, outs, ins, work=(), limit=SMALL):
    return pl.pallas_call(
        kernel,
        out_shape=outs,
        in_specs=[spec for spec, _ in ins],
        out_specs=jax.tree.map(lambda _: VMEM, outs),
        scratch_shapes=list(work),
        compiler_params=pltpu.CompilerParams(vmem_limit_bytes=limit),
    )(*[value for _, value in ins])


def exchange(pieces):
    return lax.all_to_all(pieces, BOTH, 0, 0, tiled=True)


def on_device(
    kernel_tiles, footprints, counts, readings, damping, layer_depth, inclinations, declinations,
    resid_grid,
):
    rows, cols = lax.axis_size("row"), lax.axis_size("col")
    devices = rows * cols
    slots, sources = kernel_tiles.shape[3:]
    parts = sources // LANES
    tile_east = resid_grid.shape[0]
    east = cols * tile_east
    bands = east // LANES
    own = HALF // cols
    width = east // devices
    sizes = (rows, cols, own, bands)

    turns = north_turns(rows)
    forward_tables, inverse_tables = north_forward_tables(), north_inverse_tables()
    tables, east_turns = east_tables(east)
    hats = north_hat_table(rows, cols)

    joined = 2 * width == LANES
    everywhere = shape(devices, parts, LANES)
    beside = shape(devices, 1 + own // 4, 4, LANES) if joined else everywhere
    pieces = shape(devices, own, 2 * width)

    def apart(value):
        return HBM, pltpu.with_memory_space_constraint(value, pltpu.HBM)

    tile_scratch = scratch(FOOTPRINT, slots, sources)
    tile_sems = pltpu.SemaphoreType.DMA((FOOTPRINT,))
    codes_scratch = pltpu.SMEM((1, FOOTPRINT), jnp.int32)

    nine = shape(FOOTPRINT, parts, LANES)
    sums, kept, side, meta = call(
        functools.partial(start_kernel, sizes),
        (
            shape(rows, SENT + width // 4, parts, LANES),
            nine,
            shape(side_rows(own, bands, rows)[-1], LANES),
            shape(2 + FOOTPRINT, LANES),
        ),
        [apart(footprints), (VMEM, counts), (VMEM, damping.reshape(1, 1))]
        + [
            apart(value)
            for value in (
                readings, layer_depth, inclinations, declinations,
                jnp.asarray(east_turns), jnp.asarray(hats), resid_grid, kernel_tiles,
            )
        ],
        [
            codes_scratch,
            pltpu.SMEM((LAYERS,), F32),
            pltpu.SMEM((2, 2), F32),
            scratch(1, slots),
            scratch(*resid_grid.shape),
            tile_scratch,
            scratch(slots, LANES),
            tile_sems,
            pltpu.SemaphoreType.DMA((8,)),
        ],
    )
    arrived = lax.all_to_all(sums, "row", 0, 0, tiled=True)
    summed, column_sums = call(
        functools.partial(column_kernel, rows, cols),
        (shape(cols, SENT, parts, LANES), nine),
        [(VMEM, arrived), (VMEM, kept)],
    )
    summed = lax.all_to_all(summed, "col", 0, 0, tiled=True)

    sums, right_own, *spectrum = call(
        functools.partial(normal_kernel, rows, cols),
        (beside, shape(parts, LANES)) if joined else (everywhere, shape(parts, LANES), pieces),
        [
            (VMEM, meta),
            (VMEM, kernel_tiles),
            (VMEM, summed),
            (VMEM, column_sums),
            (VMEM, arrived),
            (VMEM, turns),
            (VMEM, forward_tables[0]),
            (VMEM, forward_tables[1]),
        ],
        [scratch(FOOTPRINT, parts, LANES)]
        + [scratch(slots, LANES), scratch(slots, LANES)]
        + [scratch(rows, width, LANES)],
    )
    sums = exchange(sums)
    shared = call(
        share_kernel, shape(devices, 2, parts, LANES), [(VMEM, sums), (VMEM, right_own)]
    )
    shared = exchange(shared)
    if joined:
        spectrum, sorted_work = sums, [scratch(cols, 2 * own, tile_east)]
    else:
        spectrum, sorted_work = exchange(spectrum[0]), []
        spectrum = spectrum.reshape(rows, cols, own, 2, width).transpose(1, 3, 2, 0, 4)
        spectrum = spectrum.reshape(cols, 2 * own, tile_east)

    second, measured, carry = call(
        functools.partial(direction_kernel, rows, cols),
        (everywhere, everywhere, shape(5, parts, LANES)),
        [(VMEM, meta), (VMEM, kernel_tiles), (VMEM, shared)],
        [scratch(slots, LANES)],
    )
    work = [
        scratch(LAYERS, 2 * rows, cols * LANES),
        scratch(LAYERS * 2 * own, east),
        scratch((own + 1) * bands, 2 * LANES),
        scratch(own * bands, 2 * LANES),
        scratch(own * bands, 2 * LANES),
    ]
    known, response = call(
        functools.partial(map_kernel, sizes, width),
        (pieces, pieces),
        [
            (VMEM, spectrum),
            (VMEM, shared),
            (VMEM, second),
            (VMEM, carry),
            (VMEM, tables),
            (VMEM, side),
        ],
        work + sorted_work,
    )
    measured = exchange(measured)
    outgoing = call(
        combine_kernel,
        pieces,
        [(VMEM, measured), (VMEM, carry), (VMEM, known), (VMEM, response)],
    )
    coefficients, rtp_map = call(
        functools.partial(finish_kernel, rows, cols),
        (shape(1, sources), shape(width, rows * LANES)),
        [
            (VMEM, exchange(outgoing)),
            (VMEM, measured),
            (VMEM, carry),
            (VMEM, turns),
            (VMEM, inverse_tables[0]),
            (VMEM, inverse_tables[1]),
        ],
        [scratch(rows * HALF, 2 * width), scratch(rows // 2 + 1, width, 2 * LANES)],
    )
    return coefficients.reshape(1, 1, sources), rtp_map


def solution(mesh):
    in_specs = (
        P("row", "col", None, None, None),
        P("row", "col", None),
        P("row", "col"),
        P("row", "col", None),
        P(),
        P(),
        P(),
        P(),
        P("col", "row"),
    )
    out_specs = (P("row", "col", None), P(("row", "col"), None))
    return jax.shard_map(
        on_device, mesh=mesh, in_specs=in_specs, out_specs=out_specs, check_vma=False
    )
```

```python
import functools

import jax
import jax.numpy as jnp
import ml_dtypes
import numpy as np
from jax import lax
from jax.experimental import pallas as pl
from jax.experimental.pallas import tpu as pltpu
from jax.sharding import PartitionSpec as P

SRC_ROWS = 8
SRC_COLS = 32
LAYERS = 2
REFINE = 16
FOOTPRINT = 9
LANES = 128
SUB = 8
HALF = 64
BOTH = ("row", "col")
COUNT, ROW, COL = 9, 10, 11
SENT = 6
MIB = 1024 * 1024
SMALL, LARGE = 24 * MIB, 62 * MIB
F32 = jnp.float32
BF16 = jnp.bfloat16

VMEM = pl.BlockSpec(memory_space=pltpu.VMEM)
SMEM = pl.BlockSpec(memory_space=pltpu.SMEM)
HBM = pl.BlockSpec(memory_space=pltpu.HBM)
NN = (((1,), (0,)), ((), ()))
NT = (((1,), (1,)), ((), ()))
TN = (((0,), (0,)), ((), ()))


def split_table(table):
    high = table.astype(ml_dtypes.bfloat16)
    low = (table - high.astype(np.float64)).astype(ml_dtypes.bfloat16)
    return np.stack([high, low])


def group_start(group, rows):
    if group == 0:
        return 0
    if group == 1:
        return rows // 2
    return group // 2 + HALF * rows * (group % 2)


def unit_turn(product, period):
    angle = 2.0 * np.pi * (product % period) / period
    return np.cos(angle), np.sin(angle)


def north_starts(rows):
    return [0, rows // 2] + list(range(1, rows // 2))


def north_turns(rows):
    north = rows * LANES
    starts = np.array(north_starts(rows))
    cos, sin = unit_turn(starts[:, None] * np.arange(north // 2)[None, :], north)
    turns = np.stack([cos, -sin]).reshape(2, len(starts), rows // 2, LANES)
    return turns.astype(np.float32)


def north_forward_tables():
    cos, sin = unit_turn(np.outer(np.arange(LANES), np.arange(LANES)), LANES)
    plain = np.block([[cos, sin], [-sin, cos]])
    packed = np.concatenate([cos[:HALF], -sin[:HALF]], 0)
    packed[HALF] = 1.0 - 2.0 * (np.arange(LANES) % 2)
    return split_table(packed), split_table(plain)


def north_inverse_tables():
    cos, sin = unit_turn(np.outer(np.arange(LANES), np.arange(LANES)), LANES)
    plain = 2.0 * np.concatenate([cos, sin], 1)
    packed = plain[:HALF].copy()
    packed[0, :LANES] = 1.0
    packed[0, LANES:] = 2.0 * (np.arange(LANES) % 2) - 1.0
    return split_table(packed), split_table(plain)


def east_tables(east):
    bands = east // LANES
    cos, sin = unit_turn(np.outer(np.arange(LANES), np.arange(LANES)), LANES)
    forward = np.block([[cos, -sin], [sin, cos]])
    inverse = np.block([[cos, sin], [-sin, cos]])
    turn_cos, turn_sin = unit_turn(np.outer(np.arange(bands), np.arange(LANES)), east)
    turns = np.concatenate([turn_cos, -turn_sin]).astype(np.float32)
    up_east = hat_table(east, east // REFINE).reshape(-1, 2 * LANES, east // REFINE)
    up_east = up_east.transpose(0, 2, 1).reshape(-1, 2 * LANES).astype(ml_dtypes.bfloat16)
    tables = [split_table(forward), split_table(inverse)]
    return np.concatenate([t.reshape(-1, 2 * LANES) for t in tables] + [up_east]), turns


def hat_table(fine_count, coarse_count):
    offset = (np.arange(fine_count)[:, None] + 0.5) / REFINE - 0.5 - np.arange(coarse_count)[None, :]
    return np.maximum(0.0, 1.0 - np.abs(offset))


def north_hat_table(rows, cols):
    north = rows * LANES
    coarse = rows * SRC_ROWS
    own = HALF // cols
    spectrum = np.fft.fft(hat_table(north, coarse), axis=0)
    out = np.zeros((rows, cols, 2 * own, coarse))
    for group in range(rows):
        for col in range(cols):
            index = group_start(group, rows) + rows * (col * own + np.arange(own))
            part = spectrum[index % north]
            out[group, col, :own] = part.real
            out[group, col, own:] = part.imag
    out[0, 0, own] = spectrum[north // 2].real
    out = out.reshape(rows * cols, 2 * own, 2 * rows, 4).transpose(0, 2, 3, 1)
    out = out.reshape(rows * cols, 2 * rows, 8 * own)
    return np.pad(out, ((0, 0), (0, 0), (0, LANES - 8 * own))).astype(np.float32)


def split(x):
    high = x.astype(BF16)
    return high, (x - high.astype(F32)).astype(BF16)


def dot(a, b, dims):
    return lax.dot_general(a, b, dims, preferred_element_type=F32)


def mul_table(x, high, low, dims=NN):
    x_high, x_low = split(x)
    return dot(x_high, high, dims) + (dot(x_low, high, dims) + dot(x_high, low, dims))


def table_mul(high, low, x, dims=NN):
    x_high, x_low = split(x)
    return dot(high, x_high, dims) + (dot(high, x_low, dims) + dot(low, x_high, dims))


def transform_list(values, sign):
    count = len(values)
    if count == 1:
        return values
    even = transform_list(values[0::2], sign)
    odd = transform_list(values[1::2], sign)
    first, second = [], []
    for k in range(count // 2):
        re, im = odd[k]
        if k == 0:
            turned = (re, im)
        elif 4 * k == count:
            turned = (im, -re) if sign < 0 else (-im, re)
        else:
            cos = float(np.cos(2.0 * np.pi * k / count))
            sin = sign * float(np.sin(2.0 * np.pi * k / count))
            if 8 * k == count or 8 * k == 3 * count:
                if cos * sin > 0:
                    turned = (cos * (re - im), cos * (re + im))
                else:
                    turned = (cos * (re + im), cos * (im - re))
            else:
                turned = (re * cos - im * sin, re * sin + im * cos)
        first.append((even[k][0] + turned[0], even[k][1] + turned[1]))
        second.append((even[k][0] - turned[0], even[k][1] - turned[1]))
    return first + second


def total(x):
    lanes = jnp.sum(jnp.sum(x, axis=0), axis=0, keepdims=True)
    return jnp.sum(lanes, axis=1, keepdims=True)


def neighbour(k, ints, rows, cols):
    code = ints[k]
    near_row = ints[ROW] + code // 3 - 1
    near_col = ints[COL] + code % 3 - 1
    inside = (near_row >= 0) & (near_row < rows) & (near_col >= 0) & (near_col < cols)
    device = jnp.clip(near_row * cols + near_col, 0, rows * cols - 1)
    return device, inside


def near_blocks(ints, vector, rows, cols):
    blocks = []
    for k in range(FOOTPRINT):
        device, inside = neighbour(k, ints, rows, cols)
        blocks.append(vector[device] * jnp.where(inside, 1.0, 0.0))
    return blocks


def apply_forward(tiles, blocks, count, out):
    slots, width = tiles.shape[1:]
    parts = width // LANES
    spread = [
        [jnp.broadcast_to(block[p : p + 1], (SUB, LANES)) for p in range(parts)] for block in blocks
    ]

    def step(t, squares):
        at = pl.multiple_of(t * SUB, SUB)
        sums = [None] * parts
        for k in range(FOOTPRINT):
            for p in range(parts):
                tile = tiles[k, pl.ds(at, SUB), p * LANES : (p + 1) * LANES]
                term = tile * spread[k][p]
                sums[p] = term if sums[p] is None else sums[p] + term
        acc = functools.reduce(jnp.add, sums)
        slot = at + lax.broadcasted_iota(jnp.int32, (SUB, LANES), 0)
        value = jnp.where(slot.astype(F32) < count, jnp.sum(acc, axis=1, keepdims=True), 0.0)
        if out is not None:
            out[pl.ds(at, SUB), :] = value
        return squares + value * value

    zero = jnp.zeros((SUB, LANES), F32)
    squares = lax.fori_loop(0, slots // SUB, step, zero, unroll=8)
    return jnp.sum(squares, axis=0, keepdims=True)


def apply_adjoint(tile, values):
    slots, width = tile.shape
    parts = width // LANES
    sums = [[None, None] for _ in range(parts)]
    for t in range(slots // SUB):
        rows = slice(t * SUB, (t + 1) * SUB)
        weight = values[rows, :]
        for p in range(parts):
            term = tile[rows, p * LANES : (p + 1) * LANES] * weight
            sums[p][t % 2] = term if t < 2 else sums[p][t % 2] + term
    return jnp.concatenate([jnp.sum(a + b, axis=0, keepdims=True) for a, b in sums], axis=0)


def tile_copies(source, tiles, sems):
    copies = [
        pltpu.make_async_copy(source.at[0, 0, k], tiles.at[k], sems.at[k]) for k in range(FOOTPRINT)
    ]
    for copy in copies:
        copy.start()
    return copies


def start_kernel(
    sizes, codes, counts, damping, readings, depth, inclinations, declinations, turns, hats, resid,
    source, out, kept, side, meta, codes_in, depth_in, angles, read, map_rows, tiles, values, sems, more,
):
    rows, cols, own, bands = sizes
    row, col = lax.axis_index("row"), lax.axis_index("col")
    _, turns_at, hats_at, end = side_rows(own, bands, rows)
    pairs = [
        (codes.at[0], codes_in),
        (depth, depth_in),
        (inclinations, angles.at[0]),
        (declinations, angles.at[1]),
        (readings.at[0], read),
        (turns, side.at[turns_at:hats_at]),
        (hats.at[row * cols + col], side.at[hats_at:end]),
        (resid, map_rows),
    ]
    first = [pltpu.make_async_copy(a, b, more.at[n]) for n, (a, b) in enumerate(pairs)]
    for copy in first:
        copy.start()
    copies = tile_copies(source, tiles, sems)
    for copy in first:
        copy.wait()
    width = map_rows.shape[0] // rows
    for i in range(rows):
        for g in range(width // 4):
            at = i * width + 4 * g
            out[i, SENT + g] = map_rows[at : at + 4]
    ints = [codes_in[0, k] for k in range(FOOTPRINT)] + [None, row, col]
    meta[0:1, :] = jnp.broadcast_to(counts[...].astype(F32), (1, LANES))
    for k in range(FOOTPRINT):
        meta[2 + k : 3 + k, :] = jnp.full((1, LANES), codes_in[0, k].astype(F32), F32)
    meta[1:2, :] = jnp.broadcast_to(damping[...], (1, LANES))
    slots = read.shape[1]
    slot = lax.broadcasted_iota(jnp.int32, (1, slots), 1)
    live = jnp.where(slot < counts[...], read[...], 0.0)
    for t in range(slots // LANES):
        square = jnp.broadcast_to(live[:, t * LANES : (t + 1) * LANES], (LANES, LANES))
        values[t * LANES : (t + 1) * LANES, :] = square.T
    trig = []
    for m in range(2):
        up = jnp.full((1, LANES), angles[0, m], F32)
        turn = jnp.full((1, LANES), angles[1, m], F32)
        flat = jnp.cos(up)
        trig += [jnp.sin(up), flat * jnp.cos(turn), flat * jnp.sin(turn)]
    put_weights(sizes, row, col, [depth_in[l] for l in range(LAYERS)], trig, side)
    for k in range(FOOTPRINT):
        copies[k].wait()
        kept[ints[k]] = apply_adjoint(tiles.at[k], values)
    fill_pieces(out, kept, row)


def fill_pieces(out, kept, here):
    for peer in range(out.shape[0]):
        low = jnp.maximum(peer - here - 1, -1)
        for slot in range(2):
            at = 3 * (jnp.clip(low + slot, -1, 1) + 1)
            out[peer, 3 * slot : 3 * slot + 3] = kept[pl.ds(at, 3)]


def arrived_part(arrived, kept, here, offset, which, other):
    if offset == 0:
        return kept[3 * (which + 1) + other]
    peer, count = here - offset, arrived.shape[0]
    slot = which - max(offset - 1, -1)
    part = arrived[jnp.clip(peer, 0, count - 1), 3 * slot + other]
    return jnp.where((peer >= 0) & (peer < count), part, 0.0)


def place_rows(out, get):
    for d in range(out.shape[0]):
        for g in range(out.shape[1] - 1):
            out[d, 1 + g] = get(d, g)


def column_kernel(rows, cols, arrived, kept, out, sums):
    row, col = lax.axis_index("row"), lax.axis_index("col")
    for north in (-1, 0, 1):
        for east in (-1, 0, 1):
            parts = [
                arrived_part(arrived, kept, row, a - north, a, east + 1) for a in (-1, 0, 1)
            ]
            target, column = row + north, col + east
            inside = (target >= 0) & (target < rows) & (column >= 0) & (column < cols)
            sums[3 * (east + 1) + north + 1] = jnp.where(inside, parts[0] + parts[1] + parts[2], 0.0)
    fill_pieces(out, sums, col)


def around(rows, cols):
    row, col = lax.axis_index("row"), lax.axis_index("col")
    for code in range(FOOTPRINT):
        north, east = row + code // 3 - 1, col + code % 3 - 1
        inside = (north >= 0) & (north < rows) & (east >= 0) & (east < cols)
        yield code, jnp.clip(north * cols + east, 0, rows * cols - 1), inside


def share_kernel(rows, cols, arrived, near, everywhere, right):
    get = (lambda d: arrived[d, 0]) if len(arrived.shape) == 4 else (lambda d: arrived[d])
    for device in range(rows * cols):
        right[device] = get(device)
    block = None
    for code, device, inside in around(rows, cols):
        part = jnp.where(inside, get(device), 0.0)
        block = part if block is None else block + part

        @pl.when(inside)
        def _():
            right[device] = near[code]

    everywhere[...] = jnp.broadcast_to(block[None], everywhere.shape)


def normal_kernel(
    rows, cols, meta, source, summed, sums, arrived, turns, packed, plain, out, near, *refs
):
    (*apart, values, planes) = refs
    tiles = source.at[0, 0]
    row, col = lax.axis_index("row"), lax.axis_index("col")
    ints = [meta[2 + k, 0].astype(jnp.int32) for k in range(FOOTPRINT)] + [None, row, col]
    for code in range(FOOTPRINT):
        north, east = code // 3 - 1, code % 3 - 1
        parts = [arrived_part(summed, sums, col, b - east, b, north + 1) for b in (-1, 0, 1)]
        near[code] = parts[0] + parts[1] + parts[2]
    blocks = [near[ints[k]] for k in range(FOOTPRINT)]
    me = row * cols + col
    own = near[FOOTPRINT // 2]
    for device in range(rows * cols):
        if apart:
            out[device] = own
        else:
            out[device, 0] = own

    def store(device, piece):
        if apart:
            apart[0][device] = piece
        else:
            for g in range(out.shape[1] - 1):
                out[device, 1 + g] = piece[4 * g : 4 * g + 4]

    north_transform(rows, cols, arrived, turns, (packed, plain), planes, store)
    apply_forward(tiles, blocks, meta[0:1, :], values)
    for k in range(FOOTPRINT):
        device, inside = neighbour(k, ints, rows, cols)
        block = apply_adjoint(tiles.at[k], values)
        block = block + jnp.where(device == me, meta[1:2, :], 0.0) * own

        @pl.when(inside)
        def _():
            if apart:
                out[device] = block
            else:
                out[device, 0] = block


def north_transform(rows, cols, arrived, turns, tables, planes, store):
    own = HALF // cols
    near, count = rows // 2, planes.shape[1]
    for i in range(rows):
        for g in range(count // 4):
            planes[i, 4 * g : 4 * g + 4, :] = arrived[i, SENT + g]
    for i in range(near):
        one, other = planes[i], planes[i + near]
        planes[i] = one + other
        planes[i + near] = one - other
    packed, plain = tables
    for n, start in enumerate(north_starts(rows)):
        base = near * (start % 2)
        re, im = None, None
        for i in range(near):
            plane = planes[base + i]
            a = plane if start == 0 else plane * turns[0, n, i : i + 1]
            re = a if re is None else re + a
            if start:
                a = plane * turns[1, n, i : i + 1]
                im = a if im is None else im + a
        if start == 0:
            result = table_mul(packed[0], packed[1], re, NT)
        else:
            result = table_mul(plain[0], plain[1], jnp.concatenate([re, im], axis=1), NT)
        imag_at = result.shape[0] // 2
        groups = [n] if n < 2 else [2 * start, 2 * start + 1]
        for h, group in enumerate(groups):
            for j in range(cols):
                at = h * HALF + j * own
                real, imag = result[at : at + own], result[imag_at + at : imag_at + at + own]
                store(group * cols + j, jnp.concatenate([real, imag], axis=1))


def pole(north, east, trig):
    square = north * north + east * east
    inverse = jnp.where(square > 0.0, lax.rsqrt(jnp.where(square > 0.0, square, 1.0)), 0.0)
    a0 = (trig[1] * north + trig[2] * east) * inverse
    a1 = (trig[4] * north + trig[5] * east) * inverse
    v0, v1 = trig[0], trig[3]
    scale = 1.0 / ((v0 * v0 + a0 * a0) * (v1 * v1 + a1 * a1))
    return (v0 * v1 - a0 * a1) * scale, -(v0 * a1 + v1 * a0) * scale, square * inverse


def side_rows(own, bands, rows):
    span = (own + 1) * bands
    turns = 2 * (1 + LAYERS) * span
    return span, turns, turns + 2 * bands, turns + 2 * bands + 2 * rows


def put_weights(sizes, row, col, depth, trig, side):
    rows, _, own, bands = sizes
    span = side_rows(own, bands, rows)[0]

    def put(part, q, at, value):
        base = (part * (1 + LAYERS) + q) * span + at
        side[base : base + value.shape[0], :] = value

    north_len, east_len = rows * LANES, bands * LANES
    scale = 1.0 / (north_len * east_len)
    start = jnp.where(
        row == 0, 0, jnp.where(row == 1, rows // 2, row // 2 + HALF * rows * (row % 2))
    )

    def signed(index, length):
        return jnp.where(index < length // 2, index, index - length).astype(F32) / length

    def north_of(shape):
        index = start + rows * (col * own + lax.broadcasted_iota(jnp.int32, shape, 0))
        return signed(index, north_len)

    def weights(re, im, radius):
        damp = [None] + [jnp.exp(radius * (-2.0 * np.pi * depth[l])) for l in range(LAYERS)]
        return [(re, im) if d is None else (re * d, im * d) for d in damp]

    lane = lax.broadcasted_iota(jnp.int32, (own, LANES), 1)
    north = north_of((own, LANES))
    for band in range(bands):
        east = signed(band + bands * lane, east_len)
        re, im, radius = pole(north, east, trig)
        if band == 0:
            re2, im2, _ = pole(north, jnp.where(lane == HALF, 0.5, east), trig)
            re, im = 0.5 * (re + re2), 0.5 * (im + im2)
        for q, (wr, wi) in enumerate(weights(re * scale, im * scale, radius)):
            put(0, q, band * own, wr)
            put(1, q, band * own, wi)
            put(0, q, bands * own, jnp.zeros((bands, LANES), F32))
            put(1, q, bands * own, jnp.zeros((bands, LANES), F32))

    @pl.when((row == 0) & (col == 0))
    def _():
        band = lax.broadcasted_iota(jnp.int32, (bands, LANES), 0)
        lanes = lax.broadcasted_iota(jnp.int32, (bands, LANES), 1)
        east = signed(band + bands * lanes, east_len)
        flipped = jnp.where((band == 0) & (lanes == HALF), 0.5, east)
        pairs = []
        for one, other in ((0.0, 0.0), (-0.5, 0.5)):
            re, im, radius = pole(jnp.full_like(east, one), east, trig)
            re2, im2, _ = pole(jnp.full_like(east, other), flipped, trig)
            half = 0.5 * scale
            pairs.append(weights(half * (re + re2), half * (im + im2), radius))
        for q in range(1 + LAYERS):
            (r0, i0), (r1, i1) = pairs[0][q], pairs[1][q]
            put(0, q, bands * own, 0.5 * (r0 - r1))
            put(1, q, bands * own, 0.5 * (i0 - i1))
            for b in range(bands):
                put(0, q, b * own, 0.5 * (r0 + r1)[b : b + 1])
                put(1, q, b * own, 0.5 * (i0 + i1)[b : b + 1])


def turn_rows(side, turns_at, band, bands):
    cos, sin = turns_at + band, turns_at + bands + band
    return side[cos : cos + 1, :], side[sin : sin + 1, :]


def east_table(tables, index):
    span = 2 * LANES
    return tables[2 * index * span : (2 * index + 1) * span], tables[
        (2 * index + 1) * span : (2 * index + 2) * span
    ]


def east_forward(get, sizes, side, tables, work):
    rows, _, own, bands = sizes
    turns_at = side_rows(own, bands, rows)[1]
    for g in range(own // SUB):
        values = transform_list([get(m, g) for m in range(bands)], -1.0)
        for b in range(bands):
            cos, sin = turn_rows(side, turns_at, b, bands)
            re, im = values[b]
            at = b * own + g * SUB
            work[at : at + SUB, :LANES] = re * cos - im * sin
            work[at : at + SUB, LANES:] = re * sin + im * cos
            if g == 0:
                re, im = values[(bands - b) % bands]
                re, im = re[0:1], -im[0:1]
                at = bands * own + b
                work[at : at + 1, :LANES] = re * cos - im * sin
                work[at : at + 1, LANES:] = re * sin + im * cos
    return mul_table(work[...], *east_table(tables, 0))


def weigh(spectrum, q, sizes, side, into, first):
    rows, _, own, bands = sizes
    span = side_rows(own, bands, rows)[0]
    re, im = spectrum[:, :LANES], spectrum[:, LANES:]
    wr = side[q * span : (q + 1) * span, :]
    wi = side[(1 + LAYERS + q) * span : (2 + LAYERS + q) * span, :]
    out_re, out_im = re * wr - im * wi, re * wi + im * wr
    main = own * bands
    if first:
        into[:, :LANES] = out_re[:main]
        into[:, LANES:] = out_im[:main]
    else:
        into[:, :LANES] += out_re[:main]
        into[:, LANES:] += out_im[:main]
    for b in range(bands):
        into[b * own : b * own + 1, :LANES] += out_re[main + b : main + b + 1]
        into[b * own : b * own + 1, LANES:] += out_im[main + b : main + b + 1]


def east_inverse(spectrum, sizes, side, tables, work, store):
    rows, _, own, bands = sizes
    turns_at = side_rows(own, bands, rows)[1]
    work[...] = mul_table(spectrum[...], *east_table(tables, 1))
    for g in range(own // SUB):
        values = []
        for b in range(bands):
            at = b * own + g * SUB
            re, im = work[at : at + SUB, :LANES], work[at : at + SUB, LANES:]
            cos, sin = turn_rows(side, turns_at, b, bands)
            values.append((re * cos + im * sin, im * cos - re * sin))
        values = transform_list(values, 1.0)
        for b in range(bands):
            store(b, g, *values[b])


def store_pieces(out, width):
    per_band = LANES // width

    def store(band, g, re, im):
        for s in range(per_band):
            cut = slice(s * width, (s + 1) * width)
            piece = jnp.concatenate([re[:, cut], im[:, cut]], axis=1)
            out[band * per_band + s, g * SUB : (g + 1) * SUB] = piece

    return store


def model_rows(vector, sizes, side, coarse):
    rows, cols, own, bands = sizes
    own2 = 2 * own
    for i in range(rows):
        for j in range(cols):
            block = vector[i * cols + j]
            for layer in range(LAYERS):
                coarse[layer, 2 * i : 2 * i + 2, j * LANES : (j + 1) * LANES] = block[
                    2 * layer : 2 * layer + 2
                ]
    out = []
    _, _, hats_at, end = side_rows(own, bands, rows)
    high, low = split(side[hats_at:end, :])
    tiles = cols * SRC_COLS // LANES
    lane = lax.broadcasted_iota(jnp.int32, (own2, LANES), 1) // SRC_COLS
    for layer in range(LAYERS):
        mixed = table_mul(high, low, coarse[layer], TN)
        whole = []
        for tile in range(tiles):
            joined = None
            for place in range(LANES // SRC_COLS):
                j = tile * (LANES // SRC_COLS) + place
                summed = None
                for part in range(4):
                    piece = mixed[part * own2 : (part + 1) * own2, j * LANES : (j + 1) * LANES]
                    shift = ((place - part) * SRC_COLS) % LANES
                    if shift:
                        piece = pltpu.roll(piece, shift, 1)
                    summed = piece if summed is None else summed + piece
                joined = summed if joined is None else jnp.where(lane == place, summed, joined)
            whole.append(joined)
        out.append(whole[0] if tiles == 1 else jnp.concatenate(whole, axis=1))
    return out


def model_mix(vector, scale, sizes, side, tables, coarse, fine, work, mixed, first):
    rows, cols, own, bands = sizes
    depth = cols * SRC_COLS
    planes = jnp.concatenate(model_rows(vector, sizes, side, coarse), axis=0)
    high, low = split(planes if scale is None else planes * scale)
    for c in range(bands // 2):
        at = 8 * LANES + c * depth
        table = tables[at : at + depth, :]
        fine[:, 2 * LANES * c : 2 * LANES * (c + 1)] = dot(high, table, NN) + dot(low, table, NN)
    for layer in range(LAYERS):

        def get(m, g, base=2 * own * layer):
            at = base + g * SUB
            cut = slice(m * LANES, (m + 1) * LANES)
            return fine[at : at + SUB, cut], fine[at + own : at + own + SUB, cut]

        spectrum = east_forward(get, sizes, side, tables, work)
        weigh(spectrum, 1 + layer, sizes, side, mixed, first and layer == 0)


def sort_east(arrived, sizes, spec):
    rows, cols, own, bands = sizes
    left = lax.broadcasted_iota(jnp.int32, (SUB, LANES), 1) < HALF
    for j in range(cols):
        for i in range(0, rows, 2):
            for g in range(own // SUB):
                pair = []
                for source in (i * cols + j, (i + 1) * cols + j):
                    at = 1 + 2 * g
                    both = [arrived[source, at], arrived[source, at + 1]]
                    pair.append(jnp.concatenate(both, axis=0))
                cut = slice(i * HALF, (i + 2) * HALF)
                at = g * SUB
                spec[j, at : at + SUB, cut] = jnp.where(left, pair[0], pltpu.roll(pair[1], HALF, 1))
                at = own + g * SUB
                spec[j, at : at + SUB, cut] = jnp.where(left, pltpu.roll(pair[0], HALF, 1), pair[1])


def map_kernel(
    sizes, width, arrived, first, second, carry, tables, side, known, response,
    coarse, fine, work, mixed, back, *spec,
):
    rows, cols, own, bands = sizes
    if spec:
        sort_east(arrived, sizes, spec[0])
    spec = spec[0] if spec else arrived
    per = spec.shape[2] // LANES

    def get(m, g):
        cut = slice((m % per) * LANES, (m % per + 1) * LANES)
        at = g * SUB
        return spec[m // per, at : at + SUB, cut], spec[m // per, own + at : own + at + SUB, cut]

    spectrum = east_forward(get, sizes, side, tables, work)
    weigh(spectrum, 0, sizes, side, mixed, True)
    model_mix(first, carry[4, 0:1, 0:1], sizes, side, tables, coarse, fine, work, mixed, False)
    east_inverse(mixed, sizes, side, tables, back, store_pieces(known, width))
    model_mix(second, None, sizes, side, tables, coarse, fine, work, mixed, True)
    east_inverse(mixed, sizes, side, tables, back, store_pieces(response, width))


def direction_kernel(rows, cols, meta, source, first, applied, second, measured, carry):
    tiles = source.at[0, 0]
    row, col = lax.axis_index("row"), lax.axis_index("col")
    norm = total(first[...] * first[...])
    step = norm / total(first[...] * applied[...])
    residual = first[...] - step[None] * applied[...]
    norm_next = total(residual * residual)
    second[...] = residual + (norm_next / norm)[None] * first[...]
    ridge = meta[1:2, 0:1] * total(second[...] * second[...])
    me = row * cols + col
    carry[0] = step * first[me]
    carry[1] = second[me]
    for at, value in ((2, norm_next), (3, ridge), (4, step)):
        carry[at] = jnp.broadcast_to(value, carry.shape[1:])
    ints = [meta[2 + k, 0].astype(jnp.int32) for k in range(FOOTPRINT)] + [None, row, col]
    blocks = near_blocks(ints, second, rows, cols)
    squares = apply_forward(tiles, blocks, meta[0:1, :], None)
    measured[...] = jnp.broadcast_to(squares[None], measured.shape)


def last_step(measured, carry):
    squares = jnp.sum(measured[:, 0:1], axis=0)
    return carry[2, 0:1, 0:1] / (squares[:, 0:1] + carry[3, 0:1, 0:1])


def combine_kernel(measured, carry, known, response, out):
    out[...] = known[...] + last_step(measured, carry)[None] * response[...]


def finish_kernel(
    rows, cols, arrived, measured, carry, turns, packed, plain, coefficients, out, mixed, waves
):
    solved = carry[0] + last_step(measured, carry) * carry[1]
    for p in range(solved.shape[0]):
        coefficients[:, p * LANES : (p + 1) * LANES] = solved[p : p + 1]
    own = arrived.shape[1]
    width = out.shape[0]
    near = rows // 2
    for i in range(rows):
        for j in range(cols):
            at = i * HALF + j * own
            mixed[at : at + own, :] = arrived[i * cols + j]
    starts = north_starts(rows)
    for n, start in enumerate(starts):
        if n == 0:
            both = mul_table(mixed[0:HALF], packed[0], packed[1], TN)
        elif n == 1:
            both = mul_table(mixed[HALF : 2 * HALF], plain[0, :HALF], plain[1, :HALF], TN)
        else:
            at = 2 * start * HALF
            both = mul_table(mixed[at : at + 2 * HALF], plain[0], plain[1], TN)
        top, bottom = both[:width], both[width:]
        waves[n, :, :LANES] = top[:, :LANES] - bottom[:, LANES:]
        waves[n, :, LANES:] = top[:, LANES:] + bottom[:, :LANES]
    for at in range(0, width, SUB):
        parts = [[None, None] for _ in range(near)]
        for n, start in enumerate(starts):
            re = waves[n, at : at + SUB, :LANES]
            im = waves[n, at : at + SUB, LANES:]
            for i in range(near):
                if start == 0:
                    term = re
                else:
                    term = re * turns[0, n, i : i + 1] + im * turns[1, n, i : i + 1]
                sums = parts[i]
                sums[start % 2] = term if sums[start % 2] is None else sums[start % 2] + term
        for i in range(near):
            even, odd = parts[i]
            out[at : at + SUB, i * LANES : (i + 1) * LANES] = even + odd
            out[at : at + SUB, (near + i) * LANES : (near + i + 1) * LANES] = even - odd


def shape(*dims):
    return jax.ShapeDtypeStruct(dims, F32)


def scratch(*dims):
    return pltpu.VMEM(dims, F32)


def call(kernel, outs, ins, work=(), limit=SMALL):
    return pl.pallas_call(
        kernel,
        out_shape=outs,
        in_specs=[spec for spec, _ in ins],
        out_specs=jax.tree.map(lambda _: VMEM, outs),
        scratch_shapes=list(work),
        compiler_params=pltpu.CompilerParams(vmem_limit_bytes=limit),
    )(*[value for _, value in ins])


def exchange(pieces):
    return lax.all_to_all(pieces, BOTH, 0, 0, tiled=True)


def on_device(
    kernel_tiles, footprints, counts, readings, damping, layer_depth, inclinations, declinations,
    resid_grid,
):
    rows, cols = lax.axis_size("row"), lax.axis_size("col")
    devices = rows * cols
    slots, sources = kernel_tiles.shape[3:]
    parts = sources // LANES
    tile_east = resid_grid.shape[0]
    east = cols * tile_east
    bands = east // LANES
    own = HALF // cols
    width = east // devices
    sizes = (rows, cols, own, bands)

    turns = north_turns(rows)
    forward_tables, inverse_tables = north_forward_tables(), north_inverse_tables()
    tables, east_turns = east_tables(east)
    hats = north_hat_table(rows, cols)

    joined = 2 * width == LANES
    everywhere = shape(devices, parts, LANES)
    beside = shape(devices, 1 + own // 4, 4, LANES) if joined else everywhere
    pieces = shape(devices, own, 2 * width)

    def apart(value):
        return HBM, pltpu.with_memory_space_constraint(value, pltpu.HBM)

    tile_scratch = scratch(FOOTPRINT, slots, sources)
    tile_sems = pltpu.SemaphoreType.DMA((FOOTPRINT,))
    codes_scratch = pltpu.SMEM((1, FOOTPRINT), jnp.int32)

    nine = shape(FOOTPRINT, parts, LANES)
    sums, kept, side, meta = call(
        functools.partial(start_kernel, sizes),
        (
            shape(rows, SENT + width // 4, parts, LANES),
            nine,
            shape(side_rows(own, bands, rows)[-1], LANES),
            shape(2 + FOOTPRINT, LANES),
        ),
        [apart(footprints), (VMEM, counts), (VMEM, damping.reshape(1, 1))]
        + [
            apart(value)
            for value in (
                readings, layer_depth, inclinations, declinations,
                jnp.asarray(east_turns), jnp.asarray(hats), resid_grid, kernel_tiles,
            )
        ],
        [
            codes_scratch,
            pltpu.SMEM((LAYERS,), F32),
            pltpu.SMEM((2, 2), F32),
            scratch(1, slots),
            scratch(*resid_grid.shape),
            tile_scratch,
            scratch(slots, LANES),
            tile_sems,
            pltpu.SemaphoreType.DMA((8,)),
        ],
    )
    arrived = lax.all_to_all(sums, "row", 0, 0, tiled=True)
    summed, column_sums = call(
        functools.partial(column_kernel, rows, cols),
        (shape(cols, SENT, parts, LANES), nine),
        [(VMEM, arrived), (VMEM, kept)],
    )
    summed = lax.all_to_all(summed, "col", 0, 0, tiled=True)

    sums, near, *spectrum = call(
        functools.partial(normal_kernel, rows, cols),
        (beside, nine) if joined else (everywhere, nine, pieces),
        [
            (VMEM, meta),
            (VMEM, kernel_tiles),
            (VMEM, summed),
            (VMEM, column_sums),
            (VMEM, arrived),
            (VMEM, turns),
            (VMEM, forward_tables[0]),
            (VMEM, forward_tables[1]),
        ],
        [scratch(slots, LANES), scratch(rows, width, LANES)],
    )
    sums = exchange(sums)
    applied_all, right_side = call(
        functools.partial(share_kernel, rows, cols),
        (everywhere, everywhere),
        [(VMEM, sums), (VMEM, near)],
    )
    applied = exchange(applied_all)
    if joined:
        spectrum, sorted_work = sums, [scratch(cols, 2 * own, tile_east)]
    else:
        spectrum, sorted_work = exchange(spectrum[0]), []
        spectrum = spectrum.reshape(rows, cols, own, 2, width).transpose(1, 3, 2, 0, 4)
        spectrum = spectrum.reshape(cols, 2 * own, tile_east)

    second, measured, carry = call(
        functools.partial(direction_kernel, rows, cols),
        (everywhere, everywhere, shape(5, parts, LANES)),
        [(VMEM, meta), (VMEM, kernel_tiles), (VMEM, right_side), (VMEM, applied)],
    )
    work = [
        scratch(LAYERS, 2 * rows, cols * LANES),
        scratch(LAYERS * 2 * own, east),
        scratch((own + 1) * bands, 2 * LANES),
        scratch(own * bands, 2 * LANES),
        scratch(own * bands, 2 * LANES),
    ]
    known, response = call(
        functools.partial(map_kernel, sizes, width),
        (pieces, pieces),
        [
            (VMEM, spectrum),
            (VMEM, right_side),
            (VMEM, second),
            (VMEM, carry),
            (VMEM, tables),
            (VMEM, side),
        ],
        work + sorted_work,
    )
    measured = exchange(measured)
    outgoing = call(
        combine_kernel,
        pieces,
        [(VMEM, measured), (VMEM, carry), (VMEM, known), (VMEM, response)],
    )
    coefficients, rtp_map = call(
        functools.partial(finish_kernel, rows, cols),
        (shape(1, sources), shape(width, rows * LANES)),
        [
            (VMEM, exchange(outgoing)),
            (VMEM, measured),
            (VMEM, carry),
            (VMEM, turns),
            (VMEM, inverse_tables[0]),
            (VMEM, inverse_tables[1]),
        ],
        [scratch(rows * HALF, 2 * width), scratch(rows // 2 + 1, width, 2 * LANES)],
    )
    return coefficients.reshape(1, 1, sources), rtp_map


def solution(mesh):
    in_specs = (
        P("row", "col", None, None, None),
        P("row", "col", None),
        P("row", "col"),
        P("row", "col", None),
        P(),
        P(),
        P(),
        P(),
        P("col", "row"),
    )
    out_specs = (P("row", "col", None), P(("row", "col"), None))
    return jax.shard_map(
        on_device, mesh=mesh, in_specs=in_specs, out_specs=out_specs, check_vma=False
    )
```

```python
import functools

import jax
import jax.numpy as jnp
import ml_dtypes
import numpy as np
from jax import lax
from jax.experimental import pallas as pl
from jax.experimental.pallas import tpu as pltpu
from jax.sharding import PartitionSpec as P

SRC_ROWS = 8
SRC_COLS = 32
LAYERS = 2
REFINE = 16
FOOTPRINT = 9
LANES = 128
SUB = 8
HALF = 64
BOTH = ("row", "col")
COUNT, ROW, COL = 9, 10, 11
SENT = 6
MIB = 1024 * 1024
SMALL, LARGE = 24 * MIB, 62 * MIB
F32 = jnp.float32
BF16 = jnp.bfloat16

VMEM = pl.BlockSpec(memory_space=pltpu.VMEM)
SMEM = pl.BlockSpec(memory_space=pltpu.SMEM)
HBM = pl.BlockSpec(memory_space=pltpu.HBM)
NN = (((1,), (0,)), ((), ()))
NT = (((1,), (1,)), ((), ()))
TN = (((0,), (0,)), ((), ()))


def split_table(table):
    high = table.astype(ml_dtypes.bfloat16)
    low = (table - high.astype(np.float64)).astype(ml_dtypes.bfloat16)
    return np.stack([high, low])


def group_start(group, rows):
    if group == 0:
        return 0
    if group == 1:
        return rows // 2
    return group // 2 + HALF * rows * (group % 2)


def unit_turn(product, period):
    angle = 2.0 * np.pi * (product % period) / period
    return np.cos(angle), np.sin(angle)


def north_starts(rows):
    return [0, rows // 2] + list(range(1, rows // 2))


def north_turns(rows):
    north = rows * LANES
    starts = np.array(north_starts(rows))
    cos, sin = unit_turn(starts[:, None] * np.arange(north // 2)[None, :], north)
    turns = np.stack([cos, -sin]).reshape(2, len(starts), rows // 2, LANES)
    return turns.astype(np.float32)


def north_forward_tables():
    cos, sin = unit_turn(np.outer(np.arange(LANES), np.arange(LANES)), LANES)
    plain = np.block([[cos, sin], [-sin, cos]])
    packed = np.concatenate([cos[:HALF], -sin[:HALF]], 0)
    packed[HALF] = 1.0 - 2.0 * (np.arange(LANES) % 2)
    return split_table(packed), split_table(plain)


def north_inverse_tables():
    cos, sin = unit_turn(np.outer(np.arange(LANES), np.arange(LANES)), LANES)
    plain = 2.0 * np.concatenate([cos, sin], 1)
    packed = plain[:HALF].copy()
    packed[0, :LANES] = 1.0
    packed[0, LANES:] = 2.0 * (np.arange(LANES) % 2) - 1.0
    return split_table(packed), split_table(plain)


def east_tables(east):
    bands = east // LANES
    cos, sin = unit_turn(np.outer(np.arange(LANES), np.arange(LANES)), LANES)
    forward = np.block([[cos, -sin], [sin, cos]])
    inverse = np.block([[cos, sin], [-sin, cos]])
    turn_cos, turn_sin = unit_turn(np.outer(np.arange(bands), np.arange(LANES)), east)
    turns = np.concatenate([turn_cos, -turn_sin]).astype(np.float32)
    up_east = hat_table(east, east // REFINE).reshape(-1, 2 * LANES, east // REFINE)
    up_east = up_east.transpose(0, 2, 1).reshape(-1, 2 * LANES).astype(ml_dtypes.bfloat16)
    tables = [split_table(forward), split_table(inverse)]
    return np.concatenate([t.reshape(-1, 2 * LANES) for t in tables] + [up_east]), turns


def hat_table(fine_count, coarse_count):
    offset = (np.arange(fine_count)[:, None] + 0.5) / REFINE - 0.5 - np.arange(coarse_count)[None, :]
    return np.maximum(0.0, 1.0 - np.abs(offset))


def north_hat_table(rows, cols):
    north = rows * LANES
    coarse = rows * SRC_ROWS
    own = HALF // cols
    spectrum = np.fft.fft(hat_table(north, coarse), axis=0)
    out = np.zeros((rows, cols, 2 * own, coarse))
    for group in range(rows):
        for col in range(cols):
            index = group_start(group, rows) + rows * (col * own + np.arange(own))
            part = spectrum[index % north]
            out[group, col, :own] = part.real
            out[group, col, own:] = part.imag
    out[0, 0, own] = spectrum[north // 2].real
    out = out.reshape(rows * cols, 2 * own, 2 * rows, 4).transpose(0, 2, 3, 1)
    out = out.reshape(rows * cols, 2 * rows, 8 * own)
    return np.pad(out, ((0, 0), (0, 0), (0, LANES - 8 * own))).astype(np.float32)


def split(x):
    high = x.astype(BF16)
    return high, (x - high.astype(F32)).astype(BF16)


def dot(a, b, dims):
    return lax.dot_general(a, b, dims, preferred_element_type=F32)


def mul_table(x, high, low, dims=NN):
    x_high, x_low = split(x)
    return dot(x_high, high, dims) + (dot(x_low, high, dims) + dot(x_high, low, dims))


def table_mul(high, low, x, dims=NN):
    x_high, x_low = split(x)
    return dot(high, x_high, dims) + (dot(high, x_low, dims) + dot(low, x_high, dims))


def transform_list(values, sign):
    count = len(values)
    if count == 1:
        return values
    even = transform_list(values[0::2], sign)
    odd = transform_list(values[1::2], sign)
    first, second = [], []
    for k in range(count // 2):
        re, im = odd[k]
        if k == 0:
            turned = (re, im)
        elif 4 * k == count:
            turned = (im, -re) if sign < 0 else (-im, re)
        else:
            cos = float(np.cos(2.0 * np.pi * k / count))
            sin = sign * float(np.sin(2.0 * np.pi * k / count))
            if 8 * k == count or 8 * k == 3 * count:
                if cos * sin > 0:
                    turned = (cos * (re - im), cos * (re + im))
                else:
                    turned = (cos * (re + im), cos * (im - re))
            else:
                turned = (re * cos - im * sin, re * sin + im * cos)
        first.append((even[k][0] + turned[0], even[k][1] + turned[1]))
        second.append((even[k][0] - turned[0], even[k][1] - turned[1]))
    return first + second


def total(x):
    lanes = jnp.sum(jnp.sum(x, axis=0), axis=0, keepdims=True)
    return jnp.sum(lanes, axis=1, keepdims=True)


def neighbour(k, ints, rows, cols):
    code = ints[k]
    near_row = ints[ROW] + code // 3 - 1
    near_col = ints[COL] + code % 3 - 1
    inside = (near_row >= 0) & (near_row < rows) & (near_col >= 0) & (near_col < cols)
    device = jnp.clip(near_row * cols + near_col, 0, rows * cols - 1)
    return device, inside


def near_blocks(ints, vector, rows, cols):
    blocks = []
    for k in range(FOOTPRINT):
        device, inside = neighbour(k, ints, rows, cols)
        blocks.append(vector[device] * jnp.where(inside, 1.0, 0.0))
    return blocks


def apply_forward(tiles, blocks, count, out):
    slots, width = tiles.shape[1:]
    parts = width // LANES
    spread = [
        [jnp.broadcast_to(block[p : p + 1], (SUB, LANES)) for p in range(parts)] for block in blocks
    ]

    def step(t, squares):
        at = pl.multiple_of(t * SUB, SUB)
        sums = [None] * parts
        for k in range(FOOTPRINT):
            for p in range(parts):
                tile = tiles[k, pl.ds(at, SUB), p * LANES : (p + 1) * LANES]
                term = tile * spread[k][p]
                sums[p] = term if sums[p] is None else sums[p] + term
        acc = functools.reduce(jnp.add, sums)
        slot = at + lax.broadcasted_iota(jnp.int32, (SUB, LANES), 0)
        value = jnp.where(slot.astype(F32) < count, jnp.sum(acc, axis=1, keepdims=True), 0.0)
        if out is not None:
            out[pl.ds(at, SUB), :] = value
        return squares + value * value

    zero = jnp.zeros((SUB, LANES), F32)
    squares = lax.fori_loop(0, slots // SUB, step, zero, unroll=8)
    return jnp.sum(squares, axis=0, keepdims=True)


def apply_adjoint(tile, values):
    slots, width = tile.shape
    parts = width // LANES
    sums = [[None, None] for _ in range(parts)]
    for t in range(slots // SUB):
        rows = slice(t * SUB, (t + 1) * SUB)
        weight = values[rows, :]
        for p in range(parts):
            term = tile[rows, p * LANES : (p + 1) * LANES] * weight
            sums[p][t % 2] = term if t < 2 else sums[p][t % 2] + term
    return jnp.concatenate([jnp.sum(a + b, axis=0, keepdims=True) for a, b in sums], axis=0)


def tile_copies(source, tiles, sems):
    copies = [
        pltpu.make_async_copy(source.at[0, 0, k], tiles.at[k], sems.at[k]) for k in range(FOOTPRINT)
    ]
    for copy in copies:
        copy.start()
    return copies


def start_kernel(
    sizes, codes, counts, damping, readings, depth, inclinations, declinations, turns, hats, resid,
    source, out, kept, side, meta, codes_in, depth_in, angles, read, map_rows, tiles, values, sems, more,
):
    rows, cols, own, bands = sizes
    row, col = lax.axis_index("row"), lax.axis_index("col")
    _, turns_at, hats_at, end = side_rows(own, bands, rows)
    pairs = [
        (codes.at[0], codes_in),
        (depth, depth_in),
        (inclinations, angles.at[0]),
        (declinations, angles.at[1]),
        (readings.at[0], read),
        (turns, side.at[turns_at:hats_at]),
        (hats.at[row * cols + col], side.at[hats_at:end]),
        (resid, map_rows),
    ]
    first = [pltpu.make_async_copy(a, b, more.at[n]) for n, (a, b) in enumerate(pairs)]
    for copy in first:
        copy.start()
    copies = tile_copies(source, tiles, sems)
    for copy in first:
        copy.wait()
    width = map_rows.shape[0] // rows
    for i in range(rows):
        for g in range(width // 4):
            at = i * width + 4 * g
            out[i, SENT + g] = map_rows[at : at + 4]
    ints = [codes_in[0, k] for k in range(FOOTPRINT)] + [None, row, col]
    meta[0:1, :] = jnp.broadcast_to(counts[...].astype(F32), (1, LANES))
    for k in range(FOOTPRINT):
        meta[2 + k : 3 + k, :] = jnp.full((1, LANES), codes_in[0, k].astype(F32), F32)
    meta[1:2, :] = jnp.broadcast_to(damping[...], (1, LANES))
    slots = read.shape[1]
    slot = lax.broadcasted_iota(jnp.int32, (1, slots), 1)
    live = jnp.where(slot < counts[...], read[...], 0.0)
    for t in range(slots // LANES):
        square = jnp.broadcast_to(live[:, t * LANES : (t + 1) * LANES], (LANES, LANES))
        values[t * LANES : (t + 1) * LANES, :] = square.T
    trig = []
    for m in range(2):
        up = jnp.full((1, LANES), angles[0, m], F32)
        turn = jnp.full((1, LANES), angles[1, m], F32)
        flat = jnp.cos(up)
        trig += [jnp.sin(up), flat * jnp.cos(turn), flat * jnp.sin(turn)]
    put_weights(sizes, row, col, [depth_in[l] for l in range(LAYERS)], trig, side)
    for k in range(FOOTPRINT):
        copies[k].wait()
        kept[ints[k]] = apply_adjoint(tiles.at[k], values)
    fill_pieces(out, kept, row)


def fill_pieces(out, kept, here):
    for peer in range(out.shape[0]):
        low = jnp.maximum(peer - here - 1, -1)
        for slot in range(2):
            at = 3 * (jnp.clip(low + slot, -1, 1) + 1)
            out[peer, 3 * slot : 3 * slot + 3] = kept[pl.ds(at, 3)]


def arrived_part(arrived, kept, here, offset, which, other):
    if offset == 0:
        return kept[3 * (which + 1) + other]
    peer, count = here - offset, arrived.shape[0]
    slot = which - max(offset - 1, -1)
    part = arrived[jnp.clip(peer, 0, count - 1), 3 * slot + other]
    return jnp.where((peer >= 0) & (peer < count), part, 0.0)


def place_rows(out, get):
    for d in range(out.shape[0]):
        for g in range(out.shape[1] - 1):
            out[d, 1 + g] = get(d, g)


def column_kernel(rows, cols, arrived, kept, out, sums):
    row, col = lax.axis_index("row"), lax.axis_index("col")
    for north in (-1, 0, 1):
        for east in (-1, 0, 1):
            parts = [
                arrived_part(arrived, kept, row, a - north, a, east + 1) for a in (-1, 0, 1)
            ]
            target, column = row + north, col + east
            inside = (target >= 0) & (target < rows) & (column >= 0) & (column < cols)
            sums[3 * (east + 1) + north + 1] = jnp.where(inside, parts[0] + parts[1] + parts[2], 0.0)
    fill_pieces(out, sums, col)


def around(rows, cols):
    row, col = lax.axis_index("row"), lax.axis_index("col")
    for code in range(FOOTPRINT):
        north, east = row + code // 3 - 1, col + code % 3 - 1
        inside = (north >= 0) & (north < rows) & (east >= 0) & (east < cols)
        yield code, jnp.clip(north * cols + east, 0, rows * cols - 1), inside


def share_kernel(rows, cols, arrived, near, everywhere, right):
    get = (lambda d: arrived[d, 0]) if len(arrived.shape) == 4 else (lambda d: arrived[d])
    for device in range(rows * cols):
        right[device] = get(device)
    block = None
    for code, device, inside in around(rows, cols):
        part = jnp.where(inside, get(device), 0.0)
        block = part if block is None else block + part

        @pl.when(inside)
        def _():
            right[device] = near[code]

    everywhere[...] = jnp.broadcast_to(block[None], everywhere.shape)


def normal_kernel(
    rows, cols, meta, source, summed, sums, arrived, turns, packed, plain, out, near, *refs
):
    (*apart, values, planes) = refs
    tiles = source.at[0, 0]
    row, col = lax.axis_index("row"), lax.axis_index("col")
    ints = [meta[2 + k, 0].astype(jnp.int32) for k in range(FOOTPRINT)] + [None, row, col]
    for code in range(FOOTPRINT):
        north, east = code // 3 - 1, code % 3 - 1
        parts = [arrived_part(summed, sums, col, b - east, b, north + 1) for b in (-1, 0, 1)]
        near[code] = parts[0] + parts[1] + parts[2]
    blocks = [near[ints[k]] for k in range(FOOTPRINT)]
    me = row * cols + col
    own = near[FOOTPRINT // 2]
    for device in range(rows * cols):
        if apart:
            out[device] = own
        else:
            out[device, 0] = own

    def store(device, piece):
        if apart:
            apart[0][device] = piece
        else:
            for g in range(out.shape[1] - 1):
                out[device, 1 + g] = piece[4 * g : 4 * g + 4]

    north_transform(rows, cols, arrived, turns, (packed, plain), planes, store)
    apply_forward(tiles, blocks, meta[0:1, :], values)
    for k in range(FOOTPRINT):
        device, inside = neighbour(k, ints, rows, cols)
        block = apply_adjoint(tiles.at[k], values)
        block = block + jnp.where(device == me, meta[1:2, :], 0.0) * own

        @pl.when(inside)
        def _():
            if apart:
                out[device] = block
            else:
                out[device, 0] = block


def north_transform(rows, cols, arrived, turns, tables, planes, store):
    own = HALF // cols
    near, count = rows // 2, planes.shape[1]
    for i in range(rows):
        for g in range(count // 4):
            planes[i, 4 * g : 4 * g + 4, :] = arrived[i, SENT + g]
    for i in range(near):
        one, other = planes[i], planes[i + near]
        planes[i] = one + other
        planes[i + near] = one - other
    packed, plain = tables
    for n, start in enumerate(north_starts(rows)):
        base = near * (start % 2)
        re, im = None, None
        for i in range(near):
            plane = planes[base + i]
            a = plane if start == 0 else plane * turns[0, n, i : i + 1]
            re = a if re is None else re + a
            if start:
                a = plane * turns[1, n, i : i + 1]
                im = a if im is None else im + a
        if start == 0:
            result = table_mul(packed[0], packed[1], re, NT)
        else:
            result = table_mul(plain[0], plain[1], jnp.concatenate([re, im], axis=1), NT)
        imag_at = result.shape[0] // 2
        groups = [n] if n < 2 else [2 * start, 2 * start + 1]
        for h, group in enumerate(groups):
            for j in range(cols):
                at = h * HALF + j * own
                real, imag = result[at : at + own], result[imag_at + at : imag_at + at + own]
                store(group * cols + j, jnp.concatenate([real, imag], axis=1))


def pole(north, east, trig):
    square = north * north + east * east
    inverse = jnp.where(square > 0.0, lax.rsqrt(jnp.where(square > 0.0, square, 1.0)), 0.0)
    a0 = (trig[1] * north + trig[2] * east) * inverse
    a1 = (trig[4] * north + trig[5] * east) * inverse
    v0, v1 = trig[0], trig[3]
    scale = 1.0 / ((v0 * v0 + a0 * a0) * (v1 * v1 + a1 * a1))
    return (v0 * v1 - a0 * a1) * scale, -(v0 * a1 + v1 * a0) * scale, square * inverse


def side_rows(own, bands, rows):
    span = (own + 1) * bands
    turns = 2 * (1 + LAYERS) * span
    return span, turns, turns + 2 * bands, turns + 2 * bands + 2 * rows


def put_weights(sizes, row, col, depth, trig, side):
    rows, _, own, bands = sizes
    span = side_rows(own, bands, rows)[0]

    def put(part, q, at, value):
        base = (part * (1 + LAYERS) + q) * span + at
        side[base : base + value.shape[0], :] = value

    north_len, east_len = rows * LANES, bands * LANES
    scale = 1.0 / (north_len * east_len)
    start = jnp.where(
        row == 0, 0, jnp.where(row == 1, rows // 2, row // 2 + HALF * rows * (row % 2))
    )

    def signed(index, length):
        return jnp.where(index < length // 2, index, index - length).astype(F32) / length

    def north_of(shape):
        index = start + rows * (col * own + lax.broadcasted_iota(jnp.int32, shape, 0))
        return signed(index, north_len)

    def weights(re, im, radius):
        damp = [None] + [jnp.exp(radius * (-2.0 * np.pi * depth[l])) for l in range(LAYERS)]
        return [(re, im) if d is None else (re * d, im * d) for d in damp]

    lane = lax.broadcasted_iota(jnp.int32, (own, LANES), 1)
    north = north_of((own, LANES))
    for band in range(bands):
        east = signed(band + bands * lane, east_len)
        re, im, radius = pole(north, east, trig)
        if band == 0:
            re2, im2, _ = pole(north, jnp.where(lane == HALF, 0.5, east), trig)
            re, im = 0.5 * (re + re2), 0.5 * (im + im2)
        for q, (wr, wi) in enumerate(weights(re * scale, im * scale, radius)):
            put(0, q, band * own, wr)
            put(1, q, band * own, wi)
            put(0, q, bands * own, jnp.zeros((bands, LANES), F32))
            put(1, q, bands * own, jnp.zeros((bands, LANES), F32))

    @pl.when((row == 0) & (col == 0))
    def _():
        band = lax.broadcasted_iota(jnp.int32, (bands, LANES), 0)
        lanes = lax.broadcasted_iota(jnp.int32, (bands, LANES), 1)
        east = signed(band + bands * lanes, east_len)
        flipped = jnp.where((band == 0) & (lanes == HALF), 0.5, east)
        pairs = []
        for one, other in ((0.0, 0.0), (-0.5, 0.5)):
            re, im, radius = pole(jnp.full_like(east, one), east, trig)
            re2, im2, _ = pole(jnp.full_like(east, other), flipped, trig)
            half = 0.5 * scale
            pairs.append(weights(half * (re + re2), half * (im + im2), radius))
        for q in range(1 + LAYERS):
            (r0, i0), (r1, i1) = pairs[0][q], pairs[1][q]
            put(0, q, bands * own, 0.5 * (r0 - r1))
            put(1, q, bands * own, 0.5 * (i0 - i1))
            for b in range(bands):
                put(0, q, b * own, 0.5 * (r0 + r1)[b : b + 1])
                put(1, q, b * own, 0.5 * (i0 + i1)[b : b + 1])


def turn_rows(side, turns_at, band, bands):
    cos, sin = turns_at + band, turns_at + bands + band
    return side[cos : cos + 1, :], side[sin : sin + 1, :]


def east_table(tables, index):
    span = 2 * LANES
    return tables[2 * index * span : (2 * index + 1) * span], tables[
        (2 * index + 1) * span : (2 * index + 2) * span
    ]


def east_forward(get, sizes, side, tables, work):
    rows, _, own, bands = sizes
    turns_at = side_rows(own, bands, rows)[1]
    for g in range(own // SUB):
        values = transform_list([get(m, g) for m in range(bands)], -1.0)
        for b in range(bands):
            cos, sin = turn_rows(side, turns_at, b, bands)
            re, im = values[b]
            at = b * own + g * SUB
            work[at : at + SUB, :LANES] = re * cos - im * sin
            work[at : at + SUB, LANES:] = re * sin + im * cos
            if g == 0:
                re, im = values[(bands - b) % bands]
                re, im = re[0:1], -im[0:1]
                at = bands * own + b
                work[at : at + 1, :LANES] = re * cos - im * sin
                work[at : at + 1, LANES:] = re * sin + im * cos
    return mul_table(work[...], *east_table(tables, 0))


def weigh(spectrum, q, sizes, side, into, first):
    rows, _, own, bands = sizes
    span = side_rows(own, bands, rows)[0]
    re, im = spectrum[:, :LANES], spectrum[:, LANES:]
    wr = side[q * span : (q + 1) * span, :]
    wi = side[(1 + LAYERS + q) * span : (2 + LAYERS + q) * span, :]
    out_re, out_im = re * wr - im * wi, re * wi + im * wr
    main = own * bands
    if first:
        into[:, :LANES] = out_re[:main]
        into[:, LANES:] = out_im[:main]
    else:
        into[:, :LANES] += out_re[:main]
        into[:, LANES:] += out_im[:main]
    for b in range(bands):
        into[b * own : b * own + 1, :LANES] += out_re[main + b : main + b + 1]
        into[b * own : b * own + 1, LANES:] += out_im[main + b : main + b + 1]


def east_inverse(spectrum, sizes, side, tables, work, store):
    rows, _, own, bands = sizes
    turns_at = side_rows(own, bands, rows)[1]
    work[...] = mul_table(spectrum[...], *east_table(tables, 1))
    for g in range(own // SUB):
        values = []
        for b in range(bands):
            at = b * own + g * SUB
            re, im = work[at : at + SUB, :LANES], work[at : at + SUB, LANES:]
            cos, sin = turn_rows(side, turns_at, b, bands)
            values.append((re * cos + im * sin, im * cos - re * sin))
        values = transform_list(values, 1.0)
        for b in range(bands):
            store(b, g, *values[b])


def store_pieces(out, width):
    per_band = LANES // width

    def store(band, g, re, im):
        for s in range(per_band):
            cut = slice(s * width, (s + 1) * width)
            piece = jnp.concatenate([re[:, cut], im[:, cut]], axis=1)
            out[band * per_band + s, g * SUB : (g + 1) * SUB] = piece

    return store


def model_rows(vector, sizes, side, coarse):
    rows, cols, own, bands = sizes
    own2 = 2 * own
    for i in range(rows):
        for j in range(cols):
            block = vector[i * cols + j]
            for layer in range(LAYERS):
                coarse[layer, 2 * i : 2 * i + 2, j * LANES : (j + 1) * LANES] = block[
                    2 * layer : 2 * layer + 2
                ]
    out = []
    _, _, hats_at, end = side_rows(own, bands, rows)
    high, low = split(side[hats_at:end, :])
    tiles = cols * SRC_COLS // LANES
    lane = lax.broadcasted_iota(jnp.int32, (own2, LANES), 1) // SRC_COLS
    for layer in range(LAYERS):
        mixed = table_mul(high, low, coarse[layer], TN)
        whole = []
        for tile in range(tiles):
            joined = None
            for place in range(LANES // SRC_COLS):
                j = tile * (LANES // SRC_COLS) + place
                summed = None
                for part in range(4):
                    piece = mixed[part * own2 : (part + 1) * own2, j * LANES : (j + 1) * LANES]
                    shift = ((place - part) * SRC_COLS) % LANES
                    if shift:
                        piece = pltpu.roll(piece, shift, 1)
                    summed = piece if summed is None else summed + piece
                joined = summed if joined is None else jnp.where(lane == place, summed, joined)
            whole.append(joined)
        out.append(whole[0] if tiles == 1 else jnp.concatenate(whole, axis=1))
    return out


def model_mix(vector, scale, sizes, side, tables, coarse, fine, work, mixed, first):
    rows, cols, own, bands = sizes
    depth = cols * SRC_COLS
    planes = jnp.concatenate(model_rows(vector, sizes, side, coarse), axis=0)
    high, low = split(planes if scale is None else planes * scale)
    for c in range(bands // 2):
        at = 8 * LANES + c * depth
        table = tables[at : at + depth, :]
        fine[:, 2 * LANES * c : 2 * LANES * (c + 1)] = dot(high, table, NN) + dot(low, table, NN)
    for layer in range(LAYERS):

        def get(m, g, base=2 * own * layer):
            at = base + g * SUB
            cut = slice(m * LANES, (m + 1) * LANES)
            return fine[at : at + SUB, cut], fine[at + own : at + own + SUB, cut]

        spectrum = east_forward(get, sizes, side, tables, work)
        weigh(spectrum, 1 + layer, sizes, side, mixed, first and layer == 0)


def sort_east(arrived, sizes, spec):
    rows, cols, own, bands = sizes
    left = lax.broadcasted_iota(jnp.int32, (SUB, LANES), 1) < HALF
    for j in range(cols):
        for i in range(0, rows, 2):
            for g in range(own // SUB):
                pair = []
                for source in (i * cols + j, (i + 1) * cols + j):
                    at = 1 + 2 * g
                    both = [arrived[source, at], arrived[source, at + 1]]
                    pair.append(jnp.concatenate(both, axis=0))
                cut = slice(i * HALF, (i + 2) * HALF)
                at = g * SUB
                spec[j, at : at + SUB, cut] = jnp.where(left, pair[0], pltpu.roll(pair[1], HALF, 1))
                at = own + g * SUB
                spec[j, at : at + SUB, cut] = jnp.where(left, pltpu.roll(pair[0], HALF, 1), pair[1])


def map_kernel(
    sizes, width, arrived, first, second, meta, scalars, tables, side, known, response, carry,
    coarse, fine, work, mixed, back, *spec,
):
    rows, cols, own, bands = sizes
    step = scalars[1:2, 0:1]
    me = lax.axis_index("row") * cols + lax.axis_index("col")
    carry[0] = step * first[me]
    carry[1] = second[me]
    carry[2] = jnp.broadcast_to(scalars[0:1], carry.shape[1:])
    ridge = meta[1:2, 0:1] * total(second[...] * second[...])
    carry[3] = jnp.broadcast_to(ridge, carry.shape[1:])
    if spec:
        sort_east(arrived, sizes, spec[0])
    spec = spec[0] if spec else arrived
    per = spec.shape[2] // LANES

    def get(m, g):
        cut = slice((m % per) * LANES, (m % per + 1) * LANES)
        at = g * SUB
        return spec[m // per, at : at + SUB, cut], spec[m // per, own + at : own + at + SUB, cut]

    spectrum = east_forward(get, sizes, side, tables, work)
    weigh(spectrum, 0, sizes, side, mixed, True)
    model_mix(first, step, sizes, side, tables, coarse, fine, work, mixed, False)
    east_inverse(mixed, sizes, side, tables, back, store_pieces(known, width))
    model_mix(second, None, sizes, side, tables, coarse, fine, work, mixed, True)
    east_inverse(mixed, sizes, side, tables, back, store_pieces(response, width))


def direction_kernel(rows, cols, meta, source, first, applied, second, measured, scalars):
    tiles = source.at[0, 0]
    row, col = lax.axis_index("row"), lax.axis_index("col")
    norm = total(first[...] * first[...])
    step = norm / total(first[...] * applied[...])
    residual = first[...] - step[None] * applied[...]
    norm_next = total(residual * residual)
    second[...] = residual + (norm_next / norm)[None] * first[...]
    scalars[0:1] = jnp.broadcast_to(norm_next, (1, LANES))
    scalars[1:2] = jnp.broadcast_to(step, (1, LANES))
    ints = [meta[2 + k, 0].astype(jnp.int32) for k in range(FOOTPRINT)] + [None, row, col]
    blocks = near_blocks(ints, second, rows, cols)
    squares = apply_forward(tiles, blocks, meta[0:1, :], None)
    measured[...] = jnp.broadcast_to(squares[None], measured.shape)


def last_step(measured, carry):
    squares = jnp.sum(measured[:, 0:1], axis=0)
    return carry[2, 0:1, 0:1] / (squares[:, 0:1] + carry[3, 0:1, 0:1])


def combine_kernel(measured, carry, known, response, out):
    out[...] = known[...] + last_step(measured, carry)[None] * response[...]


def finish_kernel(
    rows, cols, arrived, measured, carry, turns, packed, plain, coefficients, out, mixed, waves
):
    solved = carry[0] + last_step(measured, carry) * carry[1]
    for p in range(solved.shape[0]):
        coefficients[:, p * LANES : (p + 1) * LANES] = solved[p : p + 1]
    own = arrived.shape[1]
    width = out.shape[0]
    near = rows // 2
    for i in range(rows):
        for j in range(cols):
            at = i * HALF + j * own
            mixed[at : at + own, :] = arrived[i * cols + j]
    starts = north_starts(rows)
    for n, start in enumerate(starts):
        if n == 0:
            both = mul_table(mixed[0:HALF], packed[0], packed[1], TN)
        elif n == 1:
            both = mul_table(mixed[HALF : 2 * HALF], plain[0, :HALF], plain[1, :HALF], TN)
        else:
            at = 2 * start * HALF
            both = mul_table(mixed[at : at + 2 * HALF], plain[0], plain[1], TN)
        top, bottom = both[:width], both[width:]
        waves[n, :, :LANES] = top[:, :LANES] - bottom[:, LANES:]
        waves[n, :, LANES:] = top[:, LANES:] + bottom[:, :LANES]
    for at in range(0, width, SUB):
        parts = [[None, None] for _ in range(near)]
        for n, start in enumerate(starts):
            re = waves[n, at : at + SUB, :LANES]
            im = waves[n, at : at + SUB, LANES:]
            for i in range(near):
                if start == 0:
                    term = re
                else:
                    term = re * turns[0, n, i : i + 1] + im * turns[1, n, i : i + 1]
                sums = parts[i]
                sums[start % 2] = term if sums[start % 2] is None else sums[start % 2] + term
        for i in range(near):
            even, odd = parts[i]
            out[at : at + SUB, i * LANES : (i + 1) * LANES] = even + odd
            out[at : at + SUB, (near + i) * LANES : (near + i + 1) * LANES] = even - odd


def shape(*dims):
    return jax.ShapeDtypeStruct(dims, F32)


def scratch(*dims):
    return pltpu.VMEM(dims, F32)


def call(kernel, outs, ins, work=(), limit=SMALL):
    return pl.pallas_call(
        kernel,
        out_shape=outs,
        in_specs=[spec for spec, _ in ins],
        out_specs=jax.tree.map(lambda _: VMEM, outs),
        scratch_shapes=list(work),
        compiler_params=pltpu.CompilerParams(vmem_limit_bytes=limit),
    )(*[value for _, value in ins])


def exchange(pieces):
    return lax.all_to_all(pieces, BOTH, 0, 0, tiled=True)


def on_device(
    kernel_tiles, footprints, counts, readings, damping, layer_depth, inclinations, declinations,
    resid_grid,
):
    rows, cols = lax.axis_size("row"), lax.axis_size("col")
    devices = rows * cols
    slots, sources = kernel_tiles.shape[3:]
    parts = sources // LANES
    tile_east = resid_grid.shape[0]
    east = cols * tile_east
    bands = east // LANES
    own = HALF // cols
    width = east // devices
    sizes = (rows, cols, own, bands)

    turns = north_turns(rows)
    forward_tables, inverse_tables = north_forward_tables(), north_inverse_tables()
    tables, east_turns = east_tables(east)
    hats = north_hat_table(rows, cols)

    joined = 2 * width == LANES
    everywhere = shape(devices, parts, LANES)
    beside = shape(devices, 1 + own // 4, 4, LANES) if joined else everywhere
    pieces = shape(devices, own, 2 * width)

    def apart(value):
        return HBM, pltpu.with_memory_space_constraint(value, pltpu.HBM)

    tile_scratch = scratch(FOOTPRINT, slots, sources)
    tile_sems = pltpu.SemaphoreType.DMA((FOOTPRINT,))
    codes_scratch = pltpu.SMEM((1, FOOTPRINT), jnp.int32)

    nine = shape(FOOTPRINT, parts, LANES)
    sums, kept, side, meta = call(
        functools.partial(start_kernel, sizes),
        (
            shape(rows, SENT + width // 4, parts, LANES),
            nine,
            shape(side_rows(own, bands, rows)[-1], LANES),
            shape(2 + FOOTPRINT, LANES),
        ),
        [apart(footprints), (VMEM, counts), (VMEM, damping.reshape(1, 1))]
        + [
            apart(value)
            for value in (
                readings, layer_depth, inclinations, declinations,
                jnp.asarray(east_turns), jnp.asarray(hats), resid_grid, kernel_tiles,
            )
        ],
        [
            codes_scratch,
            pltpu.SMEM((LAYERS,), F32),
            pltpu.SMEM((2, 2), F32),
            scratch(1, slots),
            scratch(*resid_grid.shape),
            tile_scratch,
            scratch(slots, LANES),
            tile_sems,
            pltpu.SemaphoreType.DMA((8,)),
        ],
    )
    arrived = lax.all_to_all(sums, "row", 0, 0, tiled=True)
    summed, column_sums = call(
        functools.partial(column_kernel, rows, cols),
        (shape(cols, SENT, parts, LANES), nine),
        [(VMEM, arrived), (VMEM, kept)],
    )
    summed = lax.all_to_all(summed, "col", 0, 0, tiled=True)

    sums, near, *spectrum = call(
        functools.partial(normal_kernel, rows, cols),
        (beside, nine) if joined else (everywhere, nine, pieces),
        [
            (VMEM, meta),
            (VMEM, kernel_tiles),
            (VMEM, summed),
            (VMEM, column_sums),
            (VMEM, arrived),
            (VMEM, turns),
            (VMEM, forward_tables[0]),
            (VMEM, forward_tables[1]),
        ],
        [scratch(slots, LANES), scratch(rows, width, LANES)],
    )
    sums = exchange(sums)
    applied_all, right_side = call(
        functools.partial(share_kernel, rows, cols),
        (everywhere, everywhere),
        [(VMEM, sums), (VMEM, near)],
    )
    applied = exchange(applied_all)
    if joined:
        spectrum, sorted_work = sums, [scratch(cols, 2 * own, tile_east)]
    else:
        spectrum, sorted_work = exchange(spectrum[0]), []
        spectrum = spectrum.reshape(rows, cols, own, 2, width).transpose(1, 3, 2, 0, 4)
        spectrum = spectrum.reshape(cols, 2 * own, tile_east)

    second, measured, scalars = call(
        functools.partial(direction_kernel, rows, cols),
        (everywhere, everywhere, shape(2, LANES)),
        [(VMEM, meta), (VMEM, kernel_tiles), (VMEM, right_side), (VMEM, applied)],
    )
    work = [
        scratch(LAYERS, 2 * rows, cols * LANES),
        scratch(LAYERS * 2 * own, east),
        scratch((own + 1) * bands, 2 * LANES),
        scratch(own * bands, 2 * LANES),
        scratch(own * bands, 2 * LANES),
    ]
    known, response, carry = call(
        functools.partial(map_kernel, sizes, width),
        (pieces, pieces, shape(4, parts, LANES)),
        [
            (VMEM, spectrum),
            (VMEM, right_side),
            (VMEM, second),
            (VMEM, meta),
            (VMEM, scalars),
            (VMEM, tables),
            (VMEM, side),
        ],
        work + sorted_work,
    )
    measured = exchange(measured)
    outgoing = call(
        combine_kernel,
        pieces,
        [(VMEM, measured), (VMEM, carry), (VMEM, known), (VMEM, response)],
    )
    coefficients, rtp_map = call(
        functools.partial(finish_kernel, rows, cols),
        (shape(1, sources), shape(width, rows * LANES)),
        [
            (VMEM, exchange(outgoing)),
            (VMEM, measured),
            (VMEM, carry),
            (VMEM, turns),
            (VMEM, inverse_tables[0]),
            (VMEM, inverse_tables[1]),
        ],
        [scratch(rows * HALF, 2 * width), scratch(rows // 2 + 1, width, 2 * LANES)],
    )
    return coefficients.reshape(1, 1, sources), rtp_map


def solution(mesh):
    in_specs = (
        P("row", "col", None, None, None),
        P("row", "col", None),
        P("row", "col"),
        P("row", "col", None),
        P(),
        P(),
        P(),
        P(),
        P("col", "row"),
    )
    out_specs = (P("row", "col", None), P(("row", "col"), None))
    return jax.shard_map(
        on_device, mesh=mesh, in_specs=in_specs, out_specs=out_specs, check_vma=False
    )
```

```python
import functools

import jax
import jax.numpy as jnp
import ml_dtypes
import numpy as np
from jax import lax
from jax.experimental import pallas as pl
from jax.experimental.pallas import tpu as pltpu
from jax.sharding import PartitionSpec as P

SRC_ROWS = 8
SRC_COLS = 32
LAYERS = 2
REFINE = 16
FOOTPRINT = 9
LANES = 128
SUB = 8
HALF = 64
BOTH = ("row", "col")
COUNT, ROW, COL = 9, 10, 11
SENT = 6
SMALL_AT = 2 + FOOTPRINT
MIB = 1024 * 1024
SMALL, LARGE = 24 * MIB, 62 * MIB
F32 = jnp.float32
BF16 = jnp.bfloat16

VMEM = pl.BlockSpec(memory_space=pltpu.VMEM)
SMEM = pl.BlockSpec(memory_space=pltpu.SMEM)
HBM = pl.BlockSpec(memory_space=pltpu.HBM)
NN = (((1,), (0,)), ((), ()))
NT = (((1,), (1,)), ((), ()))
TN = (((0,), (0,)), ((), ()))


def split_table(table):
    high = table.astype(ml_dtypes.bfloat16)
    low = (table - high.astype(np.float64)).astype(ml_dtypes.bfloat16)
    return np.stack([high, low])


def group_start(group, rows):
    if group == 0:
        return 0
    if group == 1:
        return rows // 2
    return group // 2 + HALF * rows * (group % 2)


def unit_turn(product, period):
    angle = 2.0 * np.pi * (product % period) / period
    return np.cos(angle), np.sin(angle)


def north_starts(rows):
    return [0, rows // 2] + list(range(1, rows // 2))


def north_turns(rows):
    north = rows * LANES
    starts = np.array(north_starts(rows))
    cos, sin = unit_turn(starts[:, None] * np.arange(north // 2)[None, :], north)
    turns = np.stack([cos, -sin]).reshape(2, len(starts), rows // 2, LANES)
    return turns.astype(np.float32)


def north_forward_tables():
    cos, sin = unit_turn(np.outer(np.arange(LANES), np.arange(LANES)), LANES)
    plain = np.block([[cos, sin], [-sin, cos]])
    packed = np.concatenate([cos[:HALF], -sin[:HALF]], 0)
    packed[HALF] = 1.0 - 2.0 * (np.arange(LANES) % 2)
    return split_table(packed), split_table(plain)


def north_inverse_tables():
    cos, sin = unit_turn(np.outer(np.arange(LANES), np.arange(LANES)), LANES)
    plain = 2.0 * np.concatenate([cos, sin], 1)
    packed = plain[:HALF].copy()
    packed[0, :LANES] = 1.0
    packed[0, LANES:] = 2.0 * (np.arange(LANES) % 2) - 1.0
    return split_table(packed), split_table(plain)


def east_tables(east):
    bands = east // LANES
    cos, sin = unit_turn(np.outer(np.arange(LANES), np.arange(LANES)), LANES)
    forward = np.block([[cos, -sin], [sin, cos]])
    inverse = np.block([[cos, sin], [-sin, cos]])
    turn_cos, turn_sin = unit_turn(np.outer(np.arange(bands), np.arange(LANES)), east)
    turns = np.concatenate([turn_cos, -turn_sin]).astype(np.float32)
    up_east = hat_table(east, east // REFINE).reshape(-1, 2 * LANES, east // REFINE)
    up_east = up_east.transpose(0, 2, 1).reshape(-1, 2 * LANES).astype(ml_dtypes.bfloat16)
    tables = [split_table(forward), split_table(inverse)]
    return np.concatenate([t.reshape(-1, 2 * LANES) for t in tables] + [up_east]), turns


def hat_table(fine_count, coarse_count):
    offset = (np.arange(fine_count)[:, None] + 0.5) / REFINE - 0.5 - np.arange(coarse_count)[None, :]
    return np.maximum(0.0, 1.0 - np.abs(offset))


def north_hat_table(rows, cols):
    north = rows * LANES
    coarse = rows * SRC_ROWS
    own = HALF // cols
    spectrum = np.fft.fft(hat_table(north, coarse), axis=0)
    out = np.zeros((rows, cols, 2 * own, coarse))
    for group in range(rows):
        for col in range(cols):
            index = group_start(group, rows) + rows * (col * own + np.arange(own))
            part = spectrum[index % north]
            out[group, col, :own] = part.real
            out[group, col, own:] = part.imag
    out[0, 0, own] = spectrum[north // 2].real
    out = out.reshape(rows * cols, 2 * own, 2 * rows, 4).transpose(0, 2, 3, 1)
    out = out.reshape(rows * cols, 2 * rows, 8 * own)
    return np.pad(out, ((0, 0), (0, 0), (0, LANES - 8 * own))).astype(np.float32)


def split(x):
    high = x.astype(BF16)
    return high, (x - high.astype(F32)).astype(BF16)


def dot(a, b, dims):
    return lax.dot_general(a, b, dims, preferred_element_type=F32)


def mul_table(x, high, low, dims=NN):
    x_high, x_low = split(x)
    return dot(x_high, high, dims) + (dot(x_low, high, dims) + dot(x_high, low, dims))


def table_mul(high, low, x, dims=NN):
    x_high, x_low = split(x)
    return dot(high, x_high, dims) + (dot(high, x_low, dims) + dot(low, x_high, dims))


def transform_list(values, sign):
    count = len(values)
    if count == 1:
        return values
    even = transform_list(values[0::2], sign)
    odd = transform_list(values[1::2], sign)
    first, second = [], []
    for k in range(count // 2):
        re, im = odd[k]
        if k == 0:
            turned = (re, im)
        elif 4 * k == count:
            turned = (im, -re) if sign < 0 else (-im, re)
        else:
            cos = float(np.cos(2.0 * np.pi * k / count))
            sin = sign * float(np.sin(2.0 * np.pi * k / count))
            if 8 * k == count or 8 * k == 3 * count:
                if cos * sin > 0:
                    turned = (cos * (re - im), cos * (re + im))
                else:
                    turned = (cos * (re + im), cos * (im - re))
            else:
                turned = (re * cos - im * sin, re * sin + im * cos)
        first.append((even[k][0] + turned[0], even[k][1] + turned[1]))
        second.append((even[k][0] - turned[0], even[k][1] - turned[1]))
    return first + second


def total(x):
    lanes = jnp.sum(jnp.sum(x, axis=0), axis=0, keepdims=True)
    return jnp.sum(lanes, axis=1, keepdims=True)


def neighbour(k, ints, rows, cols):
    code = ints[k]
    near_row = ints[ROW] + code // 3 - 1
    near_col = ints[COL] + code % 3 - 1
    inside = (near_row >= 0) & (near_row < rows) & (near_col >= 0) & (near_col < cols)
    device = jnp.clip(near_row * cols + near_col, 0, rows * cols - 1)
    return device, inside


def near_blocks(ints, vector, rows, cols):
    blocks = []
    for k in range(FOOTPRINT):
        device, inside = neighbour(k, ints, rows, cols)
        blocks.append(vector[device] * jnp.where(inside, 1.0, 0.0))
    return blocks


def apply_forward(tiles, blocks, count, out):
    slots, width = tiles.shape[1:]
    parts = width // LANES
    spread = [
        [jnp.broadcast_to(block[p : p + 1], (SUB, LANES)) for p in range(parts)] for block in blocks
    ]

    def step(t, squares):
        at = pl.multiple_of(t * SUB, SUB)
        sums = [None] * parts
        for k in range(FOOTPRINT):
            for p in range(parts):
                tile = tiles[k, pl.ds(at, SUB), p * LANES : (p + 1) * LANES]
                term = tile * spread[k][p]
                sums[p] = term if sums[p] is None else sums[p] + term
        acc = functools.reduce(jnp.add, sums)
        slot = at + lax.broadcasted_iota(jnp.int32, (SUB, LANES), 0)
        value = jnp.where(slot.astype(F32) < count, jnp.sum(acc, axis=1, keepdims=True), 0.0)
        if out is not None:
            out[pl.ds(at, SUB), :] = value
        return squares + value * value

    zero = jnp.zeros((SUB, LANES), F32)
    squares = lax.fori_loop(0, slots // SUB, step, zero, unroll=8)
    return jnp.sum(squares, axis=0, keepdims=True)


def apply_adjoint(tile, values):
    slots, width = tile.shape
    parts = width // LANES
    sums = [[None, None] for _ in range(parts)]
    for t in range(slots // SUB):
        rows = slice(t * SUB, (t + 1) * SUB)
        weight = values[rows, :]
        for p in range(parts):
            term = tile[rows, p * LANES : (p + 1) * LANES] * weight
            sums[p][t % 2] = term if t < 2 else sums[p][t % 2] + term
    return jnp.concatenate([jnp.sum(a + b, axis=0, keepdims=True) for a, b in sums], axis=0)


def tile_copies(source, tiles, sems):
    copies = [
        pltpu.make_async_copy(source.at[0, 0, k], tiles.at[k], sems.at[k]) for k in range(FOOTPRINT)
    ]
    for copy in copies:
        copy.start()
    return copies


def start_kernel(
    sizes, codes, counts, damping, readings, depth, inclinations, declinations, turns, hats, resid,
    source, out, kept, side, meta, codes_in, depth_in, angles, read, map_rows, tiles, values, sems, more,
):
    rows, cols, own, bands = sizes
    row, col = lax.axis_index("row"), lax.axis_index("col")
    _, turns_at, hats_at, end = side_rows(own, bands, rows)
    pairs = [
        (codes.at[0], codes_in),
        (depth, depth_in),
        (inclinations, angles.at[0]),
        (declinations, angles.at[1]),
        (readings.at[0], read),
        (turns, side.at[turns_at:hats_at]),
        (hats.at[row * cols + col], side.at[hats_at:end]),
        (resid, map_rows),
    ]
    first = [pltpu.make_async_copy(a, b, more.at[n]) for n, (a, b) in enumerate(pairs)]
    for copy in first:
        copy.start()
    copies = tile_copies(source, tiles, sems)
    for copy in first:
        copy.wait()
    width = map_rows.shape[0] // rows
    for i in range(rows):
        for g in range(width // 4):
            at = i * width + 4 * g
            out[i, SENT + g] = map_rows[at : at + 4]
    ints = [codes_in[0, k] for k in range(FOOTPRINT)] + [None, row, col]
    meta[0:1, :] = jnp.broadcast_to(counts[...].astype(F32), (1, LANES))
    for k in range(FOOTPRINT):
        meta[2 + k : 3 + k, :] = jnp.full((1, LANES), codes_in[0, k].astype(F32), F32)
    meta[1:2, :] = jnp.broadcast_to(damping[...], (1, LANES))
    slots = read.shape[1]
    slot = lax.broadcasted_iota(jnp.int32, (1, slots), 1)
    live = jnp.where(slot < counts[...], read[...], 0.0)
    for t in range(slots // LANES):
        square = jnp.broadcast_to(live[:, t * LANES : (t + 1) * LANES], (LANES, LANES))
        values[t * LANES : (t + 1) * LANES, :] = square.T
    trig = []
    for m in range(2):
        up = jnp.full((1, LANES), angles[0, m], F32)
        turn = jnp.full((1, LANES), angles[1, m], F32)
        flat = jnp.cos(up)
        trig += [jnp.sin(up), flat * jnp.cos(turn), flat * jnp.sin(turn)]
    small = trig + [jnp.full((1, LANES), depth_in[l], F32) for l in range(LAYERS)]
    for n, value in enumerate(small):
        meta[SMALL_AT + n : SMALL_AT + n + 1, :] = value
    for k in range(FOOTPRINT):
        copies[k].wait()
        kept[ints[k]] = apply_adjoint(tiles.at[k], values)
    fill_pieces(out, kept, row)


def fill_pieces(out, kept, here):
    for peer in range(out.shape[0]):
        low = jnp.maximum(peer - here - 1, -1)
        for slot in range(2):
            at = 3 * (jnp.clip(low + slot, -1, 1) + 1)
            out[peer, 3 * slot : 3 * slot + 3] = kept[pl.ds(at, 3)]


def arrived_part(arrived, kept, here, offset, which, other):
    if offset == 0:
        return kept[3 * (which + 1) + other]
    peer, count = here - offset, arrived.shape[0]
    slot = which - max(offset - 1, -1)
    part = arrived[jnp.clip(peer, 0, count - 1), 3 * slot + other]
    return jnp.where((peer >= 0) & (peer < count), part, 0.0)


def place_rows(out, get):
    for d in range(out.shape[0]):
        for g in range(out.shape[1] - 1):
            out[d, 1 + g] = get(d, g)


def column_kernel(rows, cols, arrived, kept, out, sums):
    row, col = lax.axis_index("row"), lax.axis_index("col")
    for north in (-1, 0, 1):
        for east in (-1, 0, 1):
            parts = [
                arrived_part(arrived, kept, row, a - north, a, east + 1) for a in (-1, 0, 1)
            ]
            target, column = row + north, col + east
            inside = (target >= 0) & (target < rows) & (column >= 0) & (column < cols)
            sums[3 * (east + 1) + north + 1] = jnp.where(inside, parts[0] + parts[1] + parts[2], 0.0)
    fill_pieces(out, sums, col)


def around(rows, cols):
    row, col = lax.axis_index("row"), lax.axis_index("col")
    for code in range(FOOTPRINT):
        north, east = row + code // 3 - 1, col + code % 3 - 1
        inside = (north >= 0) & (north < rows) & (east >= 0) & (east < cols)
        yield code, jnp.clip(north * cols + east, 0, rows * cols - 1), inside


def share_kernel(rows, cols, arrived, near, everywhere, right):
    get = (lambda d: arrived[d, 0]) if len(arrived.shape) == 4 else (lambda d: arrived[d])
    for device in range(rows * cols):
        right[device] = get(device)
    block = None
    for code, device, inside in around(rows, cols):
        part = jnp.where(inside, get(device), 0.0)
        block = part if block is None else block + part

        @pl.when(inside)
        def _():
            right[device] = near[code]

    everywhere[...] = jnp.broadcast_to(block[None], everywhere.shape)


def normal_kernel(
    rows, cols, meta, source, summed, sums, arrived, turns, packed, plain, out, near, *refs
):
    (*apart, values, planes) = refs
    tiles = source.at[0, 0]
    row, col = lax.axis_index("row"), lax.axis_index("col")
    ints = [meta[2 + k, 0].astype(jnp.int32) for k in range(FOOTPRINT)] + [None, row, col]
    for code in range(FOOTPRINT):
        north, east = code // 3 - 1, code % 3 - 1
        parts = [arrived_part(summed, sums, col, b - east, b, north + 1) for b in (-1, 0, 1)]
        near[code] = parts[0] + parts[1] + parts[2]
    blocks = [near[ints[k]] for k in range(FOOTPRINT)]
    me = row * cols + col
    own = near[FOOTPRINT // 2]
    for device in range(rows * cols):
        if apart:
            out[device] = own
        else:
            out[device, 0] = own

    def store(device, piece):
        if apart:
            apart[0][device] = piece
        else:
            for g in range(out.shape[1] - 1):
                out[device, 1 + g] = piece[4 * g : 4 * g + 4]

    north_transform(rows, cols, arrived, turns, (packed, plain), planes, store)
    apply_forward(tiles, blocks, meta[0:1, :], values)
    for k in range(FOOTPRINT):
        device, inside = neighbour(k, ints, rows, cols)
        block = apply_adjoint(tiles.at[k], values)
        block = block + jnp.where(device == me, meta[1:2, :], 0.0) * own

        @pl.when(inside)
        def _():
            if apart:
                out[device] = block
            else:
                out[device, 0] = block


def north_transform(rows, cols, arrived, turns, tables, planes, store):
    own = HALF // cols
    near, count = rows // 2, planes.shape[1]
    for i in range(rows):
        for g in range(count // 4):
            planes[i, 4 * g : 4 * g + 4, :] = arrived[i, SENT + g]
    for i in range(near):
        one, other = planes[i], planes[i + near]
        planes[i] = one + other
        planes[i + near] = one - other
    packed, plain = tables
    for n, start in enumerate(north_starts(rows)):
        base = near * (start % 2)
        re, im = None, None
        for i in range(near):
            plane = planes[base + i]
            a = plane if start == 0 else plane * turns[0, n, i : i + 1]
            re = a if re is None else re + a
            if start:
                a = plane * turns[1, n, i : i + 1]
                im = a if im is None else im + a
        if start == 0:
            result = table_mul(packed[0], packed[1], re, NT)
        else:
            result = table_mul(plain[0], plain[1], jnp.concatenate([re, im], axis=1), NT)
        imag_at = result.shape[0] // 2
        groups = [n] if n < 2 else [2 * start, 2 * start + 1]
        for h, group in enumerate(groups):
            for j in range(cols):
                at = h * HALF + j * own
                real, imag = result[at : at + own], result[imag_at + at : imag_at + at + own]
                store(group * cols + j, jnp.concatenate([real, imag], axis=1))


def pole(north, east, trig):
    square = north * north + east * east
    inverse = jnp.where(square > 0.0, lax.rsqrt(jnp.where(square > 0.0, square, 1.0)), 0.0)
    a0 = (trig[1] * north + trig[2] * east) * inverse
    a1 = (trig[4] * north + trig[5] * east) * inverse
    v0, v1 = trig[0], trig[3]
    scale = 1.0 / ((v0 * v0 + a0 * a0) * (v1 * v1 + a1 * a1))
    return (v0 * v1 - a0 * a1) * scale, -(v0 * a1 + v1 * a0) * scale, square * inverse


def side_rows(own, bands, rows):
    span = (own + 1) * bands
    turns = 2 * (1 + LAYERS) * span
    return span, turns, turns + 2 * bands, turns + 2 * bands + 2 * rows


def put_weights(sizes, row, col, depth, trig, side):
    rows, _, own, bands = sizes
    span = side_rows(own, bands, rows)[0]

    def put(part, q, at, value):
        base = (part * (1 + LAYERS) + q) * span + at
        side[base : base + value.shape[0], :] = value

    north_len, east_len = rows * LANES, bands * LANES
    scale = 1.0 / (north_len * east_len)
    start = jnp.where(
        row == 0, 0, jnp.where(row == 1, rows // 2, row // 2 + HALF * rows * (row % 2))
    )

    def signed(index, length):
        return jnp.where(index < length // 2, index, index - length).astype(F32) / length

    def north_of(shape):
        index = start + rows * (col * own + lax.broadcasted_iota(jnp.int32, shape, 0))
        return signed(index, north_len)

    def weights(re, im, radius):
        damp = [None] + [jnp.exp(radius * (-2.0 * np.pi * depth[l])) for l in range(LAYERS)]
        return [(re, im) if d is None else (re * d, im * d) for d in damp]

    lane = lax.broadcasted_iota(jnp.int32, (own, LANES), 1)
    north = north_of((own, LANES))
    for band in range(bands):
        east = signed(band + bands * lane, east_len)
        re, im, radius = pole(north, east, trig)
        if band == 0:
            re2, im2, _ = pole(north, jnp.where(lane == HALF, 0.5, east), trig)
            re, im = 0.5 * (re + re2), 0.5 * (im + im2)
        for q, (wr, wi) in enumerate(weights(re * scale, im * scale, radius)):
            put(0, q, band * own, wr)
            put(1, q, band * own, wi)
            put(0, q, bands * own, jnp.zeros((bands, LANES), F32))
            put(1, q, bands * own, jnp.zeros((bands, LANES), F32))

    @pl.when((row == 0) & (col == 0))
    def _():
        band = lax.broadcasted_iota(jnp.int32, (bands, LANES), 0)
        lanes = lax.broadcasted_iota(jnp.int32, (bands, LANES), 1)
        east = signed(band + bands * lanes, east_len)
        flipped = jnp.where((band == 0) & (lanes == HALF), 0.5, east)
        pairs = []
        for one, other in ((0.0, 0.0), (-0.5, 0.5)):
            re, im, radius = pole(jnp.full_like(east, one), east, trig)
            re2, im2, _ = pole(jnp.full_like(east, other), flipped, trig)
            half = 0.5 * scale
            pairs.append(weights(half * (re + re2), half * (im + im2), radius))
        for q in range(1 + LAYERS):
            (r0, i0), (r1, i1) = pairs[0][q], pairs[1][q]
            put(0, q, bands * own, 0.5 * (r0 - r1))
            put(1, q, bands * own, 0.5 * (i0 - i1))
            for b in range(bands):
                put(0, q, b * own, 0.5 * (r0 + r1)[b : b + 1])
                put(1, q, b * own, 0.5 * (i0 + i1)[b : b + 1])


def turn_rows(side, turns_at, band, bands):
    cos, sin = turns_at + band, turns_at + bands + band
    return side[cos : cos + 1, :], side[sin : sin + 1, :]


def east_table(tables, index):
    span = 2 * LANES
    return tables[2 * index * span : (2 * index + 1) * span], tables[
        (2 * index + 1) * span : (2 * index + 2) * span
    ]


def east_forward(get, sizes, side, tables, work):
    rows, _, own, bands = sizes
    turns_at = side_rows(own, bands, rows)[1]
    for g in range(own // SUB):
        values = transform_list([get(m, g) for m in range(bands)], -1.0)
        for b in range(bands):
            cos, sin = turn_rows(side, turns_at, b, bands)
            re, im = values[b]
            at = b * own + g * SUB
            work[at : at + SUB, :LANES] = re * cos - im * sin
            work[at : at + SUB, LANES:] = re * sin + im * cos
            if g == 0:
                re, im = values[(bands - b) % bands]
                re, im = re[0:1], -im[0:1]
                at = bands * own + b
                work[at : at + 1, :LANES] = re * cos - im * sin
                work[at : at + 1, LANES:] = re * sin + im * cos
    return mul_table(work[...], *east_table(tables, 0))


def weigh(spectrum, q, sizes, side, into, first):
    rows, _, own, bands = sizes
    span = side_rows(own, bands, rows)[0]
    re, im = spectrum[:, :LANES], spectrum[:, LANES:]
    wr = side[q * span : (q + 1) * span, :]
    wi = side[(1 + LAYERS + q) * span : (2 + LAYERS + q) * span, :]
    out_re, out_im = re * wr - im * wi, re * wi + im * wr
    main = own * bands
    if first:
        into[:, :LANES] = out_re[:main]
        into[:, LANES:] = out_im[:main]
    else:
        into[:, :LANES] += out_re[:main]
        into[:, LANES:] += out_im[:main]
    for b in range(bands):
        into[b * own : b * own + 1, :LANES] += out_re[main + b : main + b + 1]
        into[b * own : b * own + 1, LANES:] += out_im[main + b : main + b + 1]


def east_inverse(spectrum, sizes, side, tables, work, store):
    rows, _, own, bands = sizes
    turns_at = side_rows(own, bands, rows)[1]
    work[...] = mul_table(spectrum[...], *east_table(tables, 1))
    for g in range(own // SUB):
        values = []
        for b in range(bands):
            at = b * own + g * SUB
            re, im = work[at : at + SUB, :LANES], work[at : at + SUB, LANES:]
            cos, sin = turn_rows(side, turns_at, b, bands)
            values.append((re * cos + im * sin, im * cos - re * sin))
        values = transform_list(values, 1.0)
        for b in range(bands):
            store(b, g, *values[b])


def store_pieces(out, width):
    per_band = LANES // width

    def store(band, g, re, im):
        for s in range(per_band):
            cut = slice(s * width, (s + 1) * width)
            piece = jnp.concatenate([re[:, cut], im[:, cut]], axis=1)
            out[band * per_band + s, g * SUB : (g + 1) * SUB] = piece

    return store


def model_rows(vector, sizes, side, coarse):
    rows, cols, own, bands = sizes
    own2 = 2 * own
    for i in range(rows):
        for j in range(cols):
            block = vector[i * cols + j]
            for layer in range(LAYERS):
                coarse[layer, 2 * i : 2 * i + 2, j * LANES : (j + 1) * LANES] = block[
                    2 * layer : 2 * layer + 2
                ]
    out = []
    _, _, hats_at, end = side_rows(own, bands, rows)
    high, low = split(side[hats_at:end, :])
    tiles = cols * SRC_COLS // LANES
    lane = lax.broadcasted_iota(jnp.int32, (own2, LANES), 1) // SRC_COLS
    for layer in range(LAYERS):
        mixed = table_mul(high, low, coarse[layer], TN)
        whole = []
        for tile in range(tiles):
            joined = None
            for place in range(LANES // SRC_COLS):
                j = tile * (LANES // SRC_COLS) + place
                summed = None
                for part in range(4):
                    piece = mixed[part * own2 : (part + 1) * own2, j * LANES : (j + 1) * LANES]
                    shift = ((place - part) * SRC_COLS) % LANES
                    if shift:
                        piece = pltpu.roll(piece, shift, 1)
                    summed = piece if summed is None else summed + piece
                joined = summed if joined is None else jnp.where(lane == place, summed, joined)
            whole.append(joined)
        out.append(whole[0] if tiles == 1 else jnp.concatenate(whole, axis=1))
    return out


def model_mix(vector, scale, sizes, side, weights, tables, coarse, fine, work, mixed, first):
    rows, cols, own, bands = sizes
    depth = cols * SRC_COLS
    planes = jnp.concatenate(model_rows(vector, sizes, side, coarse), axis=0)
    high, low = split(planes if scale is None else planes * scale)
    for c in range(bands // 2):
        at = 8 * LANES + c * depth
        table = tables[at : at + depth, :]
        fine[:, 2 * LANES * c : 2 * LANES * (c + 1)] = dot(high, table, NN) + dot(low, table, NN)
    for layer in range(LAYERS):

        def get(m, g, base=2 * own * layer):
            at = base + g * SUB
            cut = slice(m * LANES, (m + 1) * LANES)
            return fine[at : at + SUB, cut], fine[at + own : at + own + SUB, cut]

        spectrum = east_forward(get, sizes, side, tables, work)
        weigh(spectrum, 1 + layer, sizes, weights, mixed, first and layer == 0)


def sort_east(arrived, sizes, spec):
    rows, cols, own, bands = sizes
    left = lax.broadcasted_iota(jnp.int32, (SUB, LANES), 1) < HALF
    for j in range(cols):
        for i in range(0, rows, 2):
            for g in range(own // SUB):
                pair = []
                for source in (i * cols + j, (i + 1) * cols + j):
                    at = 1 + 2 * g
                    both = [arrived[source, at], arrived[source, at + 1]]
                    pair.append(jnp.concatenate(both, axis=0))
                cut = slice(i * HALF, (i + 2) * HALF)
                at = g * SUB
                spec[j, at : at + SUB, cut] = jnp.where(left, pair[0], pltpu.roll(pair[1], HALF, 1))
                at = own + g * SUB
                spec[j, at : at + SUB, cut] = jnp.where(left, pltpu.roll(pair[0], HALF, 1), pair[1])


def map_kernel(
    sizes, width, arrived, first, second, meta, scalars, tables, side, known, response, carry,
    weights, coarse, fine, work, mixed, back, *spec,
):
    rows, cols, own, bands = sizes
    small = [meta[SMALL_AT + n : SMALL_AT + n + 1, :] for n in range(6 + LAYERS)]
    put_weights(sizes, lax.axis_index("row"), lax.axis_index("col"), small[6:], small[:6], weights)
    step = scalars[1:2, 0:1]
    me = lax.axis_index("row") * cols + lax.axis_index("col")
    carry[0] = step * first[me]
    carry[1] = second[me]
    carry[2] = jnp.broadcast_to(scalars[0:1], carry.shape[1:])
    ridge = meta[1:2, 0:1] * total(second[...] * second[...])
    carry[3] = jnp.broadcast_to(ridge, carry.shape[1:])
    if spec:
        sort_east(arrived, sizes, spec[0])
    spec = spec[0] if spec else arrived
    per = spec.shape[2] // LANES

    def get(m, g):
        cut = slice((m % per) * LANES, (m % per + 1) * LANES)
        at = g * SUB
        return spec[m // per, at : at + SUB, cut], spec[m // per, own + at : own + at + SUB, cut]

    spectrum = east_forward(get, sizes, side, tables, work)
    weigh(spectrum, 0, sizes, weights, mixed, True)
    model_mix(first, step, sizes, side, weights, tables, coarse, fine, work, mixed, False)
    east_inverse(mixed, sizes, side, tables, back, store_pieces(known, width))
    model_mix(second, None, sizes, side, weights, tables, coarse, fine, work, mixed, True)
    east_inverse(mixed, sizes, side, tables, back, store_pieces(response, width))


def direction_kernel(rows, cols, meta, source, first, applied, second, measured, scalars):
    tiles = source.at[0, 0]
    row, col = lax.axis_index("row"), lax.axis_index("col")
    norm = total(first[...] * first[...])
    step = norm / total(first[...] * applied[...])
    residual = first[...] - step[None] * applied[...]
    norm_next = total(residual * residual)
    second[...] = residual + (norm_next / norm)[None] * first[...]
    scalars[0:1] = jnp.broadcast_to(norm_next, (1, LANES))
    scalars[1:2] = jnp.broadcast_to(step, (1, LANES))
    ints = [meta[2 + k, 0].astype(jnp.int32) for k in range(FOOTPRINT)] + [None, row, col]
    blocks = near_blocks(ints, second, rows, cols)
    squares = apply_forward(tiles, blocks, meta[0:1, :], None)
    measured[...] = jnp.broadcast_to(squares[None], measured.shape)


def last_step(measured, carry):
    squares = jnp.sum(measured[:, 0:1], axis=0)
    return carry[2, 0:1, 0:1] / (squares[:, 0:1] + carry[3, 0:1, 0:1])


def combine_kernel(measured, carry, known, response, out):
    out[...] = known[...] + last_step(measured, carry)[None] * response[...]


def finish_kernel(
    rows, cols, arrived, measured, carry, turns, packed, plain, coefficients, out, mixed, waves
):
    solved = carry[0] + last_step(measured, carry) * carry[1]
    for p in range(solved.shape[0]):
        coefficients[:, p * LANES : (p + 1) * LANES] = solved[p : p + 1]
    own = arrived.shape[1]
    width = out.shape[0]
    near = rows // 2
    for i in range(rows):
        for j in range(cols):
            at = i * HALF + j * own
            mixed[at : at + own, :] = arrived[i * cols + j]
    starts = north_starts(rows)
    for n, start in enumerate(starts):
        if n == 0:
            both = mul_table(mixed[0:HALF], packed[0], packed[1], TN)
        elif n == 1:
            both = mul_table(mixed[HALF : 2 * HALF], plain[0, :HALF], plain[1, :HALF], TN)
        else:
            at = 2 * start * HALF
            both = mul_table(mixed[at : at + 2 * HALF], plain[0], plain[1], TN)
        top, bottom = both[:width], both[width:]
        waves[n, :, :LANES] = top[:, :LANES] - bottom[:, LANES:]
        waves[n, :, LANES:] = top[:, LANES:] + bottom[:, :LANES]
    for at in range(0, width, SUB):
        parts = [[None, None] for _ in range(near)]
        for n, start in enumerate(starts):
            re = waves[n, at : at + SUB, :LANES]
            im = waves[n, at : at + SUB, LANES:]
            for i in range(near):
                if start == 0:
                    term = re
                else:
                    term = re * turns[0, n, i : i + 1] + im * turns[1, n, i : i + 1]
                sums = parts[i]
                sums[start % 2] = term if sums[start % 2] is None else sums[start % 2] + term
        for i in range(near):
            even, odd = parts[i]
            out[at : at + SUB, i * LANES : (i + 1) * LANES] = even + odd
            out[at : at + SUB, (near + i) * LANES : (near + i + 1) * LANES] = even - odd


def shape(*dims):
    return jax.ShapeDtypeStruct(dims, F32)


def scratch(*dims):
    return pltpu.VMEM(dims, F32)


def call(kernel, outs, ins, work=(), limit=SMALL):
    return pl.pallas_call(
        kernel,
        out_shape=outs,
        in_specs=[spec for spec, _ in ins],
        out_specs=jax.tree.map(lambda _: VMEM, outs),
        scratch_shapes=list(work),
        compiler_params=pltpu.CompilerParams(vmem_limit_bytes=limit),
    )(*[value for _, value in ins])


def exchange(pieces):
    return lax.all_to_all(pieces, BOTH, 0, 0, tiled=True)


def on_device(
    kernel_tiles, footprints, counts, readings, damping, layer_depth, inclinations, declinations,
    resid_grid,
):
    rows, cols = lax.axis_size("row"), lax.axis_size("col")
    devices = rows * cols
    slots, sources = kernel_tiles.shape[3:]
    parts = sources // LANES
    tile_east = resid_grid.shape[0]
    east = cols * tile_east
    bands = east // LANES
    own = HALF // cols
    width = east // devices
    sizes = (rows, cols, own, bands)

    turns = north_turns(rows)
    forward_tables, inverse_tables = north_forward_tables(), north_inverse_tables()
    tables, east_turns = east_tables(east)
    hats = north_hat_table(rows, cols)

    joined = 2 * width == LANES
    everywhere = shape(devices, parts, LANES)
    beside = shape(devices, 1 + own // 4, 4, LANES) if joined else everywhere
    pieces = shape(devices, own, 2 * width)

    def apart(value):
        return HBM, pltpu.with_memory_space_constraint(value, pltpu.HBM)

    tile_scratch = scratch(FOOTPRINT, slots, sources)
    tile_sems = pltpu.SemaphoreType.DMA((FOOTPRINT,))
    codes_scratch = pltpu.SMEM((1, FOOTPRINT), jnp.int32)

    nine = shape(FOOTPRINT, parts, LANES)
    sums, kept, side, meta = call(
        functools.partial(start_kernel, sizes),
        (
            shape(rows, SENT + width // 4, parts, LANES),
            nine,
            shape(side_rows(own, bands, rows)[-1], LANES),
            shape(SMALL_AT + 6 + LAYERS, LANES),
        ),
        [apart(footprints), (VMEM, counts), (VMEM, damping.reshape(1, 1))]
        + [
            apart(value)
            for value in (
                readings, layer_depth, inclinations, declinations,
                jnp.asarray(east_turns), jnp.asarray(hats), resid_grid, kernel_tiles,
            )
        ],
        [
            codes_scratch,
            pltpu.SMEM((LAYERS,), F32),
            pltpu.SMEM((2, 2), F32),
            scratch(1, slots),
            scratch(*resid_grid.shape),
            tile_scratch,
            scratch(slots, LANES),
            tile_sems,
            pltpu.SemaphoreType.DMA((8,)),
        ],
    )
    arrived = lax.all_to_all(sums, "row", 0, 0, tiled=True)
    summed, column_sums = call(
        functools.partial(column_kernel, rows, cols),
        (shape(cols, SENT, parts, LANES), nine),
        [(VMEM, arrived), (VMEM, kept)],
    )
    summed = lax.all_to_all(summed, "col", 0, 0, tiled=True)

    sums, near, *spectrum = call(
        functools.partial(normal_kernel, rows, cols),
        (beside, nine) if joined else (everywhere, nine, pieces),
        [
            (VMEM, meta),
            (VMEM, kernel_tiles),
            (VMEM, summed),
            (VMEM, column_sums),
            (VMEM, arrived),
            (VMEM, turns),
            (VMEM, forward_tables[0]),
            (VMEM, forward_tables[1]),
        ],
        [scratch(slots, LANES), scratch(rows, width, LANES)],
    )
    sums = exchange(sums)
    applied_all, right_side = call(
        functools.partial(share_kernel, rows, cols),
        (everywhere, everywhere),
        [(VMEM, sums), (VMEM, near)],
    )
    applied = exchange(applied_all)
    if joined:
        spectrum, sorted_work = sums, [scratch(cols, 2 * own, tile_east)]
    else:
        spectrum, sorted_work = exchange(spectrum[0]), []
        spectrum = spectrum.reshape(rows, cols, own, 2, width).transpose(1, 3, 2, 0, 4)
        spectrum = spectrum.reshape(cols, 2 * own, tile_east)

    second, measured, scalars = call(
        functools.partial(direction_kernel, rows, cols),
        (everywhere, everywhere, shape(2, LANES)),
        [(VMEM, meta), (VMEM, kernel_tiles), (VMEM, right_side), (VMEM, applied)],
    )
    work = [
        scratch(side_rows(own, bands, rows)[1], LANES),
        scratch(LAYERS, 2 * rows, cols * LANES),
        scratch(LAYERS * 2 * own, east),
        scratch((own + 1) * bands, 2 * LANES),
        scratch(own * bands, 2 * LANES),
        scratch(own * bands, 2 * LANES),
    ]
    known, response, carry = call(
        functools.partial(map_kernel, sizes, width),
        (pieces, pieces, shape(4, parts, LANES)),
        [
            (VMEM, spectrum),
            (VMEM, right_side),
            (VMEM, second),
            (VMEM, meta),
            (VMEM, scalars),
            (VMEM, tables),
            (VMEM, side),
        ],
        work + sorted_work,
    )
    measured = exchange(measured)
    outgoing = call(
        combine_kernel,
        pieces,
        [(VMEM, measured), (VMEM, carry), (VMEM, known), (VMEM, response)],
    )
    coefficients, rtp_map = call(
        functools.partial(finish_kernel, rows, cols),
        (shape(1, sources), shape(width, rows * LANES)),
        [
            (VMEM, exchange(outgoing)),
            (VMEM, measured),
            (VMEM, carry),
            (VMEM, turns),
            (VMEM, inverse_tables[0]),
            (VMEM, inverse_tables[1]),
        ],
        [scratch(rows * HALF, 2 * width), scratch(rows // 2 + 1, width, 2 * LANES)],
    )
    return coefficients.reshape(1, 1, sources), rtp_map


def solution(mesh):
    in_specs = (
        P("row", "col", None, None, None),
        P("row", "col", None),
        P("row", "col"),
        P("row", "col", None),
        P(),
        P(),
        P(),
        P(),
        P("col", "row"),
    )
    out_specs = (P("row", "col", None), P(("row", "col"), None))
    return jax.shard_map(
        on_device, mesh=mesh, in_specs=in_specs, out_specs=out_specs, check_vma=False
    )
```
